32 devices in a mesh: col: 8 (over z, y), row: 4 (over x, core).
Axes of the slice: x: 2, y: 2, z: 4, core: 2. Of those that a mesh axis runs over, the one named last changes fastest.
Arguments:
- r_slab: float32 [1024, 2048], P('row', 'col'), may hold values from -4 to 8, as said below
- arc_rows: float32 [4096, 2048], P('row', 'col'), may hold values from -6 to 6
- arc_blocks: int32 [32, 8], P('row', 'col'), may hold values 0 or 1
Outputs:
- r_updated: float32 [1024, 2048], P('row', 'col')
The draws below stay inside these ranges and needn't reach their ends.
Inputs may be any that keep to these rules, and one draw needn't show every extreme that they name: r_slab is zero wherever an entry's global column index is below its row index, and its diagonal is positive.
All inputs are finite; a program needn't handle non-finite values. No bound on the sum of `arc_blocks` on one device may be relied on, other than what follows from the above.
Results may differ from the reference program's by a relative error of at most 0.000098.
Values sent between devices are 32-bit elements; how exact they have to be, the bound alone decides.
No kernel may reach another device: no remote copies, remote signals or barrier semaphores. Data moves between devices by JAX's collectives and lax.ppermute only.
A program may use at most 64 MiB of HBM per device.

```python
import jax
import jax.numpy as jnp
from jax import lax

B = 256
P_SIZE = 4
ARC_ROWS = 128
BLK_DEV = 1
NBLK = 8
NC = 2048
ROWS = 4096
ARCS = 32
N_COL = 8


def draw_r_slab(key, part):
    first_key, second_key = jax.random.split(jax.random.fold_in(key, 11))
    shape = (P_SIZE * B, NBLK * B)
    row_ids = lax.broadcasted_iota(jnp.int32, shape, 0)
    col_ids = lax.broadcasted_iota(jnp.int32, shape, 1)
    stored = col_ids // B
    inner = col_ids % B
    owner = stored // BLK_DEV
    local = stored % BLK_DEV
    global_col = (local * N_COL + owner) * B + inner
    above = jnp.clip(jax.random.normal(first_key, shape, jnp.float32), -4.0, 4.0)
    diagonal = jax.random.uniform(second_key, shape, jnp.float32, 2.0, 6.0)
    zeros = jnp.zeros(shape, jnp.float32)
    return jnp.where(global_col > row_ids, above, jnp.where(global_col == row_ids, diagonal, zeros)).astype(jnp.float32)


def touch_ends(drawn, own_key, least, largest):
    place = [jax.random.randint(jax.random.fold_in(own_key, axis), (), 0, length) for axis, length in enumerate(drawn.shape)]
    widest = drawn.shape.index(max(drawn.shape))
    next_to = place[:widest] + [(place[widest] + 1) % drawn.shape[widest]] + place[widest + 1:]
    return drawn.at[tuple(place)].set(least).at[tuple(next_to)].set(largest)


def steps_of(own_key, extent, cuts, smallest, largest):
    gain, own = 1.0, jax.random.fold_in(own_key, 6)
    for axis_at, blocks in cuts:
        heights = jnp.exp(jax.random.uniform(jax.random.fold_in(own, axis_at), (blocks,), jnp.float32, smallest / len(cuts), largest / len(cuts)))
        gain = gain * jnp.repeat(heights, extent[axis_at] // blocks).reshape([-1 if axis == axis_at else 1 for axis in range(len(extent))])
    return gain


def gaussian(stream_key, extent, width, most, shards=(), held_as=jnp.bfloat16):
    values = jax.random.normal(stream_key, extent, jnp.float32) * width
    if len(shards) > 0:
        values = steps_of(stream_key, extent, shards, -0.22, 0.18) * values
    return jnp.clip(values, min=-most, max=most).astype(held_as)


def setup_inputs(seed: int = 0) -> dict:
    streams_of = jax.random.split(jax.random.key(seed), 4)
    r_slab = draw_r_slab(jax.random.fold_in(streams_of[3], 71), 0)
    arc_rows = gaussian(streams_of[1], (ROWS, NC), 1.0, 6.0, ((0, 4), (1, 8)), jnp.float32)
    arc_blocks = touch_ends((jax.random.randint(streams_of[2], (ARCS, NBLK), 0, 2) < 1).astype(jnp.int32), jax.random.fold_in(streams_of[2], 1), 0, 1)
    return dict(r_slab=r_slab, arc_rows=arc_rows, arc_blocks=arc_blocks)


def to_global(field):
    height = field.shape[0]
    return field.reshape(height, N_COL, BLK_DEV, B).transpose(0, 2, 1, 3).reshape(height, NBLK * B)

def to_storage(field):
    height = field.shape[0]
    return field.reshape(height, BLK_DEV, N_COL, B).transpose(0, 2, 1, 3).reshape(height, NBLK * B)

def reference(r_slab, arc_rows, arc_blocks):
    live = arc_blocks.astype(jnp.float32)
    masked = (arc_rows.reshape(ARCS, ARC_ROWS, NBLK, B) * live[:, None, :, None]).reshape(ROWS, NBLK * B)
    slab = to_global(r_slab)
    rows = to_global(masked)
    lead = P_SIZE * B
    gram = jnp.dot(slab[:, :lead].T, slab, precision=lax.Precision.HIGHEST)
    gram = gram + jnp.dot(rows[:, :lead].T, rows, precision=lax.Precision.HIGHEST)
    lower = jnp.linalg.cholesky(gram[:, :lead])
    factor = jax.scipy.linalg.solve_triangular(lower, gram, lower=True)
    row_ids = lax.broadcasted_iota(jnp.int32, factor.shape, 0)
    col_ids = lax.broadcasted_iota(jnp.int32, factor.shape, 1)
    factor = jnp.where(col_ids >= row_ids, factor, jnp.zeros_like(factor))
    return to_storage(factor)
```

```python
import functools

import jax
import jax.numpy as jnp
from jax import lax
from jax.experimental import pallas as pl
from jax.experimental.pallas import tpu as pltpu
from jax.sharding import Mesh
from jax.sharding import PartitionSpec as P

B = 256
P_SIZE = 4
ARC_ROWS = 128
NB = 128
SUB = 8
HIGHEST = lax.Precision.HIGHEST


def dot(left, right):
    return jnp.dot(left, right, precision=HIGHEST, preferred_element_type=jnp.float32)


def dot_t(left, right):
    return lax.dot_general(
        left, right, (((0,), (0,)), ((), ())), precision=HIGHEST, preferred_element_type=jnp.float32
    )


def inverse_factor(rows):
    n = NB // SUB
    tile = (SUB, NB)
    row_id = lax.broadcasted_iota(jnp.int32, tile, 0)
    col_id = lax.broadcasted_iota(jnp.int32, tile, 1)
    right = [jnp.where(row_id + r * SUB == col_id, 1.0, 0.0).astype(jnp.float32) for r in range(n)]
    for b in range(n):
        j = b * SUB
        head = rows[b]
        pivot = {}
        for k in range(SUB):
            for m in range(k, SUB):
                pivot[k, m] = jnp.broadcast_to(head[k : k + 1, j + m : j + m + 1], tile)
        scale = []
        for k in range(SUB):
            scale.append(lax.rsqrt(pivot[k, k]))
            for m in range(k + 1, SUB):
                pivot[k, m] = pivot[k, m] * scale[k]
            for m in range(k + 1, SUB):
                for q in range(m, SUB):
                    pivot[m, q] = pivot[m, q] - pivot[k, m] * pivot[k, q]
        top, top_right = [], []
        for k in range(SUB):
            here = jnp.broadcast_to(rows[b][k : k + 1, :], tile)
            there = jnp.broadcast_to(right[b][k : k + 1, :], tile)
            for m in range(k):
                here = here - pivot[m, k] * top[m]
                there = there - pivot[m, k] * top_right[m]
            top.append(here * scale[k])
            top_right.append(there * scale[k])
        strip = top_right[0]
        for k in range(1, SUB):
            strip = jnp.where(row_id == k, top_right[k], strip)
        for r in range(b + 1, n):
            left = []
            for k in range(SUB):
                part = jnp.broadcast_to(rows[r][:, j + k : j + k + 1], tile)
                for m in range(k):
                    part = part - pivot[m, k] * left[m]
                left.append(part * scale[k])
            body, body_right = rows[r], right[r]
            for k in range(SUB):
                body = body - left[k] * top[k]
                body_right = body_right - left[k] * top_right[k]
            rows[r], right[r] = body, body_right
        right[b] = strip
    return right


def factor_kernel(gram_ref, own_ref, out_ref, work, inv):
    lead = P_SIZE * B
    for c in range(P_SIZE):
        for r in range(c + 1):
            work[r * B : (r + 1) * B, c * B : (c + 1) * B] = gram_ref[c, r]
    work[:, lead:] = own_ref[...]
    steps = lead // NB

    def step(b, carry):
        start = pl.multiple_of(b * NB, NB)
        rows = [
            work[pl.ds(pl.multiple_of(start + r * SUB, SUB), SUB), pl.ds(start, NB)]
            for r in range(NB // SUB)
        ]
        right = inverse_factor(rows)
        for r in range(NB // SUB):
            inv[r * SUB : (r + 1) * SUB, :] = right[r]
        for s in range(steps):

            @pl.when(b == s)
            def _(s=s):
                lo, hi = s * NB, (s + 1) * NB
                panel = dot(inv[...], work[lo:hi, lo:])
                out_ref[lo:hi, :] = panel[:, lead - lo :]
                for i in range(s + 1, steps):
                    at = i * NB
                    off = at - lo
                    work[at : at + NB, at:] = work[at : at + NB, at:] - dot_t(
                        panel[:, off : off + NB], panel[:, off:]
                    )

        return carry

    lax.fori_loop(0, steps, step, 0)


def factor_columns(gram, own):
    lead = P_SIZE * B
    columns = own.shape[1]
    return pl.pallas_call(
        factor_kernel,
        out_shape=jax.ShapeDtypeStruct((lead, columns), jnp.float32),
        in_specs=[pl.BlockSpec(memory_space=pltpu.VMEM)] * 2,
        out_specs=pl.BlockSpec(memory_space=pltpu.VMEM),
        scratch_shapes=[
            pltpu.VMEM((lead, lead + columns), jnp.float32),
            pltpu.VMEM((NB, NB), jnp.float32),
        ],
        compiler_params=pltpu.CompilerParams(vmem_limit_bytes=40 * 1024 * 1024),
        name="factor_columns",
    )(gram, own)


def from_first(value, n_hi):
    at = lax.axis_index("hi")
    have = 1
    while have < n_hi:
        more = min(have, n_hi - have)
        got = lax.ppermute(value, "hi", [(g, g + have) for g in range(more)])
        value = jnp.where(at < have, value, got)
        have += more
    return value


def on_device(r_slab, arc_rows, arc_blocks):
    n_hi = lax.axis_size("hi")
    col_index = lax.axis_index("hi") * P_SIZE + lax.axis_index("lo")
    row_index = lax.axis_index("row")
    n_arcs, blocks_here = arc_blocks.shape
    live = arc_blocks.astype(jnp.float32)
    masked = (arc_rows.reshape(n_arcs, ARC_ROWS, blocks_here, B) * live[:, None, :, None]).reshape(
        arc_rows.shape
    )
    stacked = jnp.concatenate([r_slab, masked], axis=0)
    panels = lax.all_gather(from_first(stacked, n_hi), "lo")
    cross = jnp.einsum("lkm,kn->lmn", panels, stacked, precision=HIGHEST)
    mine = lax.psum_scatter(cross, "row", scatter_dimension=0, tiled=True)
    own = lax.all_gather(mine, "row", axis=0, tiled=True).reshape(P_SIZE * B, B)
    gram = lax.all_gather(from_first(mine, n_hi), ("lo", "row"), axis=0, tiled=True)
    gram = gram.reshape(P_SIZE, P_SIZE, B, B)
    factor = factor_columns(gram, own)
    result = lax.dynamic_slice_in_dim(factor, row_index * B, B, 0)
    row_ids = row_index * B + lax.broadcasted_iota(jnp.int32, result.shape, 0)
    col_ids = col_index * B + lax.broadcasted_iota(jnp.int32, result.shape, 1)
    return jnp.where(col_ids >= row_ids, result, jnp.zeros_like(result))


def solution(mesh):
    n_col, n_row = mesh.shape["col"], mesh.shape["row"]
    split = Mesh(
        mesh.devices.reshape(n_col // P_SIZE, P_SIZE, n_row),
        ("hi", "lo", "row"),
    )
    spec = P("row", ("hi", "lo"))
    return jax.shard_map(
        on_device,
        mesh=split,
        in_specs=(spec, spec, spec),
        out_specs=spec,
        check_vma=False,
    )
```

```python
import jax
import jax.numpy as jnp
from jax import lax
from jax.experimental import pallas as pl
from jax.experimental.pallas import tpu as pltpu
from jax.sharding import Mesh
from jax.sharding import PartitionSpec as P

B = 256
P_SIZE = 4
ARC_ROWS = 128
NB = 128
SUB = 8
HIGHEST = lax.Precision.HIGHEST


def dot(left, right):
    return jnp.dot(left, right, precision=HIGHEST, preferred_element_type=jnp.float32)


def dot_t(left, right):
    return lax.dot_general(
        left, right, (((0,), (0,)), ((), ())), precision=HIGHEST, preferred_element_type=jnp.float32
    )


def inverse_factor(rows):
    n = NB // SUB
    tile = (SUB, NB)
    row_id = lax.broadcasted_iota(jnp.int32, tile, 0)
    col_id = lax.broadcasted_iota(jnp.int32, tile, 1)
    right = [jnp.where(row_id + r * SUB == col_id, 1.0, 0.0).astype(jnp.float32) for r in range(n)]
    for b in range(n):
        j = b * SUB
        head = rows[b]
        pivot = {}
        for k in range(SUB):
            for m in range(k, SUB):
                pivot[k, m] = jnp.broadcast_to(head[k : k + 1, j + m : j + m + 1], tile)
        scale = []
        for k in range(SUB):
            scale.append(lax.rsqrt(pivot[k, k]))
            for m in range(k + 1, SUB):
                pivot[k, m] = pivot[k, m] * scale[k]
            for m in range(k + 1, SUB):
                for q in range(m, SUB):
                    pivot[m, q] = pivot[m, q] - pivot[k, m] * pivot[k, q]
        top, top_right = [], []
        for k in range(SUB):
            here = jnp.broadcast_to(rows[b][k : k + 1, :], tile)
            there = jnp.broadcast_to(right[b][k : k + 1, :], tile)
            for m in range(k):
                here = here - pivot[m, k] * top[m]
                there = there - pivot[m, k] * top_right[m]
            top.append(here * scale[k])
            top_right.append(there * scale[k])
        strip = top_right[0]
        for k in range(1, SUB):
            strip = jnp.where(row_id == k, top_right[k], strip)
        for r in range(b + 1, n):
            left = []
            for k in range(SUB):
                part = jnp.broadcast_to(rows[r][:, j + k : j + k + 1], tile)
                for m in range(k):
                    part = part - pivot[m, k] * left[m]
                left.append(part * scale[k])
            body, body_right = rows[r], right[r]
            for k in range(SUB):
                body = body - left[k] * top[k]
                body_right = body_right - left[k] * top_right[k]
            rows[r], right[r] = body, body_right
        right[b] = strip
    return right


PAIRS = [(r, c) for r in range(P_SIZE) for c in range(r, P_SIZE)]


def upper_products_kernel(rows_ref, out_ref):
    for at, (r, c) in enumerate(PAIRS):
        out_ref[at] = dot_t(rows_ref[r], rows_ref[c])


def all_products_kernel(left_ref, right_ref, out_ref):
    for c in range(P_SIZE):
        for r in range(P_SIZE):
            out_ref[c, r] = dot_t(left_ref[r], right_ref[c])


def on_chip(kernel, shape, name, *operands):
    return pl.pallas_call(
        kernel,
        out_shape=jax.ShapeDtypeStruct(shape, jnp.float32),
        in_specs=[pl.BlockSpec(memory_space=pltpu.VMEM)] * len(operands),
        out_specs=pl.BlockSpec(memory_space=pltpu.VMEM),
        compiler_params=pltpu.CompilerParams(vmem_limit_bytes=32 * 1024 * 1024),
        name=name,
    )(*operands)


def factor_kernel(gram_ref, own_ref, out_ref, work, inv):
    lead = P_SIZE * B
    for at, (r, c) in enumerate(PAIRS):
        work[r * B : (r + 1) * B, c * B : (c + 1) * B] = gram_ref[at]
    work[:, lead:] = own_ref[...]
    steps = lead // NB

    def step(b, carry):
        start = pl.multiple_of(b * NB, NB)
        rows = [
            work[pl.ds(pl.multiple_of(start + r * SUB, SUB), SUB), pl.ds(start, NB)]
            for r in range(NB // SUB)
        ]
        right = inverse_factor(rows)
        for r in range(NB // SUB):
            inv[r * SUB : (r + 1) * SUB, :] = right[r]
        for s in range(steps):

            @pl.when(b == s)
            def _(s=s):
                lo, hi = s * NB, (s + 1) * NB
                panel = dot(inv[...], work[lo:hi, lo:])
                out_ref[lo:hi, :] = panel[:, lead - lo :]
                for i in range(s + 1, steps):
                    at = i * NB
                    off = at - lo
                    work[at : at + NB, at:] = work[at : at + NB, at:] - dot_t(
                        panel[:, off : off + NB], panel[:, off:]
                    )

        return carry

    lax.fori_loop(0, steps, step, 0)


def factor_columns(gram, own):
    lead = P_SIZE * B
    columns = own.shape[1]
    return pl.pallas_call(
        factor_kernel,
        out_shape=jax.ShapeDtypeStruct((lead, columns), jnp.float32),
        in_specs=[pl.BlockSpec(memory_space=pltpu.VMEM)] * 2,
        out_specs=pl.BlockSpec(memory_space=pltpu.VMEM),
        scratch_shapes=[
            pltpu.VMEM((lead, lead + columns), jnp.float32),
            pltpu.VMEM((NB, NB), jnp.float32),
        ],
        compiler_params=pltpu.CompilerParams(vmem_limit_bytes=40 * 1024 * 1024),
        name="factor_columns",
    )(gram, own)


def from_first(value, n_hi):
    at = lax.axis_index("hi")
    have = 1
    while have < n_hi:
        more = min(have, n_hi - have)
        got = lax.ppermute(value, "hi", [(g, g + have) for g in range(more)])
        value = jnp.where(at < have, value, got)
        have += more
    return value


def on_device(r_slab, arc_rows, arc_blocks):
    n_hi = lax.axis_size("hi")
    col_index = lax.axis_index("hi") * P_SIZE + lax.axis_index("lo")
    row_index = lax.axis_index("row")
    n_arcs, blocks_here = arc_blocks.shape
    columns = arc_rows.shape[1]
    live = arc_blocks.astype(jnp.float32)
    masked = (arc_rows.reshape(n_arcs, ARC_ROWS, blocks_here, B) * live[:, None, :, None]).reshape(
        arc_rows.shape
    )
    stacked = jnp.concatenate([r_slab, masked], axis=0)
    quarters = stacked.reshape(P_SIZE, stacked.shape[0] // P_SIZE, columns)
    quarters = lax.all_to_all(quarters, "lo", 0, 0)
    group = ("lo", "row")
    gram = on_chip(upper_products_kernel, (len(PAIRS), B, B), "upper_products", quarters)
    gram = lax.psum_scatter(gram.reshape(-1, B), group, scatter_dimension=0, tiled=True)
    gram = lax.all_gather(from_first(gram, n_hi), group, axis=0, tiled=True)
    gram = gram.reshape(len(PAIRS), B, B)
    panels = from_first(quarters, n_hi)
    cross = on_chip(all_products_kernel, (P_SIZE, P_SIZE, B, B), "all_products", panels, quarters)
    mine = lax.psum_scatter(cross.reshape(-1, B), group, scatter_dimension=0, tiled=True)
    own = lax.all_gather(mine, "row", axis=0, tiled=True)
    factor = factor_columns(gram, own)
    result = lax.dynamic_slice_in_dim(factor, row_index * B, B, 0)
    row_ids = row_index * B + lax.broadcasted_iota(jnp.int32, result.shape, 0)
    col_ids = col_index * B + lax.broadcasted_iota(jnp.int32, result.shape, 1)
    return jnp.where(col_ids >= row_ids, result, jnp.zeros_like(result))


def solution(mesh):
    n_col, n_row = mesh.shape["col"], mesh.shape["row"]
    split = Mesh(
        mesh.devices.reshape(n_col // P_SIZE, P_SIZE, n_row),
        ("hi", "lo", "row"),
    )
    spec = P("row", ("hi", "lo"))
    return jax.shard_map(
        on_device,
        mesh=split,
        in_specs=(spec, spec, spec),
        out_specs=spec,
        check_vma=False,
    )
```

```python
import functools

import jax
import jax.numpy as jnp
from jax import lax
from jax.experimental import pallas as pl
from jax.experimental.pallas import tpu as pltpu
from jax.sharding import Mesh
from jax.sharding import PartitionSpec as P

B = 256
P_SIZE = 4
ARC_ROWS = 128
NB = 128
SUB = 8
HIGHEST = lax.Precision.HIGHEST


def dot(left, right):
    return jnp.dot(left, right, precision=HIGHEST, preferred_element_type=jnp.float32)


def dot_t(left, right):
    return lax.dot_general(
        left, right, (((0,), (0,)), ((), ())), precision=HIGHEST, preferred_element_type=jnp.float32
    )


def inverse_factor(rows):
    n = NB // SUB
    tile = (SUB, NB)
    row_id = lax.broadcasted_iota(jnp.int32, tile, 0)
    col_id = lax.broadcasted_iota(jnp.int32, tile, 1)
    right = [jnp.where(row_id + r * SUB == col_id, 1.0, 0.0).astype(jnp.float32) for r in range(n)]
    for b in range(n):
        j = b * SUB
        head = rows[b]
        pivot = {}
        for k in range(SUB):
            for m in range(k, SUB):
                pivot[k, m] = jnp.broadcast_to(head[k : k + 1, j + m : j + m + 1], tile)
        scale = []
        for k in range(SUB):
            scale.append(lax.rsqrt(pivot[k, k]))
            for m in range(k + 1, SUB):
                pivot[k, m] = pivot[k, m] * scale[k]
            for m in range(k + 1, SUB):
                for q in range(m, SUB):
                    pivot[m, q] = pivot[m, q] - pivot[k, m] * pivot[k, q]
        top, top_right = [], []
        for k in range(SUB):
            here = jnp.broadcast_to(rows[b][k : k + 1, :], tile)
            there = jnp.broadcast_to(right[b][k : k + 1, :], tile)
            for m in range(k):
                here = here - pivot[m, k] * top[m]
                there = there - pivot[m, k] * top_right[m]
            top.append(here * scale[k])
            top_right.append(there * scale[k])
        strip = top_right[0]
        for k in range(1, SUB):
            strip = jnp.where(row_id == k, top_right[k], strip)
        for r in range(b + 1, n):
            left = []
            for k in range(SUB):
                part = jnp.broadcast_to(rows[r][:, j + k : j + k + 1], tile)
                for m in range(k):
                    part = part - pivot[m, k] * left[m]
                left.append(part * scale[k])
            body, body_right = rows[r], right[r]
            for k in range(SUB):
                body = body - left[k] * top[k]
                body_right = body_right - left[k] * top_right[k]
            rows[r], right[r] = body, body_right
        right[b] = strip
    return right


PAIRS = [(r, c) for r in range(P_SIZE) for c in range(r, P_SIZE)]
HALF = len(PAIRS) // 2


def upper_products_kernel(side_ref, rows_ref, keep_ref, send_ref):
    for at, (r, c) in enumerate(PAIRS):
        block = dot_t(rows_ref[r], rows_ref[c])
        own = side_ref[0] == at // HALF

        @pl.when(own)
        def _(block=block, at=at):
            keep_ref[at % HALF] = block

        @pl.when(jnp.logical_not(own))
        def _(block=block, at=at):
            send_ref[at % HALF] = block


def all_products_kernel(side_ref, left_ref, right_ref, after_ref, keep_ref, send_ref):
    del after_ref
    side = side_ref[0]
    for high in range(2):
        for c in range(P_SIZE):
            keep_ref[high, c] = dot_t(left_ref[2 * high + side], right_ref[c])
            send_ref[high, c] = dot_t(left_ref[2 * high + 1 - side], right_ref[c])


def on_chip(kernel, shapes, name, *operands, scratch=(), scalars=0, after=()):
    return pl.pallas_call(
        kernel,
        out_shape=[jax.ShapeDtypeStruct(shape, jnp.float32) for shape in shapes],
        in_specs=[pl.BlockSpec(memory_space=pltpu.SMEM)] * scalars
        + [pl.BlockSpec(memory_space=pltpu.VMEM)] * (len(operands) - scalars)
        + [pl.BlockSpec(memory_space=pl.ANY)] * len(after),
        out_specs=[pl.BlockSpec(memory_space=pltpu.VMEM)] * len(shapes),
        scratch_shapes=list(scratch),
        compiler_params=pltpu.CompilerParams(vmem_limit_bytes=32 * 1024 * 1024),
        name=name,
    )(*operands, *after)


def factor_step_kernel(n, gram_ref, *rest):
    if n > 1:
        row_ref, inverse_ref, next_ref, work, inv = rest
    else:
        inverse_ref, work, inv = rest
    for c in range(n):
        work[:, c * B : (c + 1) * B] = gram_ref[c]
    width = n * B

    def step(b, carry):
        start = pl.multiple_of(b * NB, NB)
        rows = [
            work[pl.ds(pl.multiple_of(start + r * SUB, SUB), SUB), pl.ds(start, NB)]
            for r in range(NB // SUB)
        ]
        right = inverse_factor(rows)
        for r in range(NB // SUB):
            inv[pl.ds(pl.multiple_of(start + r * SUB, SUB), SUB), :] = right[r]

        @pl.when(b == 0)
        def _():
            panel = dot(inv[:NB, :], work[:NB, NB:])
            work[:NB, NB:] = panel
            work[NB:, NB:] = work[NB:, NB:] - dot_t(panel[:, :NB], panel)

        return carry

    lax.fori_loop(0, B // NB, step, 0)
    first, second = inv[:NB, :], inv[NB:, :]
    inverse_ref[:NB, :NB] = first
    inverse_ref[:NB, NB:] = jnp.zeros((NB, NB), jnp.float32)
    inverse_ref[NB:, :NB] = -dot(second, dot_t(work[:NB, NB:B], first))
    inverse_ref[NB:, NB:] = second
    if n > 1:
        work[NB:, B:] = dot(second, work[NB:, B:])
        row = work[:, B:]
        row_ref[...] = row
        at = n
        for r in range(1, n):
            left = row[:, (r - 1) * B : r * B]
            for c in range(r, n):
                next_ref[at - n] = gram_ref[at] - dot_t(left, row[:, (c - 1) * B : c * B])
                at += 1


def factor(gram):
    rows, inverses = [], []
    for n in range(P_SIZE, 0, -1):
        shapes = [(B, (n - 1) * B), (B, B), (n * (n - 1) // 2, B, B)] if n > 1 else [(B, B)]
        done = on_chip(
            functools.partial(factor_step_kernel, n),
            shapes,
            "factor_step",
            gram,
            scratch=[pltpu.VMEM((B, n * B), jnp.float32), pltpu.VMEM((B, NB), jnp.float32)],
        )
        if n > 1:
            row, inverse, gram = done
            rows.append(row)
        else:
            (inverse,) = done
        inverses.append(inverse)
    return rows, inverses


def solve_kernel(place_ref, *refs):
    rows, inverses, own_ref = refs[: P_SIZE - 1], refs[P_SIZE - 1 : 2 * P_SIZE - 1], refs[-2]
    out_ref = refs[-1]
    row_index, col_index = place_ref[0], place_ref[1]
    done = []
    for i in range(P_SIZE):
        block = own_ref[i]
        for k in range(i):
            off = (i - k - 1) * B
            block = block - dot_t(rows[k][:, off : off + B], done[k])
        block = dot(inverses[i][...], block)
        done.append(block)

        @pl.when(row_index == i)
        def _(block=block):
            rows_at = i * B + lax.broadcasted_iota(jnp.int32, block.shape, 0)
            cols_at = col_index * B + lax.broadcasted_iota(jnp.int32, block.shape, 1)
            out_ref[...] = jnp.where(cols_at >= rows_at, block, 0.0)


def from_first(value, n_hi):
    at = lax.axis_index("hi")
    have = 1
    while have < n_hi:
        more = min(have, n_hi - have)
        got = lax.ppermute(value, "hi", [(g, g + have) for g in range(more)])
        value = jnp.where(at < have, value, got)
        have += more
    return value


def exchange(value, axis, bits=1):
    size = lax.axis_size(axis)
    return lax.ppermute(value, axis, [(i, i ^ bits) for i in range(size)])


def take(value, index):
    return lax.dynamic_index_in_dim(value, index, 0, keepdims=False)


def on_device(r_slab, arc_rows, arc_blocks):
    n_hi = lax.axis_size("hi")
    low = lax.axis_index("lo")
    high_row, side = lax.axis_index("rh"), lax.axis_index("rl")
    col_index = lax.axis_index("hi") * P_SIZE + low
    row_index = high_row * 2 + side
    n_arcs, blocks_here = arc_blocks.shape
    columns = arc_rows.shape[1]
    live = arc_blocks.astype(jnp.float32)
    masked = (arc_rows.reshape(n_arcs, ARC_ROWS, blocks_here, B) * live[:, None, :, None]).reshape(
        arc_rows.shape
    )
    stacked = jnp.concatenate([r_slab, masked], axis=0)
    quarters = stacked.reshape(P_SIZE, stacked.shape[0] // P_SIZE, columns)
    quarters = lax.all_to_all(quarters, "lo", 0, 0)
    sides = side.reshape(1).astype(jnp.int32)

    half = (HALF, B, B)
    keep, send = on_chip(upper_products_kernel, [half, half], "upper_products", sides, quarters, scalars=1)
    panels = from_first(quarters, n_hi)
    gram = keep + exchange(send, "rl")
    gram = lax.all_to_all(gram.reshape(2 * P_SIZE, -1, B), ("rh", "lo"), 0, 0).sum(axis=0)
    piece = from_first(gram, n_hi)
    gram = lax.all_gather(piece, ("rl", "rh", "lo"), axis=0, tiled=True)
    gram = gram.reshape(len(PAIRS), B, B)

    half = (2, P_SIZE, B, B)
    keep, send = on_chip(
        all_products_kernel,
        [half, half],
        "all_products",
        sides,
        panels,
        quarters,
        scalars=1,
        after=(piece,),
    )
    cross = keep + exchange(send, "rl")
    cross = take(cross, high_row) + exchange(take(cross, 1 - high_row), "rh")
    mine = take(cross, low)
    for bits in range(1, P_SIZE):
        mine = mine + exchange(take(cross, low ^ bits), "lo", bits)
    own = lax.all_gather(mine, ("rh", "rl"))

    rows, inverses = factor(gram)
    place = jnp.stack([row_index, col_index]).astype(jnp.int32)
    (result,) = on_chip(
        solve_kernel, [(B, columns)], "solve", place, *rows, *inverses, own, scalars=1
    )
    return result


def solution(mesh):
    n_col, n_row = mesh.shape["col"], mesh.shape["row"]
    split = Mesh(
        mesh.devices.reshape(n_col // P_SIZE, P_SIZE, n_row // 2, 2),
        ("hi", "lo", "rh", "rl"),
    )
    spec = P(("rh", "rl"), ("hi", "lo"))
    return jax.shard_map(
        on_device,
        mesh=split,
        in_specs=(spec, spec, spec),
        out_specs=spec,
        check_vma=False,
    )
```

```python
import functools

import jax
import jax.numpy as jnp
from jax import lax
from jax.experimental import pallas as pl
from jax.experimental.pallas import tpu as pltpu
from jax.sharding import Mesh
from jax.sharding import PartitionSpec as P

B = 256
P_SIZE = 4
ARC_ROWS = 128
NB = 128
SUB = 8
HIGHEST = lax.Precision.HIGHEST


def dot(left, right):
    return jnp.dot(left, right, precision=HIGHEST, preferred_element_type=jnp.float32)


def dot_t(left, right):
    return lax.dot_general(
        left, right, (((0,), (0,)), ((), ())), precision=HIGHEST, preferred_element_type=jnp.float32
    )


def inverse_factor(rows):
    n = NB // SUB
    tile = (SUB, NB)
    row_id = lax.broadcasted_iota(jnp.int32, tile, 0)
    col_id = lax.broadcasted_iota(jnp.int32, tile, 1)
    right = [jnp.where(row_id + r * SUB == col_id, 1.0, 0.0).astype(jnp.float32) for r in range(n)]
    for b in range(n):
        j = b * SUB
        head = rows[b]
        pivot = {}
        for k in range(SUB):
            for m in range(k, SUB):
                pivot[k, m] = jnp.broadcast_to(head[k : k + 1, j + m : j + m + 1], tile)
        scale = []
        for k in range(SUB):
            scale.append(lax.rsqrt(pivot[k, k]))
            for m in range(k + 1, SUB):
                pivot[k, m] = pivot[k, m] * scale[k]
            for m in range(k + 1, SUB):
                for q in range(m, SUB):
                    pivot[m, q] = pivot[m, q] - pivot[k, m] * pivot[k, q]
        top, top_right = [], []
        for k in range(SUB):
            here = jnp.broadcast_to(rows[b][k : k + 1, :], tile)
            there = jnp.broadcast_to(right[b][k : k + 1, :], tile)
            for m in range(k):
                here = here - pivot[m, k] * top[m]
                there = there - pivot[m, k] * top_right[m]
            top.append(here * scale[k])
            top_right.append(there * scale[k])
        strip = top_right[0]
        for k in range(1, SUB):
            strip = jnp.where(row_id == k, top_right[k], strip)
        for r in range(b + 1, n):
            left = []
            for k in range(SUB):
                part = jnp.broadcast_to(rows[r][:, j + k : j + k + 1], tile)
                for m in range(k):
                    part = part - pivot[m, k] * left[m]
                left.append(part * scale[k])
            body, body_right = rows[r], right[r]
            for k in range(SUB):
                body = body - left[k] * top[k]
                body_right = body_right - left[k] * top_right[k]
            rows[r], right[r] = body, body_right
        right[b] = strip
    return right


PAIRS = [(r, c) for r in range(P_SIZE) for c in range(r, P_SIZE)]
HALF = len(PAIRS) // 2
PIECES = 4 * P_SIZE


def split(value):
    high = value.astype(jnp.bfloat16)
    return high, (value - high.astype(jnp.float32)).astype(jnp.bfloat16)


def left_parts(value):
    high, low = split(value)
    return jnp.concatenate([high, high, low], axis=0)


def right_parts(value):
    high, low = split(value)
    return jnp.concatenate([high, low, high], axis=0)


def parts_dot(left, right):
    return lax.dot_general(
        left, right, (((0,), (0,)), ((), ())), preferred_element_type=jnp.float32
    )


def upper_products_kernel(place_ref, rows_ref, keep_ref, send_ref, work):
    side = place_ref[0]
    right = [right_parts(rows_ref[c]) for c in range(P_SIZE)]
    at = 0
    for r in range(P_SIZE):
        wide = jnp.concatenate(right[r:], axis=1)
        product = parts_dot(left_parts(rows_ref[r]), wide)
        for c in range(P_SIZE - r):
            work[at] = product[:, c * B : (c + 1) * B]
            at += 1
    for i in range(HALF):
        keep_ref[i] = work[side * HALF + i]
        send_ref[i] = work[(1 - side) * HALF + i]


def all_products_kernel(
    place_ref, left_ref, more_ref, right_ref, after_ref, keep_ref, send_ref, work
):
    del after_ref
    side = place_ref[0]
    right = jnp.concatenate([right_parts(right_ref[c]) for c in range(P_SIZE)], axis=1)
    for r in range(P_SIZE):
        left = left_ref[r] if r < P_SIZE // 2 else more_ref[r - P_SIZE // 2]
        product = parts_dot(left_parts(left), right)
        for b in range(P_SIZE):
            work[r, b] = product[:, b * B : (b + 1) * B]
    for a in range(2):
        keep_ref[a] = work[2 * a + side]
        send_ref[a] = work[2 * a + 1 - side]


def pass_kernel(value_ref, after_ref, out_ref):
    del after_ref
    out_ref[...] = value_ref[...]


def add_kernel(left_ref, right_ref, after_ref, out_ref):
    del after_ref
    out_ref[...] = left_ref[...] + right_ref[...]


def sum_kernel(parts_ref, after_ref, out_ref):
    del after_ref
    total = parts_ref[0]
    for i in range(1, parts_ref.shape[0]):
        total = total + parts_ref[i]
    out_ref[...] = total


def behind(value, after):
    (value,) = on_chip(pass_kernel, [value.shape], "behind", value, after=(after,))
    return value


def on_chip(kernel, shapes, name, *operands, scratch=(), scalars=0, after=()):
    return pl.pallas_call(
        kernel,
        out_shape=[jax.ShapeDtypeStruct(shape, jnp.float32) for shape in shapes],
        in_specs=[pl.BlockSpec(memory_space=pltpu.SMEM)] * scalars
        + [pl.BlockSpec(memory_space=pltpu.VMEM)] * (len(operands) - scalars)
        + [pl.BlockSpec(memory_space=pl.ANY)] * len(after),
        out_specs=[pl.BlockSpec(memory_space=pltpu.VMEM)] * len(shapes),
        scratch_shapes=list(scratch),
        compiler_params=pltpu.CompilerParams(vmem_limit_bytes=32 * 1024 * 1024),
        name=name,
    )(*operands, *after)


def collect_kernel(place_ref, mine_ref, other_ref, gram_ref):
    side, high, low = place_ref[0], place_ref[1], place_ref[2]
    at = high * P_SIZE + low
    rows = mine_ref.shape[1]
    for s in range(2):
        for p in range(PIECES // 2):
            start = ((s * PIECES) // 2 + p) * rows
            end = start + rows
            while start < end:
                block, first = start // B, start % B
                count = min(end - start, B - first)
                skip = rows - (end - start)

                @pl.when(side == s)
                def _(block=block, first=first, count=count, skip=skip, p=p):
                    gram_ref[block, first : first + count] = mine_ref[p ^ at, skip : skip + count]

                @pl.when(side != s)
                def _(block=block, first=first, count=count, skip=skip, p=p):
                    gram_ref[block, first : first + count] = other_ref[p ^ at, skip : skip + count]

                start += count


def factor_step_kernel(n, gram_ref, *rest):
    if n > 1:
        row_ref, inverse_ref, next_ref, work, inv = rest
    else:
        inverse_ref, work, inv = rest
    for c in range(n):
        work[:, c * B : (c + 1) * B] = gram_ref[c]
    width = n * B

    def step(b, carry):
        start = pl.multiple_of(b * NB, NB)
        rows = [
            work[pl.ds(pl.multiple_of(start + r * SUB, SUB), SUB), pl.ds(start, NB)]
            for r in range(NB // SUB)
        ]
        right = inverse_factor(rows)
        for r in range(NB // SUB):
            inv[pl.ds(pl.multiple_of(start + r * SUB, SUB), SUB), :] = right[r]

        @pl.when(b == 0)
        def _():
            panel = dot(inv[:NB, :], work[:NB, NB:])
            work[:NB, NB:] = panel
            work[NB:, NB:] = work[NB:, NB:] - dot_t(panel[:, :NB], panel)

        return carry

    lax.fori_loop(0, B // NB, step, 0)
    first, second = inv[:NB, :], inv[NB:, :]
    inverse_ref[:NB, :NB] = first
    inverse_ref[:NB, NB:] = jnp.zeros((NB, NB), jnp.float32)
    inverse_ref[NB:, :NB] = -dot(second, dot_t(work[:NB, NB:B], first))
    inverse_ref[NB:, NB:] = second
    if n > 1:
        work[NB:, B:] = dot(second, work[NB:, B:])
        row = work[:, B:]
        row_ref[...] = row
        at = n
        for r in range(1, n):
            left = row[:, (r - 1) * B : r * B]
            for c in range(r, n):
                next_ref[at - n] = gram_ref[at] - dot_t(left, row[:, (c - 1) * B : c * B])
                at += 1


def factor(gram):
    rows, inverses = [], []
    for n in range(P_SIZE, 0, -1):
        shapes = [(B, (n - 1) * B), (B, B), (n * (n - 1) // 2, B, B)] if n > 1 else [(B, B)]
        done = on_chip(
            functools.partial(factor_step_kernel, n),
            shapes,
            "factor_step",
            gram,
            scratch=[pltpu.VMEM((B, n * B), jnp.float32), pltpu.VMEM((B, NB), jnp.float32)],
        )
        if n > 1:
            row, inverse, gram = done
            rows.append(row)
        else:
            (inverse,) = done
        inverses.append(inverse)
    return rows, inverses


def solve_kernel(place_ref, *refs):
    rows, inverses = refs[: P_SIZE - 1], refs[P_SIZE - 1 : 2 * P_SIZE - 1]
    own_refs, out_ref, own_ref = refs[2 * P_SIZE - 1 : -2], refs[-2], refs[-1]
    row_index, col_index = 2 * place_ref[1] + place_ref[0], place_ref[3]
    for t in range(P_SIZE):
        own_ref[row_index ^ t] = own_refs[t][...]
    done = []
    for i in range(P_SIZE):
        block = own_ref[i]
        for k in range(i):
            off = (i - k - 1) * B
            block = block - dot_t(rows[k][:, off : off + B], done[k])
        block = dot(inverses[i][...], block)
        done.append(block)

        @pl.when(row_index == i)
        def _(block=block):
            rows_at = i * B + lax.broadcasted_iota(jnp.int32, block.shape, 0)
            cols_at = col_index * B + lax.broadcasted_iota(jnp.int32, block.shape, 1)
            out_ref[...] = jnp.where(cols_at >= rows_at, block, 0.0)


def from_first(value, n_hi):
    at = lax.axis_index("hi")
    have = 1
    while have < n_hi:
        more = min(have, n_hi - have)
        got = lax.ppermute(value, "hi", [(g, g + have) for g in range(more)])
        value = jnp.where(at < have, value, got)
        have += more
    return value


def exchange(value, high_bits, low_bits):
    bits = low_bits * 2 + high_bits
    return lax.ppermute(value, ("lo", "rh"), [(i, i ^ bits) for i in range(2 * P_SIZE)])


def swap(value):
    return lax.ppermute(value, "rl", [(0, 1), (1, 0)])


def spread(piece):
    y, z, x = (0, 1), (0, 2), (1, 0)
    by_z, by_y, by_x = exchange(piece, *z), exchange(piece, *y), exchange(piece, *x)
    by_zy, by_yx, by_xz = exchange(by_z, *y), exchange(by_y, *x), exchange(by_x, *z)
    by_zyx = exchange(by_zy, *x)
    return jnp.stack([piece, by_y, by_z, by_zy, by_x, by_yx, by_xz, by_zyx])


def on_device(r_slab, arc_rows, arc_blocks):
    n_hi = lax.axis_size("hi")
    low = lax.axis_index("lo")
    high_row, side = lax.axis_index("rh"), lax.axis_index("rl")
    col_index = lax.axis_index("hi") * P_SIZE + low
    row_index = high_row * 2 + side
    n_arcs, blocks_here = arc_blocks.shape
    columns = arc_rows.shape[1]
    live = arc_blocks.astype(jnp.float32)
    masked = (arc_rows.reshape(n_arcs, ARC_ROWS, blocks_here, B) * live[:, None, :, None]).reshape(
        arc_rows.shape
    )
    stacked = jnp.concatenate([r_slab, masked], axis=0)
    quarters = stacked.reshape(P_SIZE, stacked.shape[0] // P_SIZE, columns)
    quarters = lax.all_to_all(quarters, "lo", 0, 0)
    place = jnp.stack([side, high_row, low, col_index]).astype(jnp.int32)
    half_panels = P_SIZE // 2
    panels = from_first(quarters[:half_panels], n_hi)

    half = (HALF, B, B)
    keep, send = on_chip(
        upper_products_kernel,
        [half, half],
        "upper_products",
        place,
        quarters,
        scalars=1,
        scratch=[pltpu.VMEM((len(PAIRS), B, B), jnp.float32)],
    )
    gram = keep + swap(send)
    gram = lax.all_to_all(gram.reshape(2 * P_SIZE, -1, B), ("rh", "lo"), 0, 0).sum(axis=0)
    piece = from_first(gram, n_hi)
    more_panels = from_first(behind(quarters[half_panels:], piece), n_hi)
    pieces = spread(piece)
    (gram,) = on_chip(
        collect_kernel, [(len(PAIRS), B, B)], "collect", place, pieces, swap(pieces), scalars=1
    )

    half = (2, P_SIZE, B, B)
    keep, send = on_chip(
        all_products_kernel,
        [half, half],
        "all_products",
        place,
        panels,
        more_panels,
        quarters,
        scalars=1,
        scratch=[pltpu.VMEM((P_SIZE, P_SIZE, B, B), jnp.float32)],
        after=(pieces,),
    )
    (cross,) = on_chip(add_kernel, [half], "add_pair", keep, swap(send), after=(gram,))
    cross = lax.all_to_all(cross.reshape(2 * P_SIZE, B, B), ("rh", "lo"), 0, 0)
    rows, inverses = factor(gram)
    (mine,) = on_chip(sum_kernel, [(B, columns)], "sum_places", cross, after=(rows[1],))
    by_x = exchange(mine, 1, 0)
    own = [mine, swap(mine), by_x, swap(by_x)]

    (result,) = on_chip(
        solve_kernel,
        [(B, columns)],
        "solve",
        place,
        *rows,
        *inverses,
        *own,
        scalars=1,
        scratch=[pltpu.VMEM((P_SIZE, B, columns), jnp.float32)],
    )
    return result


def solution(mesh):
    n_col, n_row = mesh.shape["col"], mesh.shape["row"]
    split = Mesh(
        mesh.devices.reshape(n_col // P_SIZE, P_SIZE, n_row // 2, 2),
        ("hi", "lo", "rh", "rl"),
    )
    spec = P(("rh", "rl"), ("hi", "lo"))
    return jax.shard_map(
        on_device,
        mesh=split,
        in_specs=(spec, spec, spec),
        out_specs=spec,
        check_vma=False,
    )
```

```python
import functools

import jax
import jax.numpy as jnp
from jax import lax
from jax.experimental import pallas as pl
from jax.experimental.pallas import tpu as pltpu
from jax.sharding import Mesh
from jax.sharding import PartitionSpec as P

B = 256
P_SIZE = 4
ARC_ROWS = 128
NB = 128
SUB = 8
HIGHEST = lax.Precision.HIGHEST


def dot(left, right):
    return jnp.dot(left, right, precision=HIGHEST, preferred_element_type=jnp.float32)


def dot_t(left, right):
    return lax.dot_general(
        left, right, (((0,), (0,)), ((), ())), precision=HIGHEST, preferred_element_type=jnp.float32
    )


def inverse_factor(rows):
    n = NB // SUB
    tile = (SUB, NB)
    row_id = lax.broadcasted_iota(jnp.int32, tile, 0)
    col_id = lax.broadcasted_iota(jnp.int32, tile, 1)
    right = [jnp.where(row_id + r * SUB == col_id, 1.0, 0.0).astype(jnp.float32) for r in range(n)]
    for b in range(n):
        j = b * SUB
        head = rows[b]
        pivot = {}
        for k in range(SUB):
            for m in range(k, SUB):
                pivot[k, m] = jnp.broadcast_to(head[k : k + 1, j + m : j + m + 1], tile)
        scale = []
        for k in range(SUB):
            scale.append(lax.rsqrt(pivot[k, k]))
            for m in range(k + 1, SUB):
                pivot[k, m] = pivot[k, m] * scale[k]
            for m in range(k + 1, SUB):
                for q in range(m, SUB):
                    pivot[m, q] = pivot[m, q] - pivot[k, m] * pivot[k, q]
        top, top_right = [], []
        for k in range(SUB):
            here = jnp.broadcast_to(rows[b][k : k + 1, :], tile)
            there = jnp.broadcast_to(right[b][k : k + 1, :], tile)
            for m in range(k):
                here = here - pivot[m, k] * top[m]
                there = there - pivot[m, k] * top_right[m]
            top.append(here * scale[k])
            top_right.append(there * scale[k])
        strip = top_right[0]
        for k in range(1, SUB):
            strip = jnp.where(row_id == k, top_right[k], strip)
        for r in range(b + 1, n):
            left = []
            for k in range(SUB):
                part = jnp.broadcast_to(rows[r][:, j + k : j + k + 1], tile)
                for m in range(k):
                    part = part - pivot[m, k] * left[m]
                left.append(part * scale[k])
            body, body_right = rows[r], right[r]
            for k in range(SUB):
                body = body - left[k] * top[k]
                body_right = body_right - left[k] * top_right[k]
            rows[r], right[r] = body, body_right
        right[b] = strip
    return right


PAIRS = [(r, c) for r in range(P_SIZE) for c in range(r, P_SIZE)]
HALF = len(PAIRS) // 2
PIECES = 4 * P_SIZE


def split(value):
    high = value.astype(jnp.bfloat16)
    return high, (value - high.astype(jnp.float32)).astype(jnp.bfloat16)


def left_parts(value):
    high, low = split(value)
    return jnp.concatenate([high, high, low], axis=0)


def right_parts(value):
    high, low = split(value)
    return jnp.concatenate([high, low, high], axis=0)


def parts_dot(left, right):
    return lax.dot_general(
        left, right, (((0,), (0,)), ((), ())), preferred_element_type=jnp.float32
    )


def upper_products_kernel(place_ref, rows_ref, keep_ref, send_ref, work):
    side = place_ref[0]
    right = [right_parts(rows_ref[c]) for c in range(P_SIZE)]
    at = 0
    for r in range(P_SIZE):
        wide = jnp.concatenate(right[r:], axis=1)
        product = parts_dot(left_parts(rows_ref[r]), wide)
        for c in range(P_SIZE - r):
            work[at] = product[:, c * B : (c + 1) * B]
            at += 1
    for i in range(HALF):
        keep_ref[i] = work[side * HALF + i]
        send_ref[i] = work[(1 - side) * HALF + i]


def all_products_kernel(place_ref, left_ref, right_ref, after_ref, keep_ref, send_ref, work):
    del after_ref
    side = place_ref[0]
    first = right_ref.shape[0] - P_SIZE
    right = jnp.concatenate([right_parts(right_ref[first + c]) for c in range(P_SIZE)], axis=1)
    for r in range(P_SIZE):
        product = parts_dot(left_parts(left_ref[r]), right)
        for b in range(P_SIZE):
            work[r, b] = product[:, b * B : (b + 1) * B]
    for a in range(2):
        keep_ref[a] = work[2 * a + side]
        send_ref[a] = work[2 * a + 1 - side]


def add_kernel(left_ref, right_ref, after_ref, out_ref):
    del after_ref
    out_ref[...] = left_ref[...] + right_ref[...]


def sum_kernel(parts_ref, after_ref, out_ref):
    del after_ref
    total = parts_ref[0]
    for i in range(1, parts_ref.shape[0]):
        total = total + parts_ref[i]
    out_ref[...] = total


def on_chip(kernel, shapes, name, *operands, scratch=(), scalars=0, after=()):
    return pl.pallas_call(
        kernel,
        out_shape=[jax.ShapeDtypeStruct(shape, jnp.float32) for shape in shapes],
        in_specs=[pl.BlockSpec(memory_space=pltpu.SMEM)] * scalars
        + [pl.BlockSpec(memory_space=pltpu.VMEM)] * (len(operands) - scalars)
        + [pl.BlockSpec(memory_space=pl.ANY)] * len(after),
        out_specs=[pl.BlockSpec(memory_space=pltpu.VMEM)] * len(shapes),
        scratch_shapes=list(scratch),
        compiler_params=pltpu.CompilerParams(vmem_limit_bytes=16 * 1024 * 1024),
        name=name,
    )(*operands, *after)


def collect_kernel(place_ref, mine_ref, other_ref, gram_ref):
    side, high, low = place_ref[0], place_ref[1], place_ref[2]
    at = high * P_SIZE + low
    rows = mine_ref.shape[1]
    for s in range(2):
        for p in range(PIECES // 2):
            start = ((s * PIECES) // 2 + p) * rows
            end = start + rows
            while start < end:
                block, first = start // B, start % B
                count = min(end - start, B - first)
                skip = rows - (end - start)

                @pl.when(side == s)
                def _(block=block, first=first, count=count, skip=skip, p=p):
                    gram_ref[block, first : first + count] = mine_ref[p ^ at, skip : skip + count]

                @pl.when(side != s)
                def _(block=block, first=first, count=count, skip=skip, p=p):
                    gram_ref[block, first : first + count] = other_ref[p ^ at, skip : skip + count]

                start += count


def factor_step_kernel(n, gram_ref, *rest):
    if n > 1:
        row_ref, inverse_ref, next_ref, work, inv = rest
    else:
        inverse_ref, work, inv = rest
    for c in range(n):
        work[:, c * B : (c + 1) * B] = gram_ref[c]
    width = n * B

    def step(b, carry):
        start = pl.multiple_of(b * NB, NB)
        rows = [
            work[pl.ds(pl.multiple_of(start + r * SUB, SUB), SUB), pl.ds(start, NB)]
            for r in range(NB // SUB)
        ]
        right = inverse_factor(rows)
        for r in range(NB // SUB):
            inv[pl.ds(pl.multiple_of(start + r * SUB, SUB), SUB), :] = right[r]

        @pl.when(b == 0)
        def _():
            panel = dot(inv[:NB, :], work[:NB, NB:])
            work[:NB, NB:] = panel
            work[NB:, NB:] = work[NB:, NB:] - dot_t(panel[:, :NB], panel)

        return carry

    lax.fori_loop(0, B // NB, step, 0)
    first, second = inv[:NB, :], inv[NB:, :]
    inverse_ref[:NB, :NB] = first
    inverse_ref[:NB, NB:] = jnp.zeros((NB, NB), jnp.float32)
    inverse_ref[NB:, :NB] = -dot(second, dot_t(work[:NB, NB:B], first))
    inverse_ref[NB:, NB:] = second
    if n > 1:
        work[NB:, B:] = dot(second, work[NB:, B:])
        row = work[:, B:]
        row_ref[...] = row
        at = n
        for r in range(1, n):
            left = row[:, (r - 1) * B : r * B]
            for c in range(r, n):
                next_ref[at - n] = gram_ref[at] - dot_t(left, row[:, (c - 1) * B : c * B])
                at += 1


def factor(gram):
    rows, inverses = [], []
    for n in range(P_SIZE, 0, -1):
        shapes = [(B, (n - 1) * B), (B, B), (n * (n - 1) // 2, B, B)] if n > 1 else [(B, B)]
        done = on_chip(
            functools.partial(factor_step_kernel, n),
            shapes,
            "factor_step",
            gram,
            scratch=[pltpu.VMEM((B, n * B), jnp.float32), pltpu.VMEM((B, NB), jnp.float32)],
        )
        if n > 1:
            row, inverse, gram = done
            rows.append(row)
        else:
            (inverse,) = done
        inverses.append(inverse)
    return rows, inverses


def solve_kernel(place_ref, *refs):
    rows, inverses = refs[: P_SIZE - 1], refs[P_SIZE - 1 : 2 * P_SIZE - 1]
    gram_ref, own_refs, out_ref, own_ref = refs[-P_SIZE - 3], refs[-P_SIZE - 2 : -2], refs[-2], refs[-1]
    row_index, col_index = 2 * place_ref[1] + place_ref[0], place_ref[3]

    @pl.when(col_index >= P_SIZE)
    def _():
        for t in range(P_SIZE):
            own_ref[row_index ^ t] = own_refs[t][...]

    for c in range(P_SIZE):

        @pl.when(col_index == c)
        def _(c=c):
            for r in range(P_SIZE):
                own_ref[r] = gram_ref[PAIRS.index((min(r, c), c))]

    done = []
    for i in range(P_SIZE):
        block = own_ref[i]
        for k in range(i):
            off = (i - k - 1) * B
            block = block - dot_t(rows[k][:, off : off + B], done[k])
        block = dot(inverses[i][...], block)
        done.append(block)

        @pl.when(row_index == i)
        def _(block=block):
            rows_at = i * B + lax.broadcasted_iota(jnp.int32, block.shape, 0)
            cols_at = col_index * B + lax.broadcasted_iota(jnp.int32, block.shape, 1)
            out_ref[...] = jnp.where(cols_at >= rows_at, block, 0.0)


def from_first(value, n_hi):
    at = lax.axis_index("hi")
    have = 1
    while have < n_hi:
        more = min(have, n_hi - have)
        got = lax.ppermute(value, "hi", [(g, g + have) for g in range(more)])
        value = jnp.where(at < have, value, got)
        have += more
    return value


def exchange(value, high_bits, low_bits):
    bits = low_bits * 2 + high_bits
    return lax.ppermute(value, ("lo", "rh"), [(i, i ^ bits) for i in range(2 * P_SIZE)])


def swap(value, axis="rl"):
    return lax.ppermute(value, axis, [(0, 1), (1, 0)])


def spread(piece):
    y, z, x = (0, 1), (0, 2), (1, 0)
    by_z, by_y, by_x = exchange(piece, *z), exchange(piece, *y), exchange(piece, *x)
    by_zy, by_yx, by_xz = exchange(by_z, *y), exchange(by_y, *x), exchange(by_x, *z)
    by_zyx = exchange(by_zy, *x)
    return jnp.stack([piece, by_y, by_z, by_zy, by_x, by_yx, by_xz, by_zyx])


def on_device(r_slab, arc_rows, arc_blocks):
    n_hi = lax.axis_size("hi")
    low = lax.axis_index("lo")
    high_row, side = lax.axis_index("rh"), lax.axis_index("rl")
    col_index = lax.axis_index("hi") * P_SIZE + low
    row_index = high_row * 2 + side
    n_arcs, blocks_here = arc_blocks.shape
    columns = arc_rows.shape[1]
    live = arc_blocks.astype(jnp.float32)
    masked = (arc_rows.reshape(n_arcs, ARC_ROWS, blocks_here, B) * live[:, None, :, None]).reshape(
        arc_rows.shape
    )
    stacked = jnp.concatenate([r_slab, masked], axis=0)
    place = jnp.stack([side, high_row, low, col_index]).astype(jnp.int32)
    in_two = n_hi == 2
    owners = ("hi", "lo") if in_two else ("lo",)
    shares = P_SIZE * n_hi if in_two else P_SIZE
    blocks = stacked.reshape(shares, stacked.shape[0] // shares, columns)
    blocks = lax.all_to_all(blocks, owners, 0, 0)
    panels = blocks if in_two else from_first(blocks, n_hi)

    half = (HALF, B, B)
    keep, send = on_chip(
        upper_products_kernel,
        [half, half],
        "upper_products",
        place,
        blocks,
        scalars=1,
        scratch=[pltpu.VMEM((len(PAIRS), B, B), jnp.float32)],
    )
    gram = keep + swap(send)
    gram = lax.all_to_all(gram.reshape(2 * P_SIZE, -1, B), ("rh", "lo"), 0, 0).sum(axis=0)
    piece = gram + swap(gram, "hi") if in_two else from_first(gram, n_hi)
    pieces = spread(piece)
    (gram,) = on_chip(
        collect_kernel, [(len(PAIRS), B, B)], "collect", place, pieces, swap(pieces), scalars=1
    )

    half = (2, P_SIZE, B, B)
    keep, send = on_chip(
        all_products_kernel,
        [half, half],
        "all_products",
        place,
        panels,
        blocks,
        scalars=1,
        scratch=[pltpu.VMEM((P_SIZE, P_SIZE, B, B), jnp.float32)],
        after=(pieces,),
    )
    (cross,) = on_chip(add_kernel, [half], "add_pair", keep, swap(send), after=(gram,))
    cross = lax.all_to_all(cross.reshape(2 * P_SIZE, B, B), ("rh", "lo"), 0, 0)
    rows, inverses = factor(gram)
    (mine,) = on_chip(sum_kernel, [(B, columns)], "sum_places", cross, after=(rows[2],))
    if in_two:
        mine = mine + swap(mine, "hi")
    by_x = exchange(mine, 1, 0)
    own = [mine, swap(mine), by_x, swap(by_x)]

    (result,) = on_chip(
        solve_kernel,
        [(B, columns)],
        "solve",
        place,
        *rows,
        *inverses,
        gram,
        *own,
        scalars=1,
        scratch=[pltpu.VMEM((P_SIZE, B, columns), jnp.float32)],
    )
    return result


def solution(mesh):
    n_col, n_row = mesh.shape["col"], mesh.shape["row"]
    split = Mesh(
        mesh.devices.reshape(n_col // P_SIZE, P_SIZE, n_row // 2, 2),
        ("hi", "lo", "rh", "rl"),
    )
    spec = P(("rh", "rl"), ("hi", "lo"))
    return jax.shard_map(
        on_device,
        mesh=split,
        in_specs=(spec, spec, spec),
        out_specs=spec,
        check_vma=False,
    )
```

```python
import functools

import jax
import jax.numpy as jnp
from jax import lax
from jax.experimental import pallas as pl
from jax.experimental.pallas import tpu as pltpu
from jax.sharding import Mesh
from jax.sharding import PartitionSpec as P

B = 256
P_SIZE = 4
ARC_ROWS = 128
NB = 128
SUB = 8
HIGHEST = lax.Precision.HIGHEST


def dot(left, right):
    return jnp.dot(left, right, precision=HIGHEST, preferred_element_type=jnp.float32)


def dot_t(left, right):
    return lax.dot_general(
        left, right, (((0,), (0,)), ((), ())), precision=HIGHEST, preferred_element_type=jnp.float32
    )


def lane(value, at):
    return jnp.broadcast_to(value[:, at : at + 1], (SUB, NB))


def row(value, at):
    return jnp.broadcast_to(value[at : at + 1, :], (SUB, NB))


def inverse_factor(rows):
    n = NB // SUB
    row_id = lax.broadcasted_iota(jnp.int32, (SUB, NB), 0)
    col_id = lax.broadcasted_iota(jnp.int32, (SUB, NB), 1)
    order = range(SUB)
    ahead = [lane(rows[0], m) for m in order]
    for b in range(n):
        j = b * SUB
        pivot = {(k, m): row(ahead[m], k) for k in order for m in range(k, SUB)}
        below = [[lane(rows[r], j + k) for k in order] for r in range(b + 1, n)]
        if b + 1 < n:
            ahead = [lane(rows[b + 1], j + SUB + m) for m in order]
        scale, left = [], []
        for k in order:
            scale.append(lax.rsqrt(pivot[k, k]))
            for m in range(k + 1, SUB):
                pivot[k, m] = pivot[k, m] * scale[k]
            for m in range(k + 1, SUB):
                for q in range(m, SUB):
                    pivot[m, q] = pivot[m, q] - pivot[k, m] * pivot[k, q]
            if b + 1 < n:
                part = below[0][k]
                for m in range(k):
                    part = part - pivot[m, k] * left[m]
                part = part * scale[k]
                left.append(part)
                for m in order:
                    ahead[m] = ahead[m] - part * row(part, m)
        inside = (col_id >= j) & (col_id < j + SUB)
        head = jnp.where(inside, jnp.where(col_id - j == row_id, 1.0, 0.0), rows[b])
        top = []
        for k in order:
            part = row(head, k)
            for m in range(k):
                part = part - pivot[m, k] * top[m]
            top.append(part * scale[k])
        if b + 1 < n:
            solved = [None] * SUB
            for k in reversed(order):
                part = top[k]
                for m in range(k + 1, SUB):
                    part = part - pivot[k, m] * solved[m]
                solved[k] = part * scale[k]
            for r in range(b + 1, n):
                body = jnp.where(inside, 0.0, rows[r])
                for k in order:
                    body = body - below[r - b - 1][k] * solved[k]
                rows[r] = body
        strip = top[0]
        for k in range(1, SUB):
            strip = jnp.where(row_id == k, top[k], strip)
        rows[b] = jnp.where(col_id < j + SUB, strip, 0.0)
    return rows


PAIRS = [(r, c) for r in range(P_SIZE) for c in range(r, P_SIZE)]
HALF = len(PAIRS) // 2
PIECES = 4 * P_SIZE


def split(value):
    high = value.astype(jnp.bfloat16)
    return high, (value - high.astype(jnp.float32)).astype(jnp.bfloat16)


def left_parts(value):
    high, low = split(value)
    return jnp.concatenate([high, high, low], axis=0)


def right_parts(value):
    high, low = split(value)
    return jnp.concatenate([high, low, high], axis=0)


def parts_dot(left, right):
    return lax.dot_general(
        left, right, (((0,), (0,)), ((), ())), preferred_element_type=jnp.float32
    )


def upper_products_kernel(place_ref, rows_ref, keep_ref, send_ref, work):
    side = place_ref[0]
    right = [right_parts(rows_ref[c]) for c in range(P_SIZE)]
    at = 0
    for r in range(P_SIZE):
        wide = jnp.concatenate(right[r:], axis=1)
        product = parts_dot(left_parts(rows_ref[r]), wide)
        for c in range(P_SIZE - r):
            work[at] = product[:, c * B : (c + 1) * B]
            at += 1
    for i in range(HALF):
        keep_ref[i] = work[side * HALF + i]
        send_ref[i] = work[(1 - side) * HALF + i]


def all_products_kernel(place_ref, left_ref, right_ref, after_ref, keep_ref, send_ref, work):
    del after_ref
    side = place_ref[0]
    first = right_ref.shape[0] - P_SIZE
    right = jnp.concatenate([right_parts(right_ref[first + c]) for c in range(P_SIZE)], axis=1)
    for r in range(P_SIZE):
        product = parts_dot(left_parts(left_ref[r]), right)
        for b in range(P_SIZE):
            work[r, b] = product[:, b * B : (b + 1) * B]
    for a in range(2):
        keep_ref[a] = work[2 * a + side]
        send_ref[a] = work[2 * a + 1 - side]


def tie_kernel(value_ref, after_ref, out_ref):
    del value_ref, after_ref, out_ref


def behind(value, after):
    return pl.pallas_call(
        tie_kernel,
        out_shape=jax.ShapeDtypeStruct(value.shape, value.dtype),
        in_specs=[pl.BlockSpec(memory_space=pl.ANY)] * 2,
        out_specs=pl.BlockSpec(memory_space=pl.ANY),
        input_output_aliases={0: 0},
        name="behind",
    )(value, after)


def add_kernel(left_ref, right_ref, after_ref, out_ref):
    del after_ref
    out_ref[...] = left_ref[...] + right_ref[...]


def sum_kernel(parts_ref, after_ref, out_ref):
    del after_ref
    total = parts_ref[0]
    for i in range(1, parts_ref.shape[0]):
        total = total + parts_ref[i]
    out_ref[...] = total


def on_chip(kernel, shapes, name, *operands, scratch=(), scalars=0, after=()):
    return pl.pallas_call(
        kernel,
        out_shape=[jax.ShapeDtypeStruct(shape, jnp.float32) for shape in shapes],
        in_specs=[pl.BlockSpec(memory_space=pltpu.SMEM)] * scalars
        + [pl.BlockSpec(memory_space=pltpu.VMEM)] * (len(operands) - scalars)
        + [pl.BlockSpec(memory_space=pl.ANY)] * len(after),
        out_specs=[pl.BlockSpec(memory_space=pltpu.VMEM)] * len(shapes),
        scratch_shapes=list(scratch),
        compiler_params=pltpu.CompilerParams(vmem_limit_bytes=16 * 1024 * 1024),
        name=name,
    )(*operands, *after)


def collect_kernel(place_ref, mine_ref, other_ref, gram_ref, token_ref):
    side, high, low = place_ref[0], place_ref[1], place_ref[2]
    at = high * P_SIZE + low
    rows = mine_ref.shape[1]
    token_ref[...] = jnp.zeros_like(token_ref)
    for s in range(2):
        for p in range(PIECES // 2):
            start = ((s * PIECES) // 2 + p) * rows
            end = start + rows
            while start < end:
                block, first = start // B, start % B
                count = min(end - start, B - first)
                skip = rows - (end - start)

                @pl.when(side == s)
                def _(block=block, first=first, count=count, skip=skip, p=p):
                    gram_ref[block, first : first + count] = mine_ref[p ^ at, skip : skip + count]

                @pl.when(side != s)
                def _(block=block, first=first, count=count, skip=skip, p=p):
                    gram_ref[block, first : first + count] = other_ref[p ^ at, skip : skip + count]

                start += count


def factor_step_kernel(n, gram_ref, *rest):
    if n > 1:
        row_ref, inverse_ref, next_ref, work, inv = rest
    else:
        inverse_ref, work, inv = rest
    for c in range(n):
        work[:, c * B : (c + 1) * B] = gram_ref[c]
    width = n * B

    def step(b, carry):
        start = pl.multiple_of(b * NB, NB)
        rows = [
            work[pl.ds(pl.multiple_of(start + r * SUB, SUB), SUB), pl.ds(start, NB)]
            for r in range(NB // SUB)
        ]
        right = inverse_factor(rows)
        for r in range(NB // SUB):
            inv[pl.ds(pl.multiple_of(start + r * SUB, SUB), SUB), :] = right[r]

        @pl.when(b == 0)
        def _():
            panel = dot(inv[:NB, :], work[:NB, NB:])
            work[:NB, NB:] = panel
            work[NB:, NB:] = work[NB:, NB:] - dot_t(panel[:, :NB], panel)

        return carry

    lax.fori_loop(0, B // NB, step, 0)
    first, second = inv[:NB, :], inv[NB:, :]
    inverse_ref[:NB, :NB] = first
    inverse_ref[:NB, NB:] = jnp.zeros((NB, NB), jnp.float32)
    inverse_ref[NB:, :NB] = -dot(second, dot_t(work[:NB, NB:B], first))
    inverse_ref[NB:, NB:] = second
    if n > 1:
        work[NB:, B:] = dot(second, work[NB:, B:])
        row = work[:, B:]
        row_ref[...] = row
        at = n
        for r in range(1, n):
            left = row[:, (r - 1) * B : r * B]
            for c in range(r, n):
                next_ref[at - n] = gram_ref[at] - dot_t(left, row[:, (c - 1) * B : c * B])
                at += 1


def factor(gram):
    rows, inverses = [], []
    for n in range(P_SIZE, 0, -1):
        shapes = [(B, (n - 1) * B), (B, B), (n * (n - 1) // 2, B, B)] if n > 1 else [(B, B)]
        done = on_chip(
            functools.partial(factor_step_kernel, n),
            shapes,
            "factor_step",
            gram,
            scratch=[pltpu.VMEM((B, n * B), jnp.float32), pltpu.VMEM((B, NB), jnp.float32)],
        )
        if n > 1:
            row, inverse, gram = done
            rows.append(row)
        else:
            (inverse,) = done
        inverses.append(inverse)
    return rows, inverses


def solve_kernel(place_ref, *refs):
    rows, inverses = refs[: P_SIZE - 1], refs[P_SIZE - 1 : 2 * P_SIZE - 1]
    gram_ref, own_refs, out_ref, own_ref = refs[-P_SIZE - 3], refs[-P_SIZE - 2 : -2], refs[-2], refs[-1]
    row_index, col_index = 2 * place_ref[1] + place_ref[0], place_ref[3]

    @pl.when(col_index >= P_SIZE)
    def _():
        for t in range(P_SIZE):
            own_ref[row_index ^ t] = own_refs[t][...]

    for c in range(P_SIZE):

        @pl.when(col_index == c)
        def _(c=c):
            for r in range(P_SIZE):
                own_ref[r] = gram_ref[PAIRS.index((min(r, c), c))]

    done = []
    for i in range(P_SIZE):
        block = own_ref[i]
        for k in range(i):
            off = (i - k - 1) * B
            block = block - dot_t(rows[k][:, off : off + B], done[k])
        block = dot(inverses[i][...], block)
        done.append(block)

        @pl.when(row_index == i)
        def _(block=block):
            rows_at = i * B + lax.broadcasted_iota(jnp.int32, block.shape, 0)
            cols_at = col_index * B + lax.broadcasted_iota(jnp.int32, block.shape, 1)
            out_ref[...] = jnp.where(cols_at >= rows_at, block, 0.0)


def from_first(value, n_hi):
    at = lax.axis_index("hi")
    have = 1
    while have < n_hi:
        more = min(have, n_hi - have)
        got = lax.ppermute(value, "hi", [(g, g + have) for g in range(more)])
        value = jnp.where(at < have, value, got)
        have += more
    return value


def exchange(value, high_bits, low_bits):
    bits = low_bits * 2 + high_bits
    return lax.ppermute(value, ("lo", "rh"), [(i, i ^ bits) for i in range(2 * P_SIZE)])


def swap(value, axis="rl"):
    return lax.ppermute(value, axis, [(0, 1), (1, 0)])


def across_rows(value, bits):
    return lax.ppermute(value, ("rh", "rl"), [(i, i ^ bits) for i in range(P_SIZE)])


def spread(piece):
    y, z, x = (0, 1), (0, 2), (1, 0)
    by_z, by_y, by_x = exchange(piece, *z), exchange(piece, *y), exchange(piece, *x)
    by_zy, by_yx, by_xz = exchange(by_z, *y), exchange(by_y, *x), exchange(by_x, *z)
    by_zyx = exchange(by_zy, *x)
    return jnp.stack([piece, by_y, by_z, by_zy, by_x, by_yx, by_xz, by_zyx])


def on_device(r_slab, arc_rows, arc_blocks):
    n_hi = lax.axis_size("hi")
    low = lax.axis_index("lo")
    high_row, side = lax.axis_index("rh"), lax.axis_index("rl")
    col_index = lax.axis_index("hi") * P_SIZE + low
    row_index = high_row * 2 + side
    n_arcs, blocks_here = arc_blocks.shape
    columns = arc_rows.shape[1]
    live = arc_blocks.astype(jnp.float32)
    masked = (arc_rows.reshape(n_arcs, ARC_ROWS, blocks_here, B) * live[:, None, :, None]).reshape(
        arc_rows.shape
    )
    stacked = jnp.concatenate([r_slab, masked], axis=0)
    place = jnp.stack([side, high_row, low, col_index]).astype(jnp.int32)
    in_two = n_hi == 2
    owners = ("hi", "lo") if in_two else ("lo",)
    shares = P_SIZE * n_hi if in_two else P_SIZE
    blocks = stacked.reshape(shares, stacked.shape[0] // shares, columns)
    blocks = lax.all_to_all(blocks, owners, 0, 0)
    panels = blocks if in_two else from_first(blocks, n_hi)

    half = (HALF, B, B)
    keep, send = on_chip(
        upper_products_kernel,
        [half, half],
        "upper_products",
        place,
        blocks,
        scalars=1,
        scratch=[pltpu.VMEM((len(PAIRS), B, B), jnp.float32)],
    )
    gram = keep + swap(send)
    gram = lax.all_to_all(gram.reshape(2 * P_SIZE, -1, B), ("rh", "lo"), 0, 0).sum(axis=0)
    half = (2, P_SIZE, B, B)
    cross, send = on_chip(
        all_products_kernel,
        [half, half],
        "all_products",
        place,
        panels,
        blocks,
        scalars=1,
        scratch=[pltpu.VMEM((P_SIZE, P_SIZE, B, B), jnp.float32)],
        after=(keep,),
    )
    cross = cross + swap(send)
    piece = gram + swap(gram, "hi") if in_two else from_first(gram, n_hi)
    pieces = spread(piece)
    gram, token = on_chip(
        collect_kernel,
        [(len(PAIRS), B, B), (SUB, NB)],
        "collect",
        place,
        pieces,
        swap(pieces),
        scalars=1,
    )

    cross = behind(cross.reshape(2 * P_SIZE, B, B), token)
    cross = lax.all_to_all(cross, ("rh", "lo"), 0, 0)
    rows, inverses = factor(gram)
    (mine,) = on_chip(sum_kernel, [(B, columns)], "sum_places", cross, after=(rows[1],))
    if in_two:
        other = swap(mine, "hi")
        (mine,) = on_chip(add_kernel, [(B, columns)], "add_groups", mine, other, after=(rows[2],))
    own = [mine] + [across_rows(mine, bits) for bits in range(1, P_SIZE)]

    (result,) = on_chip(
        solve_kernel,
        [(B, columns)],
        "solve",
        place,
        *rows,
        *inverses,
        gram,
        *own,
        scalars=1,
        scratch=[pltpu.VMEM((P_SIZE, B, columns), jnp.float32)],
    )
    return result


def solution(mesh):
    n_col, n_row = mesh.shape["col"], mesh.shape["row"]
    split = Mesh(
        mesh.devices.reshape(n_col // P_SIZE, P_SIZE, n_row // 2, 2),
        ("hi", "lo", "rh", "rl"),
    )
    spec = P(("rh", "rl"), ("hi", "lo"))
    return jax.shard_map(
        on_device,
        mesh=split,
        in_specs=(spec, spec, spec),
        out_specs=spec,
        check_vma=False,
    )
```

```python
import functools

import jax
import jax.numpy as jnp
from jax import lax
from jax.experimental import pallas as pl
from jax.experimental.pallas import tpu as pltpu
from jax.sharding import Mesh
from jax.sharding import PartitionSpec as P

B = 256
P_SIZE = 4
ARC_ROWS = 128
NB = 128
SUB = 8
HIGHEST = lax.Precision.HIGHEST


def dot(left, right):
    return jnp.dot(left, right, precision=HIGHEST, preferred_element_type=jnp.float32)


def dot_t(left, right):
    return lax.dot_general(
        left, right, (((0,), (0,)), ((), ())), precision=HIGHEST, preferred_element_type=jnp.float32
    )


def lane(value, at):
    return jnp.broadcast_to(value[:, at : at + 1], (SUB, NB))


def row(value, at):
    return jnp.broadcast_to(value[at : at + 1, :], (SUB, NB))


def inverse_factor(rows):
    n = NB // SUB
    row_id = lax.broadcasted_iota(jnp.int32, (SUB, NB), 0)
    col_id = lax.broadcasted_iota(jnp.int32, (SUB, NB), 1)
    order = range(SUB)
    ahead = [lane(rows[0], m) for m in order]
    for b in range(n):
        j = b * SUB
        pivot = {(k, m): row(ahead[m], k) for k in order for m in range(k, SUB)}
        below = [[lane(rows[r], j + k) for k in order] for r in range(b + 1, n)]
        if b + 1 < n:
            ahead = [lane(rows[b + 1], j + SUB + m) for m in order]
        scale, left = [], []
        for k in order:
            scale.append(lax.rsqrt(pivot[k, k]))
            for m in range(k + 1, SUB):
                pivot[k, m] = pivot[k, m] * scale[k]
            for m in range(k + 1, SUB):
                for q in range(m, SUB):
                    pivot[m, q] = pivot[m, q] - pivot[k, m] * pivot[k, q]
            if b + 1 < n:
                part = below[0][k]
                for m in range(k):
                    part = part - pivot[m, k] * left[m]
                part = part * scale[k]
                left.append(part)
                for m in order:
                    ahead[m] = ahead[m] - part * row(part, m)
        inside = (col_id >= j) & (col_id < j + SUB)
        head = jnp.where(inside, jnp.where(col_id - j == row_id, 1.0, 0.0), rows[b])
        top = []
        for k in order:
            part = row(head, k)
            for m in range(k):
                part = part - pivot[m, k] * top[m]
            top.append(part * scale[k])
        if b + 1 < n:
            solved = [None] * SUB
            for k in reversed(order):
                part = top[k]
                for m in range(k + 1, SUB):
                    part = part - pivot[k, m] * solved[m]
                solved[k] = part * scale[k]
            for r in range(b + 1, n):
                body = jnp.where(inside, 0.0, rows[r])
                for k in order:
                    body = body - below[r - b - 1][k] * solved[k]
                rows[r] = body
        strip = top[0]
        for k in range(1, SUB):
            strip = jnp.where(row_id == k, top[k], strip)
        rows[b] = jnp.where(col_id < j + SUB, strip, 0.0)
    return rows


PAIRS = [(r, c) for r in range(P_SIZE) for c in range(r, P_SIZE)]
HALF = len(PAIRS) // 2
PIECES = 4 * P_SIZE


def split(value):
    high = value.astype(jnp.bfloat16)
    return high, (value - high.astype(jnp.float32)).astype(jnp.bfloat16)


def left_parts(value):
    high, low = split(value)
    return jnp.concatenate([high, high, low], axis=0)


def right_parts(value):
    high, low = split(value)
    return jnp.concatenate([high, low, high], axis=0)


def parts_dot(left, right):
    return lax.dot_general(
        left, right, (((0,), (0,)), ((), ())), preferred_element_type=jnp.float32
    )


def mask_kernel(place_ref, arcs_ref, slab_ref, rows_ref, *refs):
    pieces, work = refs[:-1], refs[-1]
    top = slab_ref.shape[0]
    work[:top, :] = slab_ref[...]
    for a in range(arcs_ref.shape[0]):
        live = arcs_ref[a, 0].astype(jnp.float32)
        at = a * ARC_ROWS
        work[top + at : top + at + ARC_ROWS, :] = rows_ref[at : at + ARC_ROWS, :] * live
    count = pieces[0].shape[0]
    for s, piece in enumerate(pieces):
        start = pl.multiple_of((place_ref[4] ^ s) * count, 16)
        piece[...] = work[pl.ds(start, count), :]


def upper_products_kernel(place_ref, *refs):
    blocks, (keep_ref, send_ref, columns, work) = refs[:-4], refs[-4:]
    side, place, me = place_ref[0], place_ref[1] * P_SIZE + place_ref[2], place_ref[4]
    for s, block in enumerate(blocks):
        columns[me ^ s] = block[...]
    right = [right_parts(columns[c]) for c in range(P_SIZE)]
    at = 0
    for r in range(P_SIZE):
        wide = jnp.concatenate(right[r:], axis=1)
        product = parts_dot(left_parts(columns[r]), wide)
        for c in range(P_SIZE - r):
            work[at * B : (at + 1) * B, :] = product[:, c * B : (c + 1) * B]
            at += 1
    count = keep_ref.shape[1]
    for t in range(PIECES // 2):
        piece = place ^ t
        here = pl.multiple_of((side * (PIECES // 2) + piece) * count, SUB)
        there = pl.multiple_of(((1 - side) * (PIECES // 2) + piece) * count, SUB)
        keep_ref[t] = work[pl.ds(here, count), :]
        send_ref[t] = work[pl.ds(there, count), :]


def all_products_kernel(n_left, place_ref, *refs):
    blocks, (_, keep_ref, send_ref, columns, panels, work) = refs[:-6], refs[-6:]
    left_blocks, right_blocks = blocks[:n_left], blocks[n_left:]
    side, place, me = place_ref[0], place_ref[1] * P_SIZE + place_ref[2], place_ref[4]
    for s, block in enumerate(right_blocks):
        columns[me ^ s] = block[...]
    for s, block in enumerate(left_blocks):
        panels[me ^ s] = block[...]
    left = panels if left_blocks else columns
    first = columns.shape[0] - P_SIZE
    right = jnp.concatenate([right_parts(columns[first + c]) for c in range(P_SIZE)], axis=1)
    for r in range(P_SIZE):
        product = parts_dot(left_parts(left[r]), right)
        for b in range(P_SIZE):
            work[r * P_SIZE + b] = product[:, b * B : (b + 1) * B]
    for t in range(2 * P_SIZE):
        spot = place ^ t
        block = (2 * (spot // P_SIZE)) * P_SIZE + spot % P_SIZE
        keep_ref[t] = work[block + side * P_SIZE]
        send_ref[t] = work[block + (1 - side) * P_SIZE]


def tie_kernel(value_ref, after_ref, out_ref):
    del value_ref, after_ref, out_ref


def behind(value, after):
    return pl.pallas_call(
        tie_kernel,
        out_shape=jax.ShapeDtypeStruct(value.shape, value.dtype),
        in_specs=[pl.BlockSpec(memory_space=pl.ANY)] * 2,
        out_specs=pl.BlockSpec(memory_space=pl.ANY),
        input_output_aliases={0: 0},
        name="behind",
    )(value, after)


def add_kernel(left_ref, right_ref, after_ref, out_ref):
    del after_ref
    out_ref[...] = left_ref[...] + right_ref[...]


def sum_kernel(*refs):
    parts, out_ref = refs[:-2], refs[-1]
    total = parts[0][...]
    for part in parts[1:]:
        total = total + part[...]
    out_ref[...] = total


def on_chip(kernel, shapes, name, *operands, scratch=(), scalars=0, after=()):
    done = pl.pallas_call(
        kernel,
        out_shape=[jax.ShapeDtypeStruct(shape, jnp.float32) for shape in shapes],
        in_specs=[pl.BlockSpec(memory_space=pltpu.SMEM)] * scalars
        + [pl.BlockSpec(memory_space=pltpu.VMEM)] * (len(operands) - scalars)
        + [pl.BlockSpec(memory_space=pl.ANY)] * len(after),
        out_specs=[pl.BlockSpec(memory_space=pltpu.VMEM)] * len(shapes),
        scratch_shapes=list(scratch),
        compiler_params=pltpu.CompilerParams(vmem_limit_bytes=16 * 1024 * 1024),
        name=name,
    )(*operands, *after)
    return list(done)


def collect_kernel(place_ref, mine_ref, other_ref, gram_ref, token_ref):
    side, high, low = place_ref[0], place_ref[1], place_ref[2]
    at = high * P_SIZE + low
    rows = mine_ref.shape[1]
    token_ref[...] = jnp.zeros_like(token_ref)
    for s in range(2):
        for p in range(PIECES // 2):
            start = ((s * PIECES) // 2 + p) * rows
            end = start + rows
            while start < end:
                block, first = start // B, start % B
                count = min(end - start, B - first)
                skip = rows - (end - start)

                @pl.when(side == s)
                def _(block=block, first=first, count=count, skip=skip, p=p):
                    gram_ref[block, first : first + count] = mine_ref[p ^ at, skip : skip + count]

                @pl.when(side != s)
                def _(block=block, first=first, count=count, skip=skip, p=p):
                    gram_ref[block, first : first + count] = other_ref[p ^ at, skip : skip + count]

                start += count


def factor_step_kernel(n, gram_ref, *rest):
    if n > 1:
        row_ref, inverse_ref, next_ref, work, inv = rest
    else:
        inverse_ref, work, inv = rest
    for c in range(n):
        work[:, c * B : (c + 1) * B] = gram_ref[c]
    width = n * B

    def step(b, carry):
        start = pl.multiple_of(b * NB, NB)
        rows = [
            work[pl.ds(pl.multiple_of(start + r * SUB, SUB), SUB), pl.ds(start, NB)]
            for r in range(NB // SUB)
        ]
        right = inverse_factor(rows)
        for r in range(NB // SUB):
            inv[pl.ds(pl.multiple_of(start + r * SUB, SUB), SUB), :] = right[r]

        @pl.when(b == 0)
        def _():
            panel = dot(inv[:NB, :], work[:NB, NB:])
            work[:NB, NB:] = panel
            work[NB:, NB:] = work[NB:, NB:] - dot_t(panel[:, :NB], panel)

        return carry

    lax.fori_loop(0, B // NB, step, 0)
    first, second = inv[:NB, :], inv[NB:, :]
    inverse_ref[:NB, :NB] = first
    inverse_ref[:NB, NB:] = jnp.zeros((NB, NB), jnp.float32)
    inverse_ref[NB:, :NB] = -dot(second, dot_t(work[:NB, NB:B], first))
    inverse_ref[NB:, NB:] = second
    if n > 1:
        work[NB:, B:] = dot(second, work[NB:, B:])
        row = work[:, B:]
        row_ref[...] = row
        at = n
        for r in range(1, n):
            left = row[:, (r - 1) * B : r * B]
            for c in range(r, n):
                next_ref[at - n] = gram_ref[at] - dot_t(left, row[:, (c - 1) * B : c * B])
                at += 1


def factor(gram):
    rows, inverses = [], []
    for n in range(P_SIZE, 0, -1):
        shapes = [(B, (n - 1) * B), (B, B), (n * (n - 1) // 2, B, B)] if n > 1 else [(B, B)]
        done = on_chip(
            functools.partial(factor_step_kernel, n),
            shapes,
            "factor_step",
            gram,
            scratch=[pltpu.VMEM((B, n * B), jnp.float32), pltpu.VMEM((B, NB), jnp.float32)],
        )
        if n > 1:
            row, inverse, gram = done
            rows.append(row)
        else:
            (inverse,) = done
        inverses.append(inverse)
    return rows, inverses


def solve_kernel(place_ref, *refs):
    rows, inverses = refs[: P_SIZE - 1], refs[P_SIZE - 1 : 2 * P_SIZE - 1]
    gram_ref, own_refs, out_ref, own_ref = refs[-P_SIZE - 3], refs[-P_SIZE - 2 : -2], refs[-2], refs[-1]
    row_index, col_index = 2 * place_ref[1] + place_ref[0], place_ref[3]

    @pl.when(col_index >= P_SIZE)
    def _():
        for t in range(P_SIZE):
            own_ref[row_index ^ t] = own_refs[t][...]

    for c in range(P_SIZE):

        @pl.when(col_index == c)
        def _(c=c):
            for r in range(P_SIZE):
                own_ref[r] = gram_ref[PAIRS.index((min(r, c), c))]

    done = []
    for i in range(P_SIZE):
        block = own_ref[i]
        for k in range(i):
            off = (i - k - 1) * B
            block = block - dot_t(rows[k][:, off : off + B], done[k])
        block = dot(inverses[i][...], block)
        done.append(block)

        @pl.when(row_index == i)
        def _(block=block):
            rows_at = i * B + lax.broadcasted_iota(jnp.int32, block.shape, 0)
            cols_at = col_index * B + lax.broadcasted_iota(jnp.int32, block.shape, 1)
            out_ref[...] = jnp.where(cols_at >= rows_at, block, 0.0)


def from_first(value, n_hi):
    at = lax.axis_index("hi")
    have = 1
    while have < n_hi:
        more = min(have, n_hi - have)
        got = lax.ppermute(value, "hi", [(g, g + have) for g in range(more)])
        value = jnp.where(at < have, value, got)
        have += more
    return value


def exchange(value, high_bits, low_bits):
    bits = low_bits * 2 + high_bits
    return lax.ppermute(value, ("lo", "rh"), [(i, i ^ bits) for i in range(2 * P_SIZE)])


def swap(value, axis="rl"):
    return lax.ppermute(value, axis, [(0, 1), (1, 0)])


def across_rows(value, bits):
    return lax.ppermute(value, ("rh", "rl"), [(i, i ^ bits) for i in range(P_SIZE)])


def collected(parts):
    got = [parts[0]]
    for t in range(1, 2 * P_SIZE):
        got.append(exchange(parts[t], t // P_SIZE, t % P_SIZE))
    return got


def spread(piece):
    y, z, x = (0, 1), (0, 2), (1, 0)
    by_z, by_y, by_x = exchange(piece, *z), exchange(piece, *y), exchange(piece, *x)
    by_zy, by_yx, by_xz = exchange(by_z, *y), exchange(by_y, *x), exchange(by_x, *z)
    by_zyx = exchange(by_zy, *x)
    return jnp.stack([piece, by_y, by_z, by_zy, by_x, by_yx, by_xz, by_zyx])


def on_device(r_slab, arc_rows, arc_blocks):
    n_hi = lax.axis_size("hi")
    low = lax.axis_index("lo")
    high_row, side = lax.axis_index("rh"), lax.axis_index("rl")
    col_index = lax.axis_index("hi") * P_SIZE + low
    row_index = high_row * 2 + side
    columns = arc_rows.shape[1]
    in_two = n_hi == 2
    owners = ("hi", "lo") if in_two else ("lo",)
    shares = P_SIZE * n_hi if in_two else P_SIZE
    me = col_index if in_two else low
    place = jnp.stack([side, high_row, low, col_index, me]).astype(jnp.int32)
    total = r_slab.shape[0] + arc_rows.shape[0]
    share = (total // shares, columns)
    blocks = on_chip(
        mask_kernel,
        [share] * shares,
        "mask",
        place,
        arc_blocks,
        r_slab,
        arc_rows,
        scalars=2,
        scratch=[pltpu.VMEM((total, columns), jnp.float32)],
    )
    blocks = blocks[:1] + [
        lax.ppermute(blocks[s], owners, [(i, i ^ s) for i in range(shares)])
        for s in range(1, shares)
    ]
    panels = [] if in_two else [from_first(block, n_hi) for block in blocks]

    half = (PIECES // 2, len(PAIRS) * B // PIECES, B)
    gathered = pltpu.VMEM((shares, *share), jnp.float32)
    keep, send = on_chip(
        upper_products_kernel,
        [half, half],
        "upper_products",
        place,
        *blocks,
        scalars=1,
        scratch=[gathered, pltpu.VMEM((len(PAIRS) * B, B), jnp.float32)],
    )
    gram = collected(keep + swap(send))
    gram = functools.reduce(jnp.add, gram)
    half = (2 * P_SIZE, B, B)
    cross, send = on_chip(
        functools.partial(all_products_kernel, len(panels)),
        [half, half],
        "all_products",
        place,
        *panels,
        *blocks,
        scalars=1,
        scratch=[gathered, gathered, pltpu.VMEM((P_SIZE * P_SIZE, B, B), jnp.float32)],
        after=(keep,),
    )
    cross = cross + swap(send)
    piece = gram + swap(gram, "hi") if in_two else from_first(gram, n_hi)
    pieces = spread(piece)
    gram, token = on_chip(
        collect_kernel,
        [(len(PAIRS), B, B), (SUB, NB)],
        "collect",
        place,
        pieces,
        swap(pieces),
        scalars=1,
    )
    cross = collected(behind(cross, token))
    rows, inverses = factor(gram)
    (mine,) = on_chip(sum_kernel, [(B, columns)], "sum_places", *cross, after=(rows[1],))
    if in_two:
        other = swap(mine, "hi")
        (mine,) = on_chip(add_kernel, [(B, columns)], "add_groups", mine, other, after=(rows[2],))
    own = [mine] + [across_rows(mine, bits) for bits in range(1, P_SIZE)]

    (result,) = on_chip(
        solve_kernel,
        [(B, columns)],
        "solve",
        place,
        *rows,
        *inverses,
        gram,
        *own,
        scalars=1,
        scratch=[pltpu.VMEM((P_SIZE, B, columns), jnp.float32)],
    )
    return result


def solution(mesh):
    n_col, n_row = mesh.shape["col"], mesh.shape["row"]
    split = Mesh(
        mesh.devices.reshape(n_col // P_SIZE, P_SIZE, n_row // 2, 2),
        ("hi", "lo", "rh", "rl"),
    )
    spec = P(("rh", "rl"), ("hi", "lo"))
    return jax.shard_map(
        on_device,
        mesh=split,
        in_specs=(spec, spec, spec),
        out_specs=spec,
        check_vma=False,
    )
```

```python
import functools

import jax
import jax.numpy as jnp
from jax import lax
from jax.experimental import pallas as pl
from jax.experimental.pallas import tpu as pltpu
from jax.sharding import Mesh
from jax.sharding import PartitionSpec as P

B = 256
P_SIZE = 4
ARC_ROWS = 128
NB = 128
SUB = 8


def split(value):
    high = value.astype(jnp.bfloat16)
    return high, (value - high.astype(jnp.float32)).astype(jnp.bfloat16)


def left_parts(value, axis=0):
    high, low = split(value)
    return jnp.concatenate([high, high, low], axis=axis)


def right_parts(value):
    high, low = split(value)
    return jnp.concatenate([high, low, high], axis=0)


def parts_dot(left, right):
    return lax.dot_general(
        left, right, (((0,), (0,)), ((), ())), preferred_element_type=jnp.float32
    )


def dot(left, right):
    return jnp.dot(left_parts(left, 1), right_parts(right), preferred_element_type=jnp.float32)


def dot_t(left, right):
    return parts_dot(left_parts(left), right_parts(right))


def lane(value, at):
    return jnp.broadcast_to(value[:, at : at + 1], (SUB, NB))


def row(value, at):
    return jnp.broadcast_to(value[at : at + 1, :], (SUB, NB))


def inverse_factor(rows):
    n = NB // SUB
    row_id = lax.broadcasted_iota(jnp.int32, (SUB, NB), 0)
    col_id = lax.broadcasted_iota(jnp.int32, (SUB, NB), 1)
    order = range(SUB)
    ahead = [lane(rows[0], m) for m in order]
    for b in range(n):
        j = b * SUB
        pivot = {(k, m): row(ahead[m], k) for k in order for m in range(k, SUB)}
        below = [[lane(rows[r], j + k) for k in order] for r in range(b + 1, n)]
        if b + 1 < n:
            ahead = [lane(rows[b + 1], j + SUB + m) for m in order]
        scale, left = [], []
        for k in order:
            scale.append(lax.rsqrt(pivot[k, k]))
            for m in range(k + 1, SUB):
                pivot[k, m] = pivot[k, m] * scale[k]
            for m in range(k + 1, SUB):
                for q in range(m, SUB):
                    pivot[m, q] = pivot[m, q] - pivot[k, m] * pivot[k, q]
            if b + 1 < n:
                part = below[0][k]
                for m in range(k):
                    part = part - pivot[m, k] * left[m]
                part = part * scale[k]
                left.append(part)
                for m in order:
                    ahead[m] = ahead[m] - part * row(part, m)
        inside = (col_id >= j) & (col_id < j + SUB)
        head = jnp.where(inside, jnp.where(col_id - j == row_id, 1.0, 0.0), rows[b])
        top = []
        for k in order:
            part = row(head, k)
            for m in range(k):
                part = part - pivot[m, k] * top[m]
            top.append(part * scale[k])
        if b + 1 < n:
            solved = [None] * SUB
            for k in reversed(order):
                part = top[k]
                for m in range(k + 1, SUB):
                    part = part - pivot[k, m] * solved[m]
                solved[k] = part * scale[k]
            for r in range(b + 1, n):
                body = jnp.where(inside, 0.0, rows[r])
                for k in order:
                    body = body - below[r - b - 1][k] * solved[k]
                rows[r] = body
        strip = top[0]
        for k in range(1, SUB):
            strip = jnp.where(row_id == k, top[k], strip)
        rows[b] = jnp.where(col_id < j + SUB, strip, 0.0)
    return rows


PAIRS = [(r, c) for r in range(P_SIZE) for c in range(r, P_SIZE)]
HALF = len(PAIRS) // 2
PIECES = 4 * P_SIZE


def mask_kernel(arcs_ref, slab_ref, rows_ref, out_ref):
    top = slab_ref.shape[0]
    out_ref[:top, :] = slab_ref[...]
    for a in range(arcs_ref.shape[0]):
        live = arcs_ref[a, 0].astype(jnp.float32)
        at = a * ARC_ROWS
        out_ref[top + at : top + at + ARC_ROWS, :] = rows_ref[at : at + ARC_ROWS, :] * live


def upper_products_kernel(place_ref, blocks_ref, keep_ref, send_ref, other_ref, work):
    side, group = place_ref[0], place_ref[4]
    right = [right_parts(blocks_ref[c]) for c in range(P_SIZE)]
    at = 0
    for r in range(P_SIZE):
        wide = jnp.concatenate(right[r:], axis=1)
        product = parts_dot(left_parts(blocks_ref[r]), wide)
        for c in range(P_SIZE - r):
            work[at] = product[:, c * B : (c + 1) * B]
            at += 1
    for i in range(HALF):
        keep_ref[i] = work[side * HALF + i]
        send_ref[i] = work[(1 - side) * HALF + i]
    count = other_ref.shape[1]
    start = pl.multiple_of(jnp.where(group == 0, count, 0), 16)
    for c in range(P_SIZE):
        other_ref[c] = blocks_ref[c, pl.ds(start, count), :]


def all_products_kernel(place_ref, blocks_ref, got_ref, _, keep_ref, send_ref, pair, work):
    side, group = place_ref[0], place_ref[4]
    count = got_ref.shape[1]
    if count < blocks_ref.shape[1]:
        start = pl.multiple_of(jnp.where(group == 0, 0, count), 16)
        mine = jnp.minimum(group, 1)
        for c in range(P_SIZE):
            pair[mine, c] = blocks_ref[c, pl.ds(start, count), :]
            pair[1 - mine, c] = got_ref[c]
        left, right = pair.at[0], pair.at[1]
    else:
        left, right = got_ref, blocks_ref
    right = jnp.concatenate([right_parts(right[c]) for c in range(P_SIZE)], axis=1)
    for r in range(P_SIZE):
        product = parts_dot(left_parts(left[r]), right)
        for b in range(P_SIZE):
            work[r, b] = product[:, b * B : (b + 1) * B]
    for a in range(2):
        keep_ref[a] = work[2 * a + side]
        send_ref[a] = work[2 * a + 1 - side]


def tie_kernel(value_ref, after_ref, out_ref):
    del value_ref, after_ref, out_ref


def behind(value, after):
    return pl.pallas_call(
        tie_kernel,
        out_shape=jax.ShapeDtypeStruct(value.shape, value.dtype),
        in_specs=[pl.BlockSpec(memory_space=pl.ANY)] * 2,
        out_specs=pl.BlockSpec(memory_space=pl.ANY),
        input_output_aliases={0: 0},
        name="behind",
    )(value, after)


def add_kernel(left_ref, right_ref, after_ref, out_ref):
    del after_ref
    out_ref[...] = left_ref[...] + right_ref[...]


def sum_kernel(parts_ref, _, out_ref):
    total = parts_ref[0]
    for i in range(1, parts_ref.shape[0]):
        total = total + parts_ref[i]
    out_ref[...] = total


def on_chip(kernel, shapes, name, *operands, scratch=(), scalars=0, after=()):
    done = pl.pallas_call(
        kernel,
        out_shape=[jax.ShapeDtypeStruct(shape, jnp.float32) for shape in shapes],
        in_specs=[pl.BlockSpec(memory_space=pltpu.SMEM)] * scalars
        + [pl.BlockSpec(memory_space=pltpu.VMEM)] * (len(operands) - scalars)
        + [pl.BlockSpec(memory_space=pl.ANY)] * len(after),
        out_specs=[pl.BlockSpec(memory_space=pltpu.VMEM)] * len(shapes),
        scratch_shapes=list(scratch),
        compiler_params=pltpu.CompilerParams(vmem_limit_bytes=16 * 1024 * 1024),
        name=name,
    )(*operands, *after)
    return list(done)


def collect_kernel(place_ref, mine_ref, other_ref, _, gram_ref, token_ref):
    side, high, low = place_ref[0], place_ref[1], place_ref[2]
    token_ref[...] = jnp.zeros_like(token_ref)
    at = high * P_SIZE + low
    rows = mine_ref.shape[1]
    for s in range(2):
        for p in range(PIECES // 2):
            start = ((s * PIECES) // 2 + p) * rows
            end = start + rows
            while start < end:
                block, first = start // B, start % B
                count = min(end - start, B - first)
                skip = rows - (end - start)

                @pl.when(side == s)
                def _(block=block, first=first, count=count, skip=skip, p=p):
                    gram_ref[block, first : first + count] = mine_ref[p ^ at, skip : skip + count]

                @pl.when(side != s)
                def _(block=block, first=first, count=count, skip=skip, p=p):
                    gram_ref[block, first : first + count] = other_ref[p ^ at, skip : skip + count]

                start += count


def factor_step_kernel(n, gram_ref, *rest):
    if n > 1:
        row_ref, inverse_ref, next_ref, work, inv = rest
    else:
        inverse_ref, work, inv = rest
    for c in range(n):
        work[:, c * B : (c + 1) * B] = gram_ref[c]
    width = n * B

    def step(b, carry):
        start = pl.multiple_of(b * NB, NB)
        rows = [
            work[pl.ds(pl.multiple_of(start + r * SUB, SUB), SUB), pl.ds(start, NB)]
            for r in range(NB // SUB)
        ]
        right = inverse_factor(rows)
        for r in range(NB // SUB):
            inv[pl.ds(pl.multiple_of(start + r * SUB, SUB), SUB), :] = right[r]

        @pl.when(b == 0)
        def _():
            panel = dot(inv[:NB, :], work[:NB, NB:])
            work[:NB, NB:] = panel
            work[NB:, NB:] = work[NB:, NB:] - dot_t(panel[:, :NB], panel)

        return carry

    lax.fori_loop(0, B // NB, step, 0)
    first, second = inv[:NB, :], inv[NB:, :]
    inverse_ref[:NB, :NB] = first
    inverse_ref[:NB, NB:] = jnp.zeros((NB, NB), jnp.float32)
    inverse_ref[NB:, :NB] = -dot(second, dot_t(work[:NB, NB:B], first))
    inverse_ref[NB:, NB:] = second
    if n > 1:
        work[NB:, B:] = dot(second, work[NB:, B:])
        row = work[:, B:]
        row_ref[...] = row
        at = n
        for r in range(1, n):
            left = row[:, (r - 1) * B : r * B]
            for c in range(r, n):
                next_ref[at - n] = gram_ref[at] - dot_t(left, row[:, (c - 1) * B : c * B])
                at += 1


def factor(gram):
    rows, inverses = [], []
    for n in range(P_SIZE, 0, -1):
        shapes = [(B, (n - 1) * B), (B, B), (n * (n - 1) // 2, B, B)] if n > 1 else [(B, B)]
        done = on_chip(
            functools.partial(factor_step_kernel, n),
            shapes,
            "factor_step",
            gram,
            scratch=[pltpu.VMEM((B, n * B), jnp.float32), pltpu.VMEM((B, NB), jnp.float32)],
        )
        if n > 1:
            row, inverse, gram = done
            rows.append(row)
        else:
            (inverse,) = done
        inverses.append(inverse)
    return rows, inverses


def solve_kernel(place_ref, *refs):
    rows, inverses = refs[: P_SIZE - 1], refs[P_SIZE - 1 : 2 * P_SIZE - 1]
    gram_ref, own_refs, out_ref, own_ref = refs[-P_SIZE - 3], refs[-P_SIZE - 2 : -2], refs[-2], refs[-1]
    row_index, col_index = 2 * place_ref[1] + place_ref[0], place_ref[3]

    @pl.when(col_index >= P_SIZE)
    def _():
        for t in range(P_SIZE):
            own_ref[row_index ^ t] = own_refs[t][...]

    for c in range(P_SIZE):

        @pl.when(col_index == c)
        def _(c=c):
            for r in range(P_SIZE):
                own_ref[r] = gram_ref[PAIRS.index((min(r, c), c))]

    done = []
    for i in range(P_SIZE):
        block = own_ref[i]
        for k in range(i):
            off = (i - k - 1) * B
            block = block - dot_t(rows[k][:, off : off + B], done[k])
        block = dot(inverses[i][...], block)
        done.append(block)

        @pl.when(row_index == i)
        def _(block=block):
            rows_at = i * B + lax.broadcasted_iota(jnp.int32, block.shape, 0)
            cols_at = col_index * B + lax.broadcasted_iota(jnp.int32, block.shape, 1)
            out_ref[...] = jnp.where(cols_at >= rows_at, block, 0.0)


def from_first(value, n_hi):
    at = lax.axis_index("hi")
    have = 1
    while have < n_hi:
        more = min(have, n_hi - have)
        got = lax.ppermute(value, "hi", [(g, g + have) for g in range(more)])
        value = jnp.where(at < have, value, got)
        have += more
    return value


def exchange(value, high_bits, low_bits):
    bits = low_bits * 2 + high_bits
    return lax.ppermute(value, ("lo", "rh"), [(i, i ^ bits) for i in range(2 * P_SIZE)])


def swap(value, axis="rl"):
    return lax.ppermute(value, axis, [(0, 1), (1, 0)])


def across_rows(value, bits):
    return lax.ppermute(value, ("rh", "rl"), [(i, i ^ bits) for i in range(P_SIZE)])


def spread(piece):
    y, z, x = (0, 1), (0, 2), (1, 0)
    by_z, by_y, by_x = exchange(piece, *z), exchange(piece, *y), exchange(piece, *x)
    by_zy, by_yx, by_xz = exchange(by_z, *y), exchange(by_y, *x), exchange(by_x, *z)
    by_zyx = exchange(by_zy, *x)
    return jnp.stack([piece, by_y, by_z, by_zy, by_x, by_yx, by_xz, by_zyx])


def on_device(r_slab, arc_rows, arc_blocks):
    n_hi = lax.axis_size("hi")
    low = lax.axis_index("lo")
    high_row, side = lax.axis_index("rh"), lax.axis_index("rl")
    col_index = lax.axis_index("hi") * P_SIZE + low
    row_index = high_row * 2 + side
    columns = arc_rows.shape[1]
    in_two = n_hi == 2
    place = jnp.stack([side, high_row, low, col_index, lax.axis_index("hi")]).astype(jnp.int32)
    total = r_slab.shape[0] + arc_rows.shape[0]
    share = total // P_SIZE
    (stacked,) = on_chip(
        mask_kernel, [(total, columns)], "mask", arc_blocks, r_slab, arc_rows, scalars=1
    )
    blocks = lax.all_to_all(stacked.reshape(P_SIZE, share, columns), "lo", 0, 0)

    half = (HALF, B, B)
    keep, send, other = on_chip(
        upper_products_kernel,
        [half, half, (P_SIZE, share // 2, columns)],
        "upper_products",
        place,
        blocks,
        scalars=1,
        scratch=[pltpu.VMEM((len(PAIRS), B, B), jnp.float32)],
    )
    got = swap(other, "hi") if in_two else from_first(blocks, n_hi)
    gram = keep + swap(send)
    gram = lax.all_to_all(gram.reshape(2 * P_SIZE, -1, B), ("rh", "lo"), 0, 0).sum(axis=0)
    half = (2, P_SIZE, B, B)
    cross, send = on_chip(
        all_products_kernel,
        [half, half],
        "all_products",
        place,
        blocks,
        got,
        scalars=1,
        scratch=[
            pltpu.VMEM((2, P_SIZE, share // 2, columns), jnp.float32),
            pltpu.VMEM((P_SIZE, P_SIZE, B, B), jnp.float32),
        ],
        after=(gram,),
    )
    cross = cross + swap(send)
    piece = from_first(gram, n_hi)
    pieces = spread(piece)
    gram, token = on_chip(
        collect_kernel,
        [(len(PAIRS), B, B), (SUB, NB)],
        "collect",
        place,
        pieces,
        swap(pieces),
        scalars=1,
        after=(cross,),
    )
    cross = behind(cross.reshape(2 * P_SIZE, B, B), token)
    cross = lax.all_to_all(cross, ("rh", "lo"), 0, 0)
    rows, inverses = factor(gram)
    (mine,) = on_chip(sum_kernel, [(B, columns)], "sum_places", cross, after=(rows[1],))
    if in_two:
        other = swap(mine, "hi")
        (mine,) = on_chip(add_kernel, [(B, columns)], "add_groups", mine, other, after=(rows[2],))
    own = [mine] + [across_rows(mine, bits) for bits in range(1, P_SIZE)]

    (result,) = on_chip(
        solve_kernel,
        [(B, columns)],
        "solve",
        place,
        *rows,
        *inverses,
        gram,
        *own,
        scalars=1,
        scratch=[pltpu.VMEM((P_SIZE, B, columns), jnp.float32)],
    )
    return result


def solution(mesh):
    n_col, n_row = mesh.shape["col"], mesh.shape["row"]
    split = Mesh(
        mesh.devices.reshape(n_col // P_SIZE, P_SIZE, n_row // 2, 2),
        ("hi", "lo", "rh", "rl"),
    )
    spec = P(("rh", "rl"), ("hi", "lo"))
    return jax.shard_map(
        on_device,
        mesh=split,
        in_specs=(spec, spec, spec),
        out_specs=spec,
        check_vma=False,
    )
```

```python
import functools

import jax
import jax.numpy as jnp
from jax import lax
from jax.experimental import pallas as pl
from jax.experimental.pallas import tpu as pltpu
from jax.sharding import Mesh
from jax.sharding import PartitionSpec as P

B = 256
P_SIZE = 4
ARC_ROWS = 128
NB = 128
SUB = 8


def split(value):
    high = value.astype(jnp.bfloat16)
    return high, (value - high.astype(jnp.float32)).astype(jnp.bfloat16)


def left_parts(value, axis=0):
    high, low = split(value)
    return jnp.concatenate([high, high, low], axis=axis)


def right_parts(value):
    high, low = split(value)
    return jnp.concatenate([high, low, high], axis=0)


def parts_dot(left, right):
    return lax.dot_general(
        left, right, (((0,), (0,)), ((), ())), preferred_element_type=jnp.float32
    )


def dot(left, right):
    return jnp.dot(left_parts(left, 1), right_parts(right), preferred_element_type=jnp.float32)


def dot_t(left, right):
    return parts_dot(left_parts(left), right_parts(right))


def lane(value, at):
    return jnp.broadcast_to(value[:, at : at + 1], (SUB, NB))


def row(value, at):
    return jnp.broadcast_to(value[at : at + 1, :], (SUB, NB))


def inverse_factor(rows):
    n = NB // SUB
    row_id = lax.broadcasted_iota(jnp.int32, (SUB, NB), 0)
    col_id = lax.broadcasted_iota(jnp.int32, (SUB, NB), 1)
    order = range(SUB)
    ahead = [lane(rows[0], m) for m in order]
    for b in range(n):
        j = b * SUB
        pivot = {(k, m): row(ahead[m], k) for k in order for m in range(k, SUB)}
        below = [[lane(rows[r], j + k) for k in order] for r in range(b + 1, n)]
        if b + 1 < n:
            ahead = [lane(rows[b + 1], j + SUB + m) for m in order]
        scale, left = [], []
        for k in order:
            scale.append(lax.rsqrt(pivot[k, k]))
            for m in range(k + 1, SUB):
                pivot[k, m] = pivot[k, m] * scale[k]
            for m in range(k + 1, SUB):
                for q in range(m, SUB):
                    pivot[m, q] = pivot[m, q] - pivot[k, m] * pivot[k, q]
            if b + 1 < n:
                part = below[0][k]
                for m in range(k):
                    part = part - pivot[m, k] * left[m]
                part = part * scale[k]
                left.append(part)
                for m in order:
                    ahead[m] = ahead[m] - part * row(part, m)
        inside = (col_id >= j) & (col_id < j + SUB)
        head = jnp.where(inside, jnp.where(col_id - j == row_id, 1.0, 0.0), rows[b])
        top = []
        for k in order:
            part = row(head, k)
            for m in range(k):
                part = part - pivot[m, k] * top[m]
            top.append(part * scale[k])
        if b + 1 < n:
            solved = [None] * SUB
            for k in reversed(order):
                part = top[k]
                for m in range(k + 1, SUB):
                    part = part - pivot[k, m] * solved[m]
                solved[k] = part * scale[k]
            for r in range(b + 1, n):
                body = jnp.where(inside, 0.0, rows[r])
                for k in order:
                    body = body - below[r - b - 1][k] * solved[k]
                rows[r] = body
        strip = top[0]
        for k in range(1, SUB):
            strip = jnp.where(row_id == k, top[k], strip)
        rows[b] = jnp.where(col_id < j + SUB, strip, 0.0)
    return rows


PAIRS = [(r, c) for r in range(P_SIZE) for c in range(r, P_SIZE)]
HALF = len(PAIRS) // 2
PIECES = 4 * P_SIZE


def mask_kernel(place_ref, arcs_ref, slab_ref, rows_ref, *refs):
    pieces, work, sems = refs[:-2], refs[-2], refs[-1]
    top = slab_ref.shape[0]
    arcs = arcs_ref.shape[0]
    copies = [pltpu.make_async_copy(slab_ref, work.at[pl.ds(0, top)], sems.at[arcs])]
    for a in range(arcs):
        part = pl.ds(a * ARC_ROWS, ARC_ROWS)
        spot = pl.ds(top + a * ARC_ROWS, ARC_ROWS)
        copies.append(pltpu.make_async_copy(rows_ref.at[part], work.at[spot], sems.at[a]))
    for copy in copies:
        copy.start()
    for copy in copies:
        copy.wait()
    for a in range(arcs):
        live = arcs_ref[a, 0].astype(jnp.float32)
        spot = pl.ds(top + a * ARC_ROWS, ARC_ROWS)
        work[spot, :] = work[spot, :] * live
    count = pieces[0].shape[0]
    for s, piece in enumerate(pieces):
        start = pl.multiple_of((place_ref[4] ^ s) * count, 16)
        piece[...] = work[pl.ds(start, count), :]


def upper_products_kernel(place_ref, *refs):
    blocks, (keep_ref, send_ref, columns, work) = refs[:-4], refs[-4:]
    side, me = place_ref[0], place_ref[4]
    for s, block in enumerate(blocks):
        columns[me ^ s] = block[...]
    right = [right_parts(columns[c]) for c in range(P_SIZE)]
    at = 0
    for r in range(P_SIZE):
        wide = jnp.concatenate(right[r:], axis=1)
        product = parts_dot(left_parts(columns[r]), wide)
        for c in range(P_SIZE - r):
            work[at * B : (at + 1) * B, :] = product[:, c * B : (c + 1) * B]
            at += 1
    rows = HALF * B
    keep_ref[...] = work[pl.ds(pl.multiple_of(side * rows, B), rows), :]
    send_ref[...] = work[pl.ds(pl.multiple_of((1 - side) * rows, B), rows), :]


def all_products_kernel(n_left, place_ref, *refs):
    blocks, (_, keep_ref, send_ref, columns, panels, work) = refs[:-6], refs[-6:]
    left_blocks, right_blocks = blocks[:n_left], blocks[n_left:]
    side, me = place_ref[0], place_ref[4]
    for s, block in enumerate(right_blocks):
        columns[me ^ s] = block[...]
    for s, block in enumerate(left_blocks):
        panels[me ^ s] = block[...]
    left = panels if left_blocks else columns
    first = columns.shape[0] - P_SIZE
    right = jnp.concatenate([right_parts(columns[first + c]) for c in range(P_SIZE)], axis=1)
    for r in range(P_SIZE):
        product = parts_dot(left_parts(left[r]), right)
        for b in range(P_SIZE):
            work[r * P_SIZE + b] = product[:, b * B : (b + 1) * B]
    for a in range(2):
        for c in range(P_SIZE):
            block = 2 * a * P_SIZE + c
            keep_ref[a * P_SIZE + c] = work[block + side * P_SIZE]
            send_ref[a * P_SIZE + c] = work[block + (1 - side) * P_SIZE]


def tie_kernel(value_ref, after_ref, out_ref):
    del value_ref, after_ref, out_ref


def behind(value, after):
    return pl.pallas_call(
        tie_kernel,
        out_shape=jax.ShapeDtypeStruct(value.shape, value.dtype),
        in_specs=[pl.BlockSpec(memory_space=pl.ANY)] * 2,
        out_specs=pl.BlockSpec(memory_space=pl.ANY),
        input_output_aliases={0: 0},
        name="behind",
    )(value, after)


def add_kernel(left_ref, right_ref, after_ref, out_ref):
    del after_ref
    out_ref[...] = left_ref[...] + right_ref[...]


def sum_kernel(parts_ref, _, out_ref):
    total = parts_ref[0]
    for i in range(1, parts_ref.shape[0]):
        total = total + parts_ref[i]
    out_ref[...] = total


def on_chip(kernel, shapes, name, *operands, scratch=(), scalars=0, after=(), outside=()):
    done = pl.pallas_call(
        kernel,
        out_shape=[jax.ShapeDtypeStruct(shape, jnp.float32) for shape in shapes],
        in_specs=[pl.BlockSpec(memory_space=pltpu.SMEM)] * scalars
        + [pl.BlockSpec(memory_space=pltpu.VMEM)] * (len(operands) - scalars)
        + [pl.BlockSpec(memory_space=pltpu.HBM)] * len(outside)
        + [pl.BlockSpec(memory_space=pl.ANY)] * len(after),
        out_specs=[pl.BlockSpec(memory_space=pltpu.VMEM)] * len(shapes),
        scratch_shapes=list(scratch),
        compiler_params=pltpu.CompilerParams(vmem_limit_bytes=16 * 1024 * 1024),
        name=name,
    )(*operands, *outside, *after)
    return list(done)


def collect_kernel(place_ref, mine_ref, other_ref, gram_ref):
    side, high, low = place_ref[0], place_ref[1], place_ref[2]
    at = high * P_SIZE + low
    rows = mine_ref.shape[1]
    for s in range(2):
        for p in range(PIECES // 2):
            start = ((s * PIECES) // 2 + p) * rows
            end = start + rows
            while start < end:
                block, first = start // B, start % B
                count = min(end - start, B - first)
                skip = rows - (end - start)

                @pl.when(side == s)
                def _(block=block, first=first, count=count, skip=skip, p=p):
                    gram_ref[block, first : first + count] = mine_ref[p ^ at, skip : skip + count]

                @pl.when(side != s)
                def _(block=block, first=first, count=count, skip=skip, p=p):
                    gram_ref[block, first : first + count] = other_ref[p ^ at, skip : skip + count]

                start += count


def factor_step_kernel(n, gram_ref, *rest):
    if n > 1:
        row_ref, inverse_ref, next_ref, work, inv = rest
    else:
        inverse_ref, work, inv = rest
    for c in range(n):
        work[:, c * B : (c + 1) * B] = gram_ref[c]
    width = n * B

    def step(b, carry):
        start = pl.multiple_of(b * NB, NB)
        rows = [
            work[pl.ds(pl.multiple_of(start + r * SUB, SUB), SUB), pl.ds(start, NB)]
            for r in range(NB // SUB)
        ]
        right = inverse_factor(rows)
        for r in range(NB // SUB):
            inv[pl.ds(pl.multiple_of(start + r * SUB, SUB), SUB), :] = right[r]

        @pl.when(b == 0)
        def _():
            panel = dot(inv[:NB, :], work[:NB, NB:])
            work[:NB, NB:] = panel
            work[NB:, NB:] = work[NB:, NB:] - dot_t(panel[:, :NB], panel)

        return carry

    lax.fori_loop(0, B // NB, step, 0)
    first, second = inv[:NB, :], inv[NB:, :]
    inverse_ref[:NB, :NB] = first
    inverse_ref[:NB, NB:] = jnp.zeros((NB, NB), jnp.float32)
    inverse_ref[NB:, :NB] = -dot(second, dot_t(work[:NB, NB:B], first))
    inverse_ref[NB:, NB:] = second
    if n > 1:
        work[NB:, B:] = dot(second, work[NB:, B:])
        row = work[:, B:]
        row_ref[...] = row
        at = n
        for r in range(1, n):
            left = row[:, (r - 1) * B : r * B]
            for c in range(r, n):
                next_ref[at - n] = gram_ref[at] - dot_t(left, row[:, (c - 1) * B : c * B])
                at += 1


def factor(gram):
    rows, inverses = [], []
    for n in range(P_SIZE, 0, -1):
        shapes = [(B, (n - 1) * B), (B, B), (n * (n - 1) // 2, B, B)] if n > 1 else [(B, B)]
        done = on_chip(
            functools.partial(factor_step_kernel, n),
            shapes,
            "factor_step",
            gram,
            scratch=[pltpu.VMEM((B, n * B), jnp.float32), pltpu.VMEM((B, NB), jnp.float32)],
        )
        if n > 1:
            row, inverse, gram = done
            rows.append(row)
        else:
            (inverse,) = done
        inverses.append(inverse)
    return rows, inverses


def solve_kernel(place_ref, *refs):
    rows, inverses = refs[: P_SIZE - 1], refs[P_SIZE - 1 : 2 * P_SIZE - 1]
    gram_ref, own_refs, out_ref, own_ref = refs[-P_SIZE - 3], refs[-P_SIZE - 2 : -2], refs[-2], refs[-1]
    row_index, col_index = 2 * place_ref[1] + place_ref[0], place_ref[3]

    @pl.when(col_index >= P_SIZE)
    def _():
        for t in range(P_SIZE):
            own_ref[row_index ^ t] = own_refs[t][...]

    for c in range(P_SIZE):

        @pl.when(col_index == c)
        def _(c=c):
            for r in range(P_SIZE):
                own_ref[r] = gram_ref[PAIRS.index((min(r, c), c))]

    done = []
    for i in range(P_SIZE):
        block = own_ref[i]
        for k in range(i):
            off = (i - k - 1) * B
            block = block - dot_t(rows[k][:, off : off + B], done[k])
        block = dot(inverses[i][...], block)
        done.append(block)

        @pl.when(row_index == i)
        def _(block=block):
            rows_at = i * B + lax.broadcasted_iota(jnp.int32, block.shape, 0)
            cols_at = col_index * B + lax.broadcasted_iota(jnp.int32, block.shape, 1)
            out_ref[...] = jnp.where(cols_at >= rows_at, block, 0.0)


def from_first(value, n_hi):
    at = lax.axis_index("hi")
    have = 1
    while have < n_hi:
        more = min(have, n_hi - have)
        got = lax.ppermute(value, "hi", [(g, g + have) for g in range(more)])
        value = jnp.where(at < have, value, got)
        have += more
    return value


def exchange(value, high_bits, low_bits):
    bits = low_bits * 2 + high_bits
    return lax.ppermute(value, ("lo", "rh"), [(i, i ^ bits) for i in range(2 * P_SIZE)])


def swap(value, axis="rl"):
    return lax.ppermute(value, axis, [(0, 1), (1, 0)])


def across_rows(value, bits):
    return lax.ppermute(value, ("rh", "rl"), [(i, i ^ bits) for i in range(P_SIZE)])


def spread(piece):
    y, z, x = (0, 1), (0, 2), (1, 0)
    by_z, by_y, by_x = exchange(piece, *z), exchange(piece, *y), exchange(piece, *x)
    by_zy, by_yx, by_xz = exchange(by_z, *y), exchange(by_y, *x), exchange(by_x, *z)
    by_zyx = exchange(by_zy, *x)
    return jnp.stack([piece, by_y, by_z, by_zy, by_x, by_yx, by_xz, by_zyx])


def on_device(r_slab, arc_rows, arc_blocks):
    n_hi = lax.axis_size("hi")
    low = lax.axis_index("lo")
    high_row, side = lax.axis_index("rh"), lax.axis_index("rl")
    col_index = lax.axis_index("hi") * P_SIZE + low
    row_index = high_row * 2 + side
    columns = arc_rows.shape[1]
    in_two = n_hi == 2
    owners = ("hi", "lo") if in_two else ("lo",)
    shares = P_SIZE * n_hi if in_two else P_SIZE
    me = col_index if in_two else low
    place = jnp.stack([side, high_row, low, col_index, me]).astype(jnp.int32)
    total = r_slab.shape[0] + arc_rows.shape[0]
    share = (total // shares, columns)
    blocks = on_chip(
        mask_kernel,
        [share] * shares,
        "mask",
        place,
        arc_blocks,
        scalars=2,
        scratch=[
            pltpu.VMEM((total, columns), jnp.float32),
            pltpu.SemaphoreType.DMA((arc_blocks.shape[0] + 1,)),
        ],
        outside=(r_slab, arc_rows),
    )
    blocks = blocks[:1] + [
        lax.ppermute(blocks[s], owners, [(i, i ^ s) for i in range(shares)])
        for s in range(1, shares)
    ]
    panels = [] if in_two else [from_first(block, n_hi) for block in blocks]

    half = (HALF * B, B)
    gathered = pltpu.VMEM((shares, *share), jnp.float32)
    keep, send = on_chip(
        upper_products_kernel,
        [half, half],
        "upper_products",
        place,
        *blocks,
        scalars=1,
        scratch=[gathered, pltpu.VMEM((len(PAIRS) * B, B), jnp.float32)],
    )
    gram = (keep + swap(send)).reshape(PIECES // 2, -1, B)
    gram = lax.all_to_all(gram, ("rh", "lo"), 0, 0)
    half = (2 * P_SIZE, B, B)
    cross, send = on_chip(
        functools.partial(all_products_kernel, len(panels)),
        [half, half],
        "all_products",
        place,
        *panels,
        *blocks,
        scalars=1,
        scratch=[gathered, gathered, pltpu.VMEM((P_SIZE * P_SIZE, B, B), jnp.float32)],
        after=(keep,),
    )
    cross = cross + swap(send)
    (gram,) = on_chip(sum_kernel, [gram.shape[1:]], "sum_pieces", gram, after=(cross,))
    cross = lax.all_to_all(behind(cross, gram), ("rh", "lo"), 0, 0)
    piece = gram + swap(gram, "hi") if in_two else from_first(gram, n_hi)
    pieces = spread(piece)
    (gram,) = on_chip(
        collect_kernel,
        [(len(PAIRS), B, B)],
        "collect",
        place,
        pieces,
        swap(pieces),
        scalars=1,
    )
    rows, inverses = factor(gram)
    (mine,) = on_chip(sum_kernel, [(B, columns)], "sum_places", cross, after=(rows[0],))
    if in_two:
        other = swap(mine, "hi")
        (mine,) = on_chip(add_kernel, [(B, columns)], "add_groups", mine, other, after=(rows[1],))
    own = [mine] + [across_rows(mine, bits) for bits in range(1, P_SIZE)]

    (result,) = on_chip(
        solve_kernel,
        [(B, columns)],
        "solve",
        place,
        *rows,
        *inverses,
        gram,
        *own,
        scalars=1,
        scratch=[pltpu.VMEM((P_SIZE, B, columns), jnp.float32)],
    )
    return result


def solution(mesh):
    n_col, n_row = mesh.shape["col"], mesh.shape["row"]
    split = Mesh(
        mesh.devices.reshape(n_col // P_SIZE, P_SIZE, n_row // 2, 2),
        ("hi", "lo", "rh", "rl"),
    )
    spec = P(("rh", "rl"), ("hi", "lo"))
    return jax.shard_map(
        on_device,
        mesh=split,
        in_specs=(spec, spec, spec),
        out_specs=spec,
        check_vma=False,
    )
```

```python
import functools

import jax
import jax.numpy as jnp
from jax import lax
from jax.experimental import pallas as pl
from jax.experimental.pallas import tpu as pltpu
from jax.sharding import Mesh
from jax.sharding import PartitionSpec as P

B = 256
P_SIZE = 4
ARC_ROWS = 128
NB = 128
SUB = 8


def split(value):
    high = value.astype(jnp.bfloat16)
    return high, (value - high.astype(jnp.float32)).astype(jnp.bfloat16)


def left_parts(value, axis=0):
    high, low = split(value)
    return jnp.concatenate([high, high, low], axis=axis)


def right_parts(value):
    high, low = split(value)
    return jnp.concatenate([high, low, high], axis=0)


def parts_dot(left, right):
    return lax.dot_general(
        left, right, (((0,), (0,)), ((), ())), preferred_element_type=jnp.float32
    )


def dot(left, right):
    return jnp.dot(left_parts(left, 1), right_parts(right), preferred_element_type=jnp.float32)


def dot_t(left, right):
    return parts_dot(left_parts(left), right_parts(right))


def lane(value, at):
    return jnp.broadcast_to(value[:, at : at + 1], (SUB, NB))


def row(value, at):
    return jnp.broadcast_to(value[at : at + 1, :], (SUB, NB))


def inverse_factor(rows):
    n = NB // SUB
    row_id = lax.broadcasted_iota(jnp.int32, (SUB, NB), 0)
    col_id = lax.broadcasted_iota(jnp.int32, (SUB, NB), 1)
    order = range(SUB)
    ahead = [lane(rows[0], m) for m in order]
    for b in range(n):
        j = b * SUB
        pivot = {(k, m): row(ahead[m], k) for k in order for m in range(k, SUB)}
        below = [[lane(rows[r], j + k) for k in order] for r in range(b + 1, n)]
        if b + 1 < n:
            ahead = [lane(rows[b + 1], j + SUB + m) for m in order]
        scale, left = [], []
        for k in order:
            scale.append(lax.rsqrt(pivot[k, k]))
            for m in range(k + 1, SUB):
                pivot[k, m] = pivot[k, m] * scale[k]
            for m in range(k + 1, SUB):
                for q in range(m, SUB):
                    pivot[m, q] = pivot[m, q] - pivot[k, m] * pivot[k, q]
            if b + 1 < n:
                part = below[0][k]
                for m in range(k):
                    part = part - pivot[m, k] * left[m]
                part = part * scale[k]
                left.append(part)
                for m in order:
                    ahead[m] = ahead[m] - part * row(part, m)
        inside = (col_id >= j) & (col_id < j + SUB)
        head = jnp.where(inside, jnp.where(col_id - j == row_id, 1.0, 0.0), rows[b])
        top = []
        for k in order:
            part = row(head, k)
            for m in range(k):
                part = part - pivot[m, k] * top[m]
            top.append(part * scale[k])
        if b + 1 < n:
            solved = [None] * SUB
            for k in reversed(order):
                part = top[k]
                for m in range(k + 1, SUB):
                    part = part - pivot[k, m] * solved[m]
                solved[k] = part * scale[k]
            for r in range(b + 1, n):
                body = jnp.where(inside, 0.0, rows[r])
                for k in order:
                    body = body - below[r - b - 1][k] * solved[k]
                rows[r] = body
        strip = top[0]
        for k in range(1, SUB):
            strip = jnp.where(row_id == k, top[k], strip)
        rows[b] = jnp.where(col_id < j + SUB, strip, 0.0)
    return rows


PAIRS = [(r, c) for r in range(P_SIZE) for c in range(r, P_SIZE)]
CHUNKS = 2


def mask_kernel(place_ref, arcs_ref, slab_ref, rows_ref, *refs):
    chunks, work, sems = refs[:-2], refs[-2], refs[-1]
    top = slab_ref.shape[0]
    arcs = arcs_ref.shape[0]
    copies = [pltpu.make_async_copy(slab_ref, work.at[pl.ds(0, top)], sems.at[arcs])]
    for a in range(arcs):
        part = pl.ds(a * ARC_ROWS, ARC_ROWS)
        spot = pl.ds(top + a * ARC_ROWS, ARC_ROWS)
        copies.append(pltpu.make_async_copy(rows_ref.at[part], work.at[spot], sems.at[a]))
    for copy in copies:
        copy.start()
    for copy in copies:
        copy.wait()
    for a in range(arcs):
        live = arcs_ref[a, 0].astype(jnp.float32)
        spot = pl.ds(top + a * ARC_ROWS, ARC_ROWS)
        work[spot, :] = work[spot, :] * live
    count = chunks[0].shape[0]
    if len(chunks) > CHUNKS:
        first = jnp.where(place_ref[4] == 0, 0, CHUNKS * count)
    else:
        first = 0
    for s, chunk in enumerate(chunks):
        start = first + s * count if s < CHUNKS else CHUNKS * count - first + (s - CHUNKS) * count
        chunk[...] = work[pl.ds(pl.multiple_of(start, 16), count), :]


def products_kernel(place_ref, *refs):
    panels, right = refs[: P_SIZE * CHUNKS], refs[P_SIZE * CHUNKS : (P_SIZE + 1) * CHUNKS]
    keep_ref, keep_cross_ref, send_ref, work = refs[(P_SIZE + 1) * CHUNKS :]
    side, own = place_ref[0], place_ref[2]

    def whole(chunks):
        return jnp.concatenate([chunk[...] for chunk in chunks], axis=0)

    both = jnp.concatenate(
        [right_parts(whole(panels[:CHUNKS])), right_parts(whole(right))], axis=1
    )
    for t in range(P_SIZE):
        left = left_parts(whole(panels[t * CHUNKS : (t + 1) * CHUNKS]))
        product = parts_dot(left, both)
        work[0, own ^ t] = product[:, :B]
        work[1, own ^ t] = product[:, B:]
    for h in range(2):
        keep_ref[h] = work[0, 2 * h + side]
        keep_cross_ref[h] = work[1, 2 * h + side]
        for k in range(2):
            send_ref[k, h] = work[k, 2 * h + 1 - side]


def pick_kernel(k, place_ref, keep_ref, got_ref, _, own_ref, other_ref):
    high = place_ref[1]
    own_ref[...] = keep_ref[high] + got_ref[k, high]
    other_ref[...] = keep_ref[1 - high] + got_ref[k, 1 - high]


def stack_kernel(first_ref, second_ref, _, out_ref):
    out_ref[0] = first_ref[...]
    out_ref[1] = second_ref[...]


def add_kernel(left_ref, right_ref, after_ref, out_ref):
    del after_ref
    out_ref[...] = left_ref[...] + right_ref[...]


def on_chip(kernel, shapes, name, *operands, scratch=(), scalars=0, after=(), outside=()):
    done = pl.pallas_call(
        kernel,
        out_shape=[jax.ShapeDtypeStruct(shape, jnp.float32) for shape in shapes],
        in_specs=[pl.BlockSpec(memory_space=pltpu.SMEM)] * scalars
        + [pl.BlockSpec(memory_space=pltpu.VMEM)] * (len(operands) - scalars)
        + [pl.BlockSpec(memory_space=pltpu.HBM)] * len(outside)
        + [pl.BlockSpec(memory_space=pl.ANY)] * len(after),
        out_specs=[pl.BlockSpec(memory_space=pltpu.VMEM)] * len(shapes),
        scratch_shapes=list(scratch),
        compiler_params=pltpu.CompilerParams(vmem_limit_bytes=16 * 1024 * 1024),
        name=name,
    )(*operands, *outside, *after)
    return list(done)


def collect_kernel(place_ref, mine_ref, other_ref, gram_ref):
    side, at = place_ref[0], place_ref[1] * P_SIZE + place_ref[2]
    for i, (r, c) in enumerate(PAIRS):
        spot = ((r // 2) * P_SIZE + c) ^ at

        @pl.when(side == r % 2)
        def _(i=i, spot=spot):
            gram_ref[i] = mine_ref[spot]

        @pl.when(side != r % 2)
        def _(i=i, spot=spot):
            gram_ref[i] = other_ref[spot]


def factor_step_kernel(n, gram_ref, *rest):
    if n > 1:
        row_ref, inverse_ref, next_ref, work, inv = rest
    else:
        inverse_ref, work, inv = rest
    for c in range(n):
        work[:, c * B : (c + 1) * B] = gram_ref[c]
    width = n * B

    def step(b, carry):
        start = pl.multiple_of(b * NB, NB)
        rows = [
            work[pl.ds(pl.multiple_of(start + r * SUB, SUB), SUB), pl.ds(start, NB)]
            for r in range(NB // SUB)
        ]
        right = inverse_factor(rows)
        for r in range(NB // SUB):
            inv[pl.ds(pl.multiple_of(start + r * SUB, SUB), SUB), :] = right[r]

        @pl.when(b == 0)
        def _():
            panel = dot(inv[:NB, :], work[:NB, NB:])
            work[:NB, NB:] = panel
            work[NB:, NB:] = work[NB:, NB:] - dot_t(panel[:, :NB], panel)

        return carry

    lax.fori_loop(0, B // NB, step, 0)
    first, second = inv[:NB, :], inv[NB:, :]
    inverse_ref[:NB, :NB] = first
    inverse_ref[:NB, NB:] = jnp.zeros((NB, NB), jnp.float32)
    inverse_ref[NB:, :NB] = -dot(second, dot_t(work[:NB, NB:B], first))
    inverse_ref[NB:, NB:] = second
    if n > 1:
        work[NB:, B:] = dot(second, work[NB:, B:])
        row = work[:, B:]
        row_ref[...] = row
        at = n
        for r in range(1, n):
            left = row[:, (r - 1) * B : r * B]
            for c in range(r, n):
                next_ref[at - n] = gram_ref[at] - dot_t(left, row[:, (c - 1) * B : c * B])
                at += 1


def factor(gram):
    rows, inverses = [], []
    for n in range(P_SIZE, 0, -1):
        shapes = [(B, (n - 1) * B), (B, B), (n * (n - 1) // 2, B, B)] if n > 1 else [(B, B)]
        done = on_chip(
            functools.partial(factor_step_kernel, n),
            shapes,
            "factor_step",
            gram,
            scratch=[pltpu.VMEM((B, n * B), jnp.float32), pltpu.VMEM((B, NB), jnp.float32)],
        )
        if n > 1:
            row, inverse, gram = done
            rows.append(row)
        else:
            (inverse,) = done
        inverses.append(inverse)
    return rows, inverses


def solve_kernel(place_ref, *refs):
    rows, inverses = refs[: P_SIZE - 1], refs[P_SIZE - 1 : 2 * P_SIZE - 1]
    gram_ref, pair_ref, other_ref, out_ref, own_ref = refs[-5:]
    row_index, col_index = 2 * place_ref[1] + place_ref[0], place_ref[3]

    @pl.when(col_index >= P_SIZE)
    def _():
        for h in range(2):
            own_ref[row_index ^ (2 * h)] = pair_ref[h]
            own_ref[row_index ^ (2 * h + 1)] = other_ref[h]

    for c in range(P_SIZE):

        @pl.when(col_index == c)
        def _(c=c):
            for r in range(P_SIZE):
                own_ref[r] = gram_ref[PAIRS.index((min(r, c), c))]

    done = []
    for i in range(P_SIZE):
        block = own_ref[i]
        for k in range(i):
            off = (i - k - 1) * B
            block = block - dot_t(rows[k][:, off : off + B], done[k])
        block = dot(inverses[i][...], block)
        done.append(block)

        @pl.when(row_index == i)
        def _(block=block):
            rows_at = i * B + lax.broadcasted_iota(jnp.int32, block.shape, 0)
            cols_at = col_index * B + lax.broadcasted_iota(jnp.int32, block.shape, 1)
            out_ref[...] = jnp.where(cols_at >= rows_at, block, 0.0)


def from_first(value, n_hi):
    at = lax.axis_index("hi")
    have = 1
    while have < n_hi:
        more = min(have, n_hi - have)
        got = lax.ppermute(value, "hi", [(g, g + have) for g in range(more)])
        value = jnp.where(at < have, value, got)
        have += more
    return value


def exchange(value, high_bits, low_bits):
    bits = low_bits * 2 + high_bits
    return lax.ppermute(value, ("lo", "rh"), [(i, i ^ bits) for i in range(2 * P_SIZE)])


def swap(value, axis="rl"):
    return lax.ppermute(value, axis, [(0, 1), (1, 0)])


def other_group(value):
    return lax.ppermute(value, ("hi", "lo"), [(i, i ^ 6) for i in range(2 * P_SIZE)])


def spread(piece):
    y, z, x = (0, 1), (0, 2), (1, 0)
    by_z, by_y, by_x = exchange(piece, *z), exchange(piece, *y), exchange(piece, *x)
    by_zy, by_yx, by_xz = exchange(by_z, *y), exchange(by_y, *x), exchange(by_x, *z)
    by_zyx = exchange(by_zy, *x)
    return jnp.stack([piece, by_y, by_z, by_zy, by_x, by_yx, by_xz, by_zyx])


def on_device(r_slab, arc_rows, arc_blocks):
    n_hi = lax.axis_size("hi")
    group, low = lax.axis_index("hi"), lax.axis_index("lo")
    high_row, side = lax.axis_index("rh"), lax.axis_index("rl")
    col_index = group * P_SIZE + low
    columns = arc_rows.shape[1]
    in_two = n_hi == 2
    panel = low ^ (2 * group) if in_two else low
    place = jnp.stack([side, high_row, panel, col_index, group]).astype(jnp.int32)
    total = r_slab.shape[0] + arc_rows.shape[0]
    parts = 2 * CHUNKS if in_two else CHUNKS
    chunks = on_chip(
        mask_kernel,
        [(total // parts, columns)] * parts,
        "mask",
        place,
        arc_blocks,
        scalars=2,
        scratch=[
            pltpu.VMEM((total, columns), jnp.float32),
            pltpu.SemaphoreType.DMA((arc_blocks.shape[0] + 1,)),
        ],
        outside=(r_slab, arc_rows),
    )
    if in_two:
        kept, got = chunks[:CHUNKS], [other_group(chunk) for chunk in chunks[CHUNKS:]]
        first = [jnp.where(group == 0, k, g) for k, g in zip(kept, got)]
        right = [jnp.where(group == 0, g, k) for k, g in zip(kept, got)]
    else:
        first, right = [from_first(chunk, n_hi) for chunk in chunks], chunks
    y, z = (0, 1), (0, 2)
    by_y, by_z = exchange(first[0], *y), exchange(first[1], *z)
    panels = [
        first[0],
        first[1],
        by_y,
        exchange(first[1], *y),
        exchange(first[0], *z),
        by_z,
        exchange(by_y, *z),
        exchange(by_z, *y),
    ]

    pair, block = (2, B, B), (B, B)
    keep, keep_cross, send = on_chip(
        products_kernel,
        [pair, pair, (2, *pair)],
        "products",
        place,
        *panels,
        *right,
        scalars=1,
        scratch=[pltpu.VMEM((2, P_SIZE, B, B), jnp.float32)],
    )
    got = swap(send)

    def picked(k, kept, after):
        return on_chip(
            functools.partial(pick_kernel, k),
            [block, block],
            "pick",
            place,
            kept,
            got,
            scalars=1,
            after=(after,),
        )

    mine, other = picked(0, keep, send)
    piece = mine + exchange(other, 1, 0)
    if in_two:
        piece = piece + other_group(piece)
    pieces = spread(piece)
    (gram,) = on_chip(
        collect_kernel,
        [(len(PAIRS), B, B)],
        "collect",
        place,
        pieces,
        swap(pieces),
        scalars=1,
    )

    def added(left, right, after):
        (total,) = on_chip(add_kernel, [block], "add", left, right, after=(after,))
        return total

    rows, inverses = factor(gram)
    mine, other = picked(1, keep_cross, gram)
    mine = added(mine, exchange(other, 1, 0), rows[0])
    if in_two:
        mine = added(mine, other_group(mine), rows[1])
    (own,) = on_chip(stack_kernel, [pair], "stack", mine, exchange(mine, 1, 0), after=(rows[2],))
    (result,) = on_chip(
        solve_kernel,
        [(B, columns)],
        "solve",
        place,
        *rows,
        *inverses,
        gram,
        own,
        swap(own),
        scalars=1,
        scratch=[pltpu.VMEM((P_SIZE, B, columns), jnp.float32)],
    )
    return result


def solution(mesh):
    n_col, n_row = mesh.shape["col"], mesh.shape["row"]
    split = Mesh(
        mesh.devices.reshape(n_col // P_SIZE, P_SIZE, n_row // 2, 2),
        ("hi", "lo", "rh", "rl"),
    )
    spec = P(("rh", "rl"), ("hi", "lo"))
    return jax.shard_map(
        on_device,
        mesh=split,
        in_specs=(spec, spec, spec),
        out_specs=spec,
        check_vma=False,
    )
```

```python
import functools

import jax
import jax.numpy as jnp
from jax import lax
from jax.experimental import pallas as pl
from jax.experimental.pallas import tpu as pltpu
from jax.sharding import Mesh
from jax.sharding import PartitionSpec as P

B = 256
P_SIZE = 4
ARC_ROWS = 128
NB = 128
SUB = 8


def split(value):
    high = value.astype(jnp.bfloat16)
    return high, (value - high.astype(jnp.float32)).astype(jnp.bfloat16)


def left_parts(value, axis=0):
    high, low = split(value)
    return jnp.concatenate([high, high, low], axis=axis)


def right_parts(value):
    high, low = split(value)
    return jnp.concatenate([high, low, high], axis=0)


def parts_dot(left, right):
    return lax.dot_general(
        left, right, (((0,), (0,)), ((), ())), preferred_element_type=jnp.float32
    )


def dot(left, right):
    return jnp.dot(left_parts(left, 1), right_parts(right), preferred_element_type=jnp.float32)


def dot_t(left, right):
    return parts_dot(left_parts(left), right_parts(right))


def lane(value, at):
    return jnp.broadcast_to(value[:, at : at + 1], (SUB, NB))


def row(value, at):
    return jnp.broadcast_to(value[at : at + 1, :], (SUB, NB))


def inverse_factor(rows):
    n = NB // SUB
    row_id = lax.broadcasted_iota(jnp.int32, (SUB, NB), 0)
    col_id = lax.broadcasted_iota(jnp.int32, (SUB, NB), 1)
    order = range(SUB)
    ahead = [lane(rows[0], m) for m in order]
    for b in range(n):
        j = b * SUB
        pivot = {(k, m): row(ahead[m], k) for k in order for m in range(k, SUB)}
        below = [[lane(rows[r], j + k) for k in order] for r in range(b + 1, n)]
        if b + 1 < n:
            ahead = [lane(rows[b + 1], j + SUB + m) for m in order]
        scale, left = [], []
        for k in order:
            scale.append(lax.rsqrt(pivot[k, k]))
            for m in range(k + 1, SUB):
                pivot[k, m] = pivot[k, m] * scale[k]
            for m in range(k + 1, SUB):
                for q in range(m, SUB):
                    pivot[m, q] = pivot[m, q] - pivot[k, m] * pivot[k, q]
            if b + 1 < n:
                part = below[0][k]
                for m in range(k):
                    part = part - pivot[m, k] * left[m]
                part = part * scale[k]
                left.append(part)
                for m in order:
                    ahead[m] = ahead[m] - part * row(part, m)
        inside = (col_id >= j) & (col_id < j + SUB)
        head = jnp.where(inside, jnp.where(col_id - j == row_id, 1.0, 0.0), rows[b])
        top = []
        for k in order:
            part = row(head, k)
            for m in range(k):
                part = part - pivot[m, k] * top[m]
            top.append(part * scale[k])
        if b + 1 < n:
            solved = [None] * SUB
            for k in reversed(order):
                part = top[k]
                for m in range(k + 1, SUB):
                    part = part - pivot[k, m] * solved[m]
                solved[k] = part * scale[k]
            for r in range(b + 1, n):
                body = jnp.where(inside, 0.0, rows[r])
                for k in order:
                    body = body - below[r - b - 1][k] * solved[k]
                rows[r] = body
        strip = top[0]
        for k in range(1, SUB):
            strip = jnp.where(row_id == k, top[k], strip)
        rows[b] = jnp.where(col_id < j + SUB, strip, 0.0)
    return rows


PAIRS = [(r, c) for r in range(P_SIZE) for c in range(r, P_SIZE)]
PIECES = 4 * P_SIZE
CHUNKS = 2


def mask_kernel(place_ref, arcs_ref, slab_ref, rows_ref, *refs):
    chunks, quarters, work = refs[:CHUNKS], refs[CHUNKS:-1], refs[-1]
    top = slab_ref.shape[0]
    work[:top, :] = slab_ref[...]
    for a in range(arcs_ref.shape[0]):
        live = arcs_ref[a, 0].astype(jnp.float32)
        at = a * ARC_ROWS
        work[top + at : top + at + ARC_ROWS, :] = rows_ref[at : at + ARC_ROWS, :] * live
    count = chunks[0].shape[0]
    for s, chunk in enumerate(chunks):
        chunk[...] = work[s * count : (s + 1) * count, :]
    count = quarters[0].shape[0]
    for t, quarter in enumerate(quarters):
        start = pl.multiple_of((place_ref[4] ^ t) * count, 16)
        quarter[...] = work[pl.ds(start, count), :]


def upper_products_kernel(n_blocks, place_ref, *refs):
    blocks, (keep_ref, send_ref, columns, work) = refs[:n_blocks], refs[-4:]
    side, place, low = place_ref[0], place_ref[1] * P_SIZE + place_ref[4], place_ref[4]
    for t, block in enumerate(blocks):
        columns[low ^ t] = block[...]
    right = [right_parts(columns[c]) for c in range(P_SIZE)]
    at = 0
    for r in range(P_SIZE):
        wide = jnp.concatenate(right[r:], axis=1)
        product = parts_dot(left_parts(columns[r]), wide)
        for c in range(P_SIZE - r):
            work[at * B : (at + 1) * B, :] = product[:, c * B : (c + 1) * B]
            at += 1
    count = keep_ref.shape[1]
    for t in range(PIECES // 2):
        piece = place ^ t
        here = pl.multiple_of((side * (PIECES // 2) + piece) * count, SUB)
        there = pl.multiple_of(((1 - side) * (PIECES // 2) + piece) * count, SUB)
        keep_ref[t] = work[pl.ds(here, count), :]
        send_ref[t] = work[pl.ds(there, count), :]


def cross_products_kernel(place_ref, *refs):
    panel, columns = refs[:CHUNKS], refs[CHUNKS : (P_SIZE + 1) * CHUNKS]
    _, keep_ref, send_ref, work = refs[(P_SIZE + 1) * CHUNKS :]
    side, low = place_ref[0], place_ref[4]

    def whole(chunks):
        return jnp.concatenate([chunk[...] for chunk in chunks], axis=0)

    left = left_parts(whole(panel))
    for t in range(P_SIZE):
        right = right_parts(whole(columns[t * CHUNKS : (t + 1) * CHUNKS]))
        work[low ^ t] = parts_dot(left, right)
    for h in range(2):
        keep_ref[h] = work[2 * h + side]
        send_ref[h] = work[2 * h + 1 - side]


def pick_kernel(place_ref, keep_ref, got_ref, _, own_ref, other_ref):
    high = place_ref[1]
    own_ref[...] = keep_ref[high] + got_ref[high]
    other_ref[...] = keep_ref[1 - high] + got_ref[1 - high]


def pass_kernel(*refs):
    for value_ref, out_ref in zip(refs, refs[-CHUNKS:]):
        out_ref[...] = value_ref[...]


def stack_kernel(first_ref, second_ref, _, out_ref):
    out_ref[0] = first_ref[...]
    out_ref[1] = second_ref[...]


def add_kernel(left_ref, right_ref, *refs):
    out_ref = refs[-1]
    out_ref[...] = left_ref[...] + right_ref[...]


def on_chip(kernel, shapes, name, *operands, scratch=(), scalars=0, after=(), outside=()):
    done = pl.pallas_call(
        kernel,
        out_shape=[jax.ShapeDtypeStruct(shape, jnp.float32) for shape in shapes],
        in_specs=[pl.BlockSpec(memory_space=pltpu.SMEM)] * scalars
        + [pl.BlockSpec(memory_space=pltpu.VMEM)] * (len(operands) - scalars)
        + [pl.BlockSpec(memory_space=pltpu.HBM)] * len(outside)
        + [pl.BlockSpec(memory_space=pl.ANY)] * len(after),
        out_specs=[pl.BlockSpec(memory_space=pltpu.VMEM)] * len(shapes),
        scratch_shapes=list(scratch),
        compiler_params=pltpu.CompilerParams(vmem_limit_bytes=16 * 1024 * 1024),
        name=name,
    )(*operands, *outside, *after)
    return list(done)


def collect_kernel(place_ref, mine_ref, other_ref, gram_ref):
    side, high, low = place_ref[0], place_ref[1], place_ref[2]
    at = high * P_SIZE + low
    rows = mine_ref.shape[1]
    for s in range(2):
        for p in range(PIECES // 2):
            start = ((s * PIECES) // 2 + p) * rows
            end = start + rows
            while start < end:
                block, first = start // B, start % B
                count = min(end - start, B - first)
                skip = rows - (end - start)

                @pl.when(side == s)
                def _(block=block, first=first, count=count, skip=skip, p=p):
                    gram_ref[block, first : first + count] = mine_ref[p ^ at, skip : skip + count]

                @pl.when(side != s)
                def _(block=block, first=first, count=count, skip=skip, p=p):
                    gram_ref[block, first : first + count] = other_ref[p ^ at, skip : skip + count]

                start += count


def factor_step_kernel(n, gram_ref, *rest):
    if n > 1:
        row_ref, inverse_ref, next_ref, work, inv = rest
    else:
        inverse_ref, work, inv = rest
    for c in range(n):
        work[:, c * B : (c + 1) * B] = gram_ref[c]
    width = n * B

    def step(b, carry):
        start = pl.multiple_of(b * NB, NB)
        rows = [
            work[pl.ds(pl.multiple_of(start + r * SUB, SUB), SUB), pl.ds(start, NB)]
            for r in range(NB // SUB)
        ]
        right = inverse_factor(rows)
        for r in range(NB // SUB):
            inv[pl.ds(pl.multiple_of(start + r * SUB, SUB), SUB), :] = right[r]

        @pl.when(b == 0)
        def _():
            panel = dot(inv[:NB, :], work[:NB, NB:])
            work[:NB, NB:] = panel
            work[NB:, NB:] = work[NB:, NB:] - dot_t(panel[:, :NB], panel)

        return carry

    lax.fori_loop(0, B // NB, step, 0)
    first, second = inv[:NB, :], inv[NB:, :]
    inverse_ref[:NB, :NB] = first
    inverse_ref[:NB, NB:] = jnp.zeros((NB, NB), jnp.float32)
    inverse_ref[NB:, :NB] = -dot(second, dot_t(work[:NB, NB:B], first))
    inverse_ref[NB:, NB:] = second
    if n > 1:
        work[NB:, B:] = dot(second, work[NB:, B:])
        row = work[:, B:]
        row_ref[...] = row
        at = n
        for r in range(1, n):
            left = row[:, (r - 1) * B : r * B]
            for c in range(r, n):
                next_ref[at - n] = gram_ref[at] - dot_t(left, row[:, (c - 1) * B : c * B])
                at += 1


def factor(gram):
    rows, inverses = [], []
    for n in range(P_SIZE, 0, -1):
        shapes = [(B, (n - 1) * B), (B, B), (n * (n - 1) // 2, B, B)] if n > 1 else [(B, B)]
        done = on_chip(
            functools.partial(factor_step_kernel, n),
            shapes,
            "factor_step",
            gram,
            scratch=[pltpu.VMEM((B, n * B), jnp.float32), pltpu.VMEM((B, NB), jnp.float32)],
        )
        if n > 1:
            row, inverse, gram = done
            rows.append(row)
        else:
            (inverse,) = done
        inverses.append(inverse)
    return rows, inverses


def solve_kernel(place_ref, *refs):
    rows, inverses = refs[: P_SIZE - 1], refs[P_SIZE - 1 : 2 * P_SIZE - 1]
    gram_ref, pair_ref, other_ref, out_ref, own_ref = refs[-5:]
    row_index, col_index = 2 * place_ref[1] + place_ref[0], place_ref[3]

    @pl.when(col_index >= P_SIZE)
    def _():
        for h in range(2):
            own_ref[row_index ^ (2 * h)] = pair_ref[h]
            own_ref[row_index ^ (2 * h + 1)] = other_ref[h]

    for c in range(P_SIZE):

        @pl.when(col_index == c)
        def _(c=c):
            for r in range(P_SIZE):
                own_ref[r] = gram_ref[PAIRS.index((min(r, c), c))]

    done = []
    for i in range(P_SIZE):
        block = own_ref[i]
        for k in range(i):
            off = (i - k - 1) * B
            block = block - dot_t(rows[k][:, off : off + B], done[k])
        block = dot(inverses[i][...], block)
        done.append(block)

        @pl.when(row_index == i)
        def _(block=block):
            rows_at = i * B + lax.broadcasted_iota(jnp.int32, block.shape, 0)
            cols_at = col_index * B + lax.broadcasted_iota(jnp.int32, block.shape, 1)
            out_ref[...] = jnp.where(cols_at >= rows_at, block, 0.0)


def from_first(value, n_hi):
    at = lax.axis_index("hi")
    if n_hi == 2:
        got = lax.ppermute(value, ("hi", "lo"), [(i, i ^ 6) for i in range(P_SIZE)])
        return jnp.where(at == 0, value, got)
    have = 1
    while have < n_hi:
        more = min(have, n_hi - have)
        got = lax.ppermute(value, "hi", [(g, g + have) for g in range(more)])
        value = jnp.where(at < have, value, got)
        have += more
    return value


def exchange(value, high_bits, low_bits, groups):
    count, bits = 2 * P_SIZE, low_bits * 2 + high_bits
    pairs = [(g * count + i, g * count + (i ^ bits)) for g in groups for i in range(count)]
    return lax.ppermute(value, ("hi", "lo", "rh"), pairs)


def swap(value):
    return lax.ppermute(value, "rl", [(0, 1), (1, 0)])


def transposed(value, flip, groups):
    rows = P_SIZE
    pairs = []
    for g in groups:
        for low in range(P_SIZE):
            for r in range(rows):
                source = (g * P_SIZE + low) * rows + r
                pairs.append((source, (g * P_SIZE + r) * rows + (low ^ flip)))
    return lax.ppermute(value, ("hi", "lo", "rh", "rl"), pairs)


def collected(parts, groups):
    got = [parts[0]]
    for t in range(1, PIECES // 2):
        got.append(exchange(parts[t], t // P_SIZE, t % P_SIZE, groups))
    return functools.reduce(jnp.add, got)


def spread(piece, groups):
    def go(value, bits):
        return exchange(value, *bits, groups)

    y, z, x = (0, 1), (0, 2), (1, 0)
    by_z, by_y, by_x = go(piece, z), go(piece, y), go(piece, x)
    by_zy, by_yx, by_xz = go(by_z, y), go(by_y, x), go(by_x, z)
    by_zyx = go(by_zy, x)
    return jnp.stack([piece, by_y, by_z, by_zy, by_x, by_yx, by_xz, by_zyx])


def on_device(r_slab, arc_rows, arc_blocks):
    n_hi = lax.axis_size("hi")
    group, low = lax.axis_index("hi"), lax.axis_index("lo")
    high_row, side = lax.axis_index("rh"), lax.axis_index("rl")
    col_index = group * P_SIZE + low
    columns = arc_rows.shape[1]
    flip = 2 if n_hi == 2 else 0
    panel = jnp.where(group == 0, low, low ^ flip)
    place = jnp.stack([side, high_row, panel, col_index, low]).astype(jnp.int32)
    first, others, every = range(1), range(1, n_hi), range(n_hi)
    total = r_slab.shape[0] + arc_rows.shape[0]
    share = (total // P_SIZE, columns)
    pieces = on_chip(
        mask_kernel,
        [(total // CHUNKS, columns)] * CHUNKS + [share] * P_SIZE,
        "mask",
        place,
        arc_blocks,
        r_slab,
        arc_rows,
        scalars=2,
        scratch=[pltpu.VMEM((total, columns), jnp.float32)],
    )
    chunks, quarters = pieces[:CHUNKS], pieces[CHUNKS:]
    blocks = [quarters[0]] + [exchange(quarters[t], 0, t, first) for t in range(1, P_SIZE)]

    panels = [from_first(chunk, n_hi) for chunk in chunks]
    chunks = on_chip(
        pass_kernel, [chunk.shape for chunk in chunks], "chunks", *chunks, after=blocks[1:]
    )
    y, z = (0, 1), (0, 2)
    by_y, by_z = exchange(chunks[0], *y, others), exchange(chunks[1], *z, others)
    group_columns = [
        chunks[0],
        chunks[1],
        by_y,
        exchange(chunks[1], *y, others),
        exchange(chunks[0], *z, others),
        by_z,
        exchange(by_y, *z, others),
        exchange(by_z, *y, others),
    ]

    half = (PIECES // 2, len(PAIRS) * B // PIECES, B)
    keep, send = on_chip(
        functools.partial(upper_products_kernel, P_SIZE),
        [half, half],
        "upper_products",
        place,
        *blocks,
        scalars=1,
        after=group_columns[2:] + panels,
        scratch=[
            pltpu.VMEM((P_SIZE, *share), jnp.float32),
            pltpu.VMEM((len(PAIRS) * B, B), jnp.float32),
        ],
    )
    (summed,) = on_chip(add_kernel, [half], "add_pair", keep, swap(send))
    piece = from_first(collected(summed, first), n_hi)
    pair, block = (2, B, B), (B, B)
    keep_cross, send = on_chip(
        cross_products_kernel,
        [pair, pair],
        "cross_products",
        place,
        *panels,
        *group_columns,
        scalars=1,
        scratch=[pltpu.VMEM((P_SIZE, B, B), jnp.float32)],
        after=(piece,),
    )
    got_cross = swap(send)
    pieces = spread(piece, every)
    (gram,) = on_chip(
        collect_kernel,
        [(len(PAIRS), B, B)],
        "collect",
        place,
        pieces,
        swap(pieces),
        scalars=1,
    )

    def added(left, right, after):
        (total,) = on_chip(add_kernel, [block], "add", left, right, after=(after,))
        return total

    rows, inverses = factor(gram)
    mine, other = on_chip(
        pick_kernel,
        [block, block],
        "pick",
        place,
        keep_cross,
        got_cross,
        scalars=1,
        after=(gram,),
    )
    mine = added(mine, exchange(other, 1, 0, others), rows[0])
    mine = transposed(mine, flip, others)
    mine, _ = on_chip(pass_kernel, [block, block], "row_block", mine, mine, after=(rows[1],))
    by_x = exchange(mine, 1, 0, others)
    (own,) = on_chip(stack_kernel, [pair], "stack", mine, by_x, after=(rows[2],))
    (result,) = on_chip(
        solve_kernel,
        [(B, columns)],
        "solve",
        place,
        *rows,
        *inverses,
        gram,
        own,
        swap(own),
        scalars=1,
        scratch=[pltpu.VMEM((P_SIZE, B, columns), jnp.float32)],
    )
    return result


def solution(mesh):
    n_col, n_row = mesh.shape["col"], mesh.shape["row"]
    split = Mesh(
        mesh.devices.reshape(n_col // P_SIZE, P_SIZE, n_row // 2, 2),
        ("hi", "lo", "rh", "rl"),
    )
    spec = P(("rh", "rl"), ("hi", "lo"))
    return jax.shard_map(
        on_device,
        mesh=split,
        in_specs=(spec, spec, spec),
        out_specs=spec,
        check_vma=False,
    )
```

```python
import functools

import jax
import jax.numpy as jnp
from jax import lax
from jax.experimental import pallas as pl
from jax.experimental.pallas import tpu as pltpu
from jax.sharding import Mesh
from jax.sharding import PartitionSpec as P

B = 256
P_SIZE = 4
ARC_ROWS = 128
NB = 128
SUB = 8


def split(value):
    high = value.astype(jnp.bfloat16)
    return high, (value - high.astype(jnp.float32)).astype(jnp.bfloat16)


def left_parts(value, axis=0):
    high, low = split(value)
    return jnp.concatenate([high, high, low], axis=axis)


def right_parts(value):
    high, low = split(value)
    return jnp.concatenate([high, low, high], axis=0)


def parts_dot(left, right):
    return lax.dot_general(
        left, right, (((0,), (0,)), ((), ())), preferred_element_type=jnp.float32
    )


def dot(left, right):
    return jnp.dot(left_parts(left, 1), right_parts(right), preferred_element_type=jnp.float32)


def dot_t(left, right):
    return parts_dot(left_parts(left), right_parts(right))


def lane(value, at):
    return jnp.broadcast_to(value[:, at : at + 1], (SUB, NB))


def row(value, at):
    return jnp.broadcast_to(value[at : at + 1, :], (SUB, NB))


def inverse_factor(rows):
    n = NB // SUB
    row_id = lax.broadcasted_iota(jnp.int32, (SUB, NB), 0)
    col_id = lax.broadcasted_iota(jnp.int32, (SUB, NB), 1)
    order = range(SUB)
    ahead = [lane(rows[0], m) for m in order]
    for b in range(n):
        j = b * SUB
        pivot = {(k, m): row(ahead[m], k) for k in order for m in range(k, SUB)}
        below = [[lane(rows[r], j + k) for k in order] for r in range(b + 1, n)]
        if b + 1 < n:
            ahead = [lane(rows[b + 1], j + SUB + m) for m in order]
        scale, left = [], []
        for k in order:
            scale.append(lax.rsqrt(pivot[k, k]))
            for m in range(k + 1, SUB):
                pivot[k, m] = pivot[k, m] * scale[k]
            for m in range(k + 1, SUB):
                for q in range(m, SUB):
                    pivot[m, q] = pivot[m, q] - pivot[k, m] * pivot[k, q]
            if b + 1 < n:
                part = below[0][k]
                for m in range(k):
                    part = part - pivot[m, k] * left[m]
                part = part * scale[k]
                left.append(part)
                for m in order:
                    ahead[m] = ahead[m] - part * row(part, m)
        inside = (col_id >= j) & (col_id < j + SUB)
        head = jnp.where(inside, jnp.where(col_id - j == row_id, 1.0, 0.0), rows[b])
        top = []
        for k in order:
            part = row(head, k)
            for m in range(k):
                part = part - pivot[m, k] * top[m]
            top.append(part * scale[k])
        if b + 1 < n:
            solved = [None] * SUB
            for k in reversed(order):
                part = top[k]
                for m in range(k + 1, SUB):
                    part = part - pivot[k, m] * solved[m]
                solved[k] = part * scale[k]
            for r in range(b + 1, n):
                body = jnp.where(inside, 0.0, rows[r])
                for k in order:
                    body = body - below[r - b - 1][k] * solved[k]
                rows[r] = body
        strip = top[0]
        for k in range(1, SUB):
            strip = jnp.where(row_id == k, top[k], strip)
        rows[b] = jnp.where(col_id < j + SUB, strip, 0.0)
    return rows


PAIRS = [(r, c) for r in range(P_SIZE) for c in range(r, P_SIZE)]
CHUNKS = 2


def mask_kernel(place_ref, arcs_ref, slab_ref, rows_ref, *refs):
    chunks, work = refs[:-1], refs[-1]
    top = slab_ref.shape[0]
    work[:top, :] = slab_ref[...]
    for a in range(arcs_ref.shape[0]):
        live = arcs_ref[a, 0].astype(jnp.float32)
        at = a * ARC_ROWS
        work[top + at : top + at + ARC_ROWS, :] = rows_ref[at : at + ARC_ROWS, :] * live
    count = chunks[0].shape[0]
    if len(chunks) > CHUNKS:
        first = jnp.where(place_ref[4] == 0, 0, CHUNKS * count)
    else:
        first = 0
    for s, chunk in enumerate(chunks):
        start = first + s * count if s < CHUNKS else CHUNKS * count - first + (s - CHUNKS) * count
        chunk[...] = work[pl.ds(pl.multiple_of(start, 16), count), :]


def select_kernel(place_ref, kept_ref, got_ref, *refs):
    panel_ref, right_ref = refs[-2:]

    @pl.when(place_ref[4] == 0)
    def _():
        panel_ref[...] = kept_ref[...]
        right_ref[...] = got_ref[...]

    @pl.when(place_ref[4] != 0)
    def _():
        panel_ref[...] = got_ref[...]
        right_ref[...] = kept_ref[...]


def products_kernel(place_ref, *refs):
    panels, right = refs[: P_SIZE * CHUNKS], refs[P_SIZE * CHUNKS : (P_SIZE + 1) * CHUNKS]
    keep_ref, keep_cross_ref, send_ref, upper, cross = refs[(P_SIZE + 1) * CHUNKS :]
    side, own = place_ref[0], place_ref[2]

    def whole(chunks):
        return jnp.concatenate([chunk[...] for chunk in chunks], axis=0)

    both = jnp.concatenate(
        [right_parts(whole(panels[:CHUNKS])), right_parts(whole(right))], axis=1
    )
    for t in range(P_SIZE):
        left = left_parts(whole(panels[t * CHUNKS : (t + 1) * CHUNKS]))
        product = parts_dot(left, both)
        cross[own ^ t] = product[:, B:]
        if t == 0:
            upper[:B, :] = product[:, :B]
            continue
        at = B + (t - 1) * B // 2

        @pl.when(own < (own ^ t))
        def _(at=at, product=product):
            upper[at : at + B // 2, :] = product[:, : B // 2].T

        @pl.when(own > (own ^ t))
        def _(at=at, product=product):
            upper[at : at + B // 2, :] = product[B // 2 :, :B]

    count = keep_ref.shape[1]
    for h in range(2):
        here, there = 2 * h + side, 2 * h + 1 - side
        keep_ref[h] = upper[pl.ds(pl.multiple_of(here * count, SUB), count), :]
        keep_cross_ref[h] = cross[here]
        send_ref[h, :count] = upper[pl.ds(pl.multiple_of(there * count, SUB), count), :]
        send_ref[h, count:] = cross[there]


def pick_kernel(first, place_ref, keep_ref, got_ref, _, own_ref, other_ref):
    high = place_ref[1]
    rows = pl.ds(first, own_ref.shape[0])
    own_ref[...] = keep_ref[high] + got_ref[high, rows]
    other_ref[...] = keep_ref[1 - high] + got_ref[1 - high, rows]


def stack_kernel(first_ref, second_ref, _, out_ref):
    out_ref[0] = first_ref[...]
    out_ref[1] = second_ref[...]


def add_kernel(left_ref, right_ref, after_ref, out_ref):
    del after_ref
    out_ref[...] = left_ref[...] + right_ref[...]


def on_chip(kernel, shapes, name, *operands, scratch=(), scalars=0, after=(), outside=()):
    done = pl.pallas_call(
        kernel,
        out_shape=[jax.ShapeDtypeStruct(shape, jnp.float32) for shape in shapes],
        in_specs=[pl.BlockSpec(memory_space=pltpu.SMEM)] * scalars
        + [pl.BlockSpec(memory_space=pltpu.VMEM)] * (len(operands) - scalars)
        + [pl.BlockSpec(memory_space=pltpu.HBM)] * len(outside)
        + [pl.BlockSpec(memory_space=pl.ANY)] * len(after),
        out_specs=[pl.BlockSpec(memory_space=pltpu.VMEM)] * len(shapes),
        scratch_shapes=list(scratch),
        compiler_params=pltpu.CompilerParams(vmem_limit_bytes=16 * 1024 * 1024),
        name=name,
    )(*operands, *outside, *after)
    return list(done)


def collect_kernel(place_ref, mine_ref, other_ref, gram_ref):
    side, at = place_ref[0], place_ref[1] * P_SIZE + place_ref[2]
    count = mine_ref.shape[1]
    for q in range(P_SIZE):
        runs = [(q, q, 0, B)]
        for t in range(1, P_SIZE):
            j = q ^ t
            runs.append((min(q, j), max(q, j), 0 if q < j else B // 2, B // 2))
        done = 0
        for r, c, first, size in runs:
            block, start, end = PAIRS.index((r, c)), done, done + size
            while start < end:
                piece, skip = start // count, start % count
                rows = min(end - start, count - skip)
                spot = ((piece // 2) * P_SIZE + q) ^ at
                into = slice(first + start - done, first + start - done + rows)

                @pl.when(side == piece % 2)
                def _(block=block, into=into, spot=spot, skip=skip, rows=rows):
                    gram_ref[block, into] = mine_ref[spot, skip : skip + rows]

                @pl.when(side != piece % 2)
                def _(block=block, into=into, spot=spot, skip=skip, rows=rows):
                    gram_ref[block, into] = other_ref[spot, skip : skip + rows]

                start += rows
            done = end


def factor_step_kernel(n, gram_ref, *rest):
    if n > 1:
        row_ref, inverse_ref, next_ref, work, inv = rest
    else:
        inverse_ref, work, inv = rest
    for c in range(n):
        work[:, c * B : (c + 1) * B] = gram_ref[c]
    width = n * B

    def step(b, carry):
        start = pl.multiple_of(b * NB, NB)
        rows = [
            work[pl.ds(pl.multiple_of(start + r * SUB, SUB), SUB), pl.ds(start, NB)]
            for r in range(NB // SUB)
        ]
        right = inverse_factor(rows)
        for r in range(NB // SUB):
            inv[pl.ds(pl.multiple_of(start + r * SUB, SUB), SUB), :] = right[r]

        @pl.when(b == 0)
        def _():
            panel = dot(inv[:NB, :], work[:NB, NB:])
            work[:NB, NB:] = panel
            work[NB:, NB:] = work[NB:, NB:] - dot_t(panel[:, :NB], panel)

        return carry

    lax.fori_loop(0, B // NB, step, 0)
    first, second = inv[:NB, :], inv[NB:, :]
    inverse_ref[:NB, :NB] = first
    inverse_ref[:NB, NB:] = jnp.zeros((NB, NB), jnp.float32)
    inverse_ref[NB:, :NB] = -dot(second, dot_t(work[:NB, NB:B], first))
    inverse_ref[NB:, NB:] = second
    if n > 1:
        work[NB:, B:] = dot(second, work[NB:, B:])
        row = work[:, B:]
        row_ref[...] = row
        at = n
        for r in range(1, n):
            left = row[:, (r - 1) * B : r * B]
            for c in range(r, n):
                next_ref[at - n] = gram_ref[at] - dot_t(left, row[:, (c - 1) * B : c * B])
                at += 1


def factor(gram):
    rows, inverses = [], []
    for n in range(P_SIZE, 0, -1):
        shapes = [(B, (n - 1) * B), (B, B), (n * (n - 1) // 2, B, B)] if n > 1 else [(B, B)]
        done = on_chip(
            functools.partial(factor_step_kernel, n),
            shapes,
            "factor_step",
            gram,
            scratch=[pltpu.VMEM((B, n * B), jnp.float32), pltpu.VMEM((B, NB), jnp.float32)],
        )
        if n > 1:
            row, inverse, gram = done
            rows.append(row)
        else:
            (inverse,) = done
        inverses.append(inverse)
    return rows, inverses


def solve_kernel(place_ref, *refs):
    rows, inverses = refs[: P_SIZE - 1], refs[P_SIZE - 1 : 2 * P_SIZE - 1]
    gram_ref, pair_ref, other_ref, out_ref, own_ref = refs[-5:]
    row_index, col_index = 2 * place_ref[1] + place_ref[0], place_ref[3]

    @pl.when(col_index >= P_SIZE)
    def _():
        for h in range(2):
            own_ref[row_index ^ (2 * h)] = pair_ref[h]
            own_ref[row_index ^ (2 * h + 1)] = other_ref[h]

    for c in range(P_SIZE):

        @pl.when(col_index == c)
        def _(c=c):
            for r in range(P_SIZE):
                own_ref[r] = gram_ref[PAIRS.index((min(r, c), c))]

    done = []
    for i in range(P_SIZE):
        block = own_ref[i]
        for k in range(i):
            off = (i - k - 1) * B
            block = block - dot_t(rows[k][:, off : off + B], done[k])
        block = dot(inverses[i][...], block)
        done.append(block)

        @pl.when(row_index == i)
        def _(block=block):
            rows_at = i * B + lax.broadcasted_iota(jnp.int32, block.shape, 0)
            cols_at = col_index * B + lax.broadcasted_iota(jnp.int32, block.shape, 1)
            out_ref[...] = jnp.where(cols_at >= rows_at, block, 0.0)


def from_first(value, n_hi):
    at = lax.axis_index("hi")
    have = 1
    while have < n_hi:
        more = min(have, n_hi - have)
        got = lax.ppermute(value, "hi", [(g, g + have) for g in range(more)])
        value = jnp.where(at < have, value, got)
        have += more
    return value


def exchange(value, high_bits, low_bits):
    bits = low_bits * 2 + high_bits
    return lax.ppermute(value, ("lo", "rh"), [(i, i ^ bits) for i in range(2 * P_SIZE)])


def swap(value, axis="rl"):
    return lax.ppermute(value, axis, [(0, 1), (1, 0)])


def other_group(value):
    return lax.ppermute(value, ("hi", "lo"), [(i, i ^ 6) for i in range(2 * P_SIZE)])


def spread(piece):
    y, z, x = (0, 1), (0, 2), (1, 0)
    by_z, by_y, by_x = exchange(piece, *z), exchange(piece, *y), exchange(piece, *x)
    by_zy, by_yx, by_xz = exchange(by_z, *y), exchange(by_y, *x), exchange(by_x, *z)
    by_zyx = exchange(by_zy, *x)
    return jnp.stack([piece, by_y, by_z, by_zy, by_x, by_yx, by_xz, by_zyx])


def on_device(r_slab, arc_rows, arc_blocks):
    n_hi = lax.axis_size("hi")
    group, low = lax.axis_index("hi"), lax.axis_index("lo")
    high_row, side = lax.axis_index("rh"), lax.axis_index("rl")
    col_index = group * P_SIZE + low
    columns = arc_rows.shape[1]
    in_two = n_hi == 2
    panel = low ^ (2 * group) if in_two else low
    place = jnp.stack([side, high_row, panel, col_index, group]).astype(jnp.int32)
    total = r_slab.shape[0] + arc_rows.shape[0]
    parts = 2 * CHUNKS if in_two else CHUNKS
    chunks = on_chip(
        mask_kernel,
        [(total // parts, columns)] * parts,
        "mask",
        place,
        arc_blocks,
        r_slab,
        arc_rows,
        scalars=2,
        scratch=[pltpu.VMEM((total, columns), jnp.float32)],
    )
    y, z = (0, 1), (0, 2)

    def halves(k, after):
        if not in_two:
            return from_first(chunks[k], n_hi), chunks[k]
        shape = chunks[k].shape
        return on_chip(
            select_kernel,
            [shape, shape],
            "select",
            place,
            chunks[k],
            other_group(chunks[CHUNKS + k]),
            scalars=1,
            after=after,
        )

    first, first_right = halves(0, ())
    first_y, first_z = exchange(first, *y), exchange(first, *z)
    first_zy = exchange(first_y, *z)
    second, second_right = halves(1, (first_z, first_zy))
    second_y, second_z = exchange(second, *y), exchange(second, *z)
    second_zy = exchange(second_z, *y)
    panels = [first, second, first_y, second_y, first_z, second_z, first_zy, second_zy]
    right = [first_right, second_right]

    pair, block = (2, B, B), (B, B)
    count = len(PAIRS) * B // P_SIZE // P_SIZE
    keep, keep_cross, send = on_chip(
        products_kernel,
        [(2, count, B), pair, (2, count + B, B)],
        "products",
        place,
        *panels,
        *right,
        scalars=1,
        scratch=[
            pltpu.VMEM((P_SIZE * count, B), jnp.float32),
            pltpu.VMEM((P_SIZE, B, B), jnp.float32),
        ],
    )
    got = swap(send)

    def picked(first, kept, after):
        return on_chip(
            functools.partial(pick_kernel, first),
            [kept.shape[1:]] * 2,
            "pick",
            place,
            kept,
            got,
            scalars=1,
            after=(after,),
        )

    mine, other = picked(0, keep, send)
    piece = mine + exchange(other, 1, 0)
    if in_two:
        piece = piece + other_group(piece)
    pieces = spread(piece)
    (gram,) = on_chip(
        collect_kernel,
        [(len(PAIRS), B, B)],
        "collect",
        place,
        pieces,
        swap(pieces),
        scalars=1,
    )

    def added(left, right, after):
        (total,) = on_chip(add_kernel, [block], "add", left, right, after=(after,))
        return total

    rows, inverses = factor(gram)
    mine, other = picked(count, keep_cross, gram)
    mine = added(mine, exchange(other, 1, 0), rows[0])
    if in_two:
        mine = added(mine, other_group(mine), rows[1])
    (own,) = on_chip(stack_kernel, [pair], "stack", mine, exchange(mine, 1, 0), after=(rows[2],))
    (result,) = on_chip(
        solve_kernel,
        [(B, columns)],
        "solve",
        place,
        *rows,
        *inverses,
        gram,
        own,
        swap(own),
        scalars=1,
        scratch=[pltpu.VMEM((P_SIZE, B, columns), jnp.float32)],
    )
    return result


def solution(mesh):
    n_col, n_row = mesh.shape["col"], mesh.shape["row"]
    split = Mesh(
        mesh.devices.reshape(n_col // P_SIZE, P_SIZE, n_row // 2, 2),
        ("hi", "lo", "rh", "rl"),
    )
    spec = P(("rh", "rl"), ("hi", "lo"))
    return jax.shard_map(
        on_device,
        mesh=split,
        in_specs=(spec, spec, spec),
        out_specs=spec,
        check_vma=False,
    )
```

```python
import functools

import jax
import jax.numpy as jnp
from jax import lax
from jax.experimental import pallas as pl
from jax.experimental.pallas import tpu as pltpu
from jax.sharding import Mesh
from jax.sharding import PartitionSpec as P

B = 256
P_SIZE = 4
ARC_ROWS = 128
NB = 128
SUB = 8


def split(value):
    high = value.astype(jnp.bfloat16)
    return high, (value - high.astype(jnp.float32)).astype(jnp.bfloat16)


def left_parts(value, axis=0):
    high, low = split(value)
    return jnp.concatenate([high, high, low], axis=axis)


def right_parts(value):
    high, low = split(value)
    return jnp.concatenate([high, low, high], axis=0)


def parts_dot(left, right):
    return lax.dot_general(
        left, right, (((0,), (0,)), ((), ())), preferred_element_type=jnp.float32
    )


def dot(left, right):
    return jnp.dot(left_parts(left, 1), right_parts(right), preferred_element_type=jnp.float32)


def dot_t(left, right):
    return parts_dot(left_parts(left), right_parts(right))


def lane(value, at):
    return jnp.broadcast_to(value[:, at : at + 1], (SUB, NB))


def row(value, at):
    return jnp.broadcast_to(value[at : at + 1, :], (SUB, NB))


def inverse_factor(rows):
    n = NB // SUB
    row_id = lax.broadcasted_iota(jnp.int32, (SUB, NB), 0)
    col_id = lax.broadcasted_iota(jnp.int32, (SUB, NB), 1)
    order = range(SUB)
    ahead = [lane(rows[0], m) for m in order]
    for b in range(n):
        j = b * SUB
        pivot = {(k, m): row(ahead[m], k) for k in order for m in range(k, SUB)}
        below = [[lane(rows[r], j + k) for k in order] for r in range(b + 1, n)]
        if b + 1 < n:
            ahead = [lane(rows[b + 1], j + SUB + m) for m in order]
        scale, left = [], []
        for k in order:
            scale.append(lax.rsqrt(pivot[k, k]))
            for m in range(k + 1, SUB):
                pivot[k, m] = pivot[k, m] * scale[k]
            for m in range(k + 1, SUB):
                for q in range(m, SUB):
                    pivot[m, q] = pivot[m, q] - pivot[k, m] * pivot[k, q]
            if b + 1 < n:
                part = below[0][k]
                for m in range(k):
                    part = part - pivot[m, k] * left[m]
                part = part * scale[k]
                left.append(part)
                for m in order:
                    ahead[m] = ahead[m] - part * row(part, m)
        inside = (col_id >= j) & (col_id < j + SUB)
        head = jnp.where(inside, jnp.where(col_id - j == row_id, 1.0, 0.0), rows[b])
        top = []
        for k in order:
            part = row(head, k)
            for m in range(k):
                part = part - pivot[m, k] * top[m]
            top.append(part * scale[k])
        if b + 1 < n:
            solved = [None] * SUB
            for k in reversed(order):
                part = top[k]
                for m in range(k + 1, SUB):
                    part = part - pivot[k, m] * solved[m]
                solved[k] = part * scale[k]
            for r in range(b + 1, n):
                body = jnp.where(inside, 0.0, rows[r])
                for k in order:
                    body = body - below[r - b - 1][k] * solved[k]
                rows[r] = body
        strip = top[0]
        for k in range(1, SUB):
            strip = jnp.where(row_id == k, top[k], strip)
        rows[b] = jnp.where(col_id < j + SUB, strip, 0.0)
    return rows


PAIRS = [(r, c) for r in range(P_SIZE) for c in range(r, P_SIZE)]
CHUNKS = 2


def mask_kernel(place_ref, arcs_ref, slab_ref, rows_ref, *refs):
    chunks, work = refs[:-1], refs[-1]
    top = slab_ref.shape[0]
    work[:top, :] = slab_ref[...]
    for a in range(arcs_ref.shape[0]):
        live = arcs_ref[a, 0].astype(jnp.float32)
        at = a * ARC_ROWS
        work[top + at : top + at + ARC_ROWS, :] = rows_ref[at : at + ARC_ROWS, :] * live
    count = chunks[0].shape[0]
    if len(chunks) > CHUNKS:
        first = jnp.where(place_ref[4] == 0, 0, CHUNKS * count)
    else:
        first = 0
    for s, chunk in enumerate(chunks):
        start = first + s * count if s < CHUNKS else CHUNKS * count - first + (s - CHUNKS) * count
        chunk[...] = work[pl.ds(pl.multiple_of(start, 16), count), :]


def select_kernel(place_ref, kept_ref, got_ref, *refs):
    panel_ref, right_ref = refs[-2:]

    @pl.when(place_ref[4] == 0)
    def _():
        panel_ref[...] = kept_ref[...]
        right_ref[...] = got_ref[...]

    @pl.when(place_ref[4] != 0)
    def _():
        panel_ref[...] = got_ref[...]
        right_ref[...] = kept_ref[...]


def products_kernel(place_ref, *refs):
    panels, right = refs[: P_SIZE * CHUNKS], refs[P_SIZE * CHUNKS : (P_SIZE + 1) * CHUNKS]
    keep_ref, keep_cross_ref, send_ref, upper, cross = refs[(P_SIZE + 1) * CHUNKS :]
    side, own = place_ref[0], place_ref[2]

    def whole(chunks):
        return jnp.concatenate([chunk[...] for chunk in chunks], axis=0)

    both = jnp.concatenate(
        [right_parts(whole(panels[:CHUNKS])), right_parts(whole(right))], axis=1
    )
    for t in range(P_SIZE):
        left = left_parts(whole(panels[t * CHUNKS : (t + 1) * CHUNKS]))
        product = parts_dot(left, both)
        cross[own ^ t] = product[:, B:]
        if t == 0:
            upper[:B, :] = product[:, :B]
            continue
        at = B + (t - 1) * B // 2

        @pl.when(own < (own ^ t))
        def _(at=at, product=product):
            upper[at : at + B // 2, :] = product[:, : B // 2].T

        @pl.when(own > (own ^ t))
        def _(at=at, product=product):
            upper[at : at + B // 2, :] = product[B // 2 :, :B]

    count = keep_ref.shape[1]
    for h in range(2):
        here, there = 2 * h + side, 2 * h + 1 - side
        keep_ref[h] = upper[pl.ds(pl.multiple_of(here * count, SUB), count), :]
        keep_cross_ref[h] = cross[here]
        send_ref[h, :count] = upper[pl.ds(pl.multiple_of(there * count, SUB), count), :]
        send_ref[h, count:] = cross[there]


def pick_kernel(first, place_ref, keep_ref, got_ref, _, own_ref, other_ref):
    high = place_ref[1]
    rows = pl.ds(first, own_ref.shape[0])
    own_ref[...] = keep_ref[high] + got_ref[high, rows]
    other_ref[...] = keep_ref[1 - high] + got_ref[1 - high, rows]


def pass_kernel(value_ref, _, out_ref):
    out_ref[...] = value_ref[...]


def stack_kernel(first_ref, second_ref, _, out_ref):
    out_ref[0] = first_ref[...]
    out_ref[1] = second_ref[...]


def add_kernel(left_ref, right_ref, after_ref, out_ref):
    del after_ref
    out_ref[...] = left_ref[...] + right_ref[...]


def on_chip(kernel, shapes, name, *operands, scratch=(), scalars=0, after=(), outside=()):
    done = pl.pallas_call(
        kernel,
        out_shape=[jax.ShapeDtypeStruct(shape, jnp.float32) for shape in shapes],
        in_specs=[pl.BlockSpec(memory_space=pltpu.SMEM)] * scalars
        + [pl.BlockSpec(memory_space=pltpu.VMEM)] * (len(operands) - scalars)
        + [pl.BlockSpec(memory_space=pltpu.HBM)] * len(outside)
        + [pl.BlockSpec(memory_space=pl.ANY)] * len(after),
        out_specs=[pl.BlockSpec(memory_space=pltpu.VMEM)] * len(shapes),
        scratch_shapes=list(scratch),
        compiler_params=pltpu.CompilerParams(vmem_limit_bytes=16 * 1024 * 1024),
        name=name,
    )(*operands, *outside, *after)
    return list(done)


def collect_kernel(place_ref, mine_ref, other_ref, gram_ref):
    side, at = place_ref[0], place_ref[1] * P_SIZE + place_ref[2]
    count = mine_ref.shape[1]
    for q in range(P_SIZE):
        runs = [(q, q, 0, B)]
        for t in range(1, P_SIZE):
            j = q ^ t
            runs.append((min(q, j), max(q, j), 0 if q < j else B // 2, B // 2))
        done = 0
        for r, c, first, size in runs:
            block, start, end = PAIRS.index((r, c)), done, done + size
            while start < end:
                piece, skip = start // count, start % count
                rows = min(end - start, count - skip)
                spot = ((piece // 2) * P_SIZE + q) ^ at
                into = slice(first + start - done, first + start - done + rows)

                @pl.when(side == piece % 2)
                def _(block=block, into=into, spot=spot, skip=skip, rows=rows):
                    gram_ref[block, into] = mine_ref[spot, skip : skip + rows]

                @pl.when(side != piece % 2)
                def _(block=block, into=into, spot=spot, skip=skip, rows=rows):
                    gram_ref[block, into] = other_ref[spot, skip : skip + rows]

                start += rows
            done = end


def factor_step_kernel(n, gram_ref, *rest):
    if n > 1:
        row_ref, inverse_ref, next_ref, work, inv = rest
    else:
        inverse_ref, work, inv = rest
    for c in range(n):
        work[:, c * B : (c + 1) * B] = gram_ref[c]
    width = n * B

    def step(b, carry):
        start = pl.multiple_of(b * NB, NB)
        rows = [
            work[pl.ds(pl.multiple_of(start + r * SUB, SUB), SUB), pl.ds(start, NB)]
            for r in range(NB // SUB)
        ]
        right = inverse_factor(rows)
        for r in range(NB // SUB):
            inv[pl.ds(pl.multiple_of(start + r * SUB, SUB), SUB), :] = right[r]

        @pl.when(b == 0)
        def _():
            panel = dot(inv[:NB, :], work[:NB, NB:])
            work[:NB, NB:] = panel
            work[NB:, NB:] = work[NB:, NB:] - dot_t(panel[:, :NB], panel)

        return carry

    lax.fori_loop(0, B // NB, step, 0)
    first, second = inv[:NB, :], inv[NB:, :]
    inverse_ref[:NB, :NB] = first
    inverse_ref[:NB, NB:] = jnp.zeros((NB, NB), jnp.float32)
    inverse_ref[NB:, :NB] = -dot(second, dot_t(work[:NB, NB:B], first))
    inverse_ref[NB:, NB:] = second
    if n > 1:
        work[NB:, B:] = dot(second, work[NB:, B:])
        row = work[:, B:]
        row_ref[...] = row
        at = n
        for r in range(1, n):
            left = row[:, (r - 1) * B : r * B]
            for c in range(r, n):
                next_ref[at - n] = gram_ref[at] - dot_t(left, row[:, (c - 1) * B : c * B])
                at += 1


def factor(gram):
    rows, inverses = [], []
    for n in range(P_SIZE, 0, -1):
        shapes = [(B, (n - 1) * B), (B, B), (n * (n - 1) // 2, B, B)] if n > 1 else [(B, B)]
        done = on_chip(
            functools.partial(factor_step_kernel, n),
            shapes,
            "factor_step",
            gram,
            scratch=[pltpu.VMEM((B, n * B), jnp.float32), pltpu.VMEM((B, NB), jnp.float32)],
        )
        if n > 1:
            row, inverse, gram = done
            rows.append(row)
        else:
            (inverse,) = done
        inverses.append(inverse)
    return rows, inverses


def solve_kernel(place_ref, *refs):
    rows, inverses = refs[: P_SIZE - 1], refs[P_SIZE - 1 : 2 * P_SIZE - 1]
    gram_ref, pair_ref, other_ref, out_ref, own_ref = refs[-5:]
    row_index, col_index = 2 * place_ref[1] + place_ref[0], place_ref[3]

    @pl.when(col_index >= P_SIZE)
    def _():
        for h in range(2):
            own_ref[row_index ^ (2 * h)] = pair_ref[h]
            own_ref[row_index ^ (2 * h + 1)] = other_ref[h]

    for c in range(P_SIZE):

        @pl.when(col_index == c)
        def _(c=c):
            for r in range(P_SIZE):
                own_ref[r] = gram_ref[PAIRS.index((min(r, c), c))]

    done = []
    for i in range(P_SIZE):
        block = own_ref[i]
        for k in range(i):
            off = (i - k - 1) * B
            block = block - dot_t(rows[k][:, off : off + B], done[k])
        block = dot(inverses[i][...], block)
        done.append(block)

        @pl.when(row_index == i)
        def _(block=block):
            rows_at = i * B + lax.broadcasted_iota(jnp.int32, block.shape, 0)
            cols_at = col_index * B + lax.broadcasted_iota(jnp.int32, block.shape, 1)
            out_ref[...] = jnp.where(cols_at >= rows_at, block, 0.0)


def from_first(value, n_hi):
    at = lax.axis_index("hi")
    have = 1
    while have < n_hi:
        more = min(have, n_hi - have)
        got = lax.ppermute(value, "hi", [(g, g + have) for g in range(more)])
        value = jnp.where(at < have, value, got)
        have += more
    return value


def exchange(value, high_bits, low_bits):
    bits = low_bits * 2 + high_bits
    return lax.ppermute(value, ("lo", "rh"), [(i, i ^ bits) for i in range(2 * P_SIZE)])


def swap(value, axis="rl"):
    return lax.ppermute(value, axis, [(0, 1), (1, 0)])


def other_group(value):
    return lax.ppermute(value, ("hi", "lo"), [(i, i ^ 6) for i in range(2 * P_SIZE)])


def spread(piece):
    y, z, x = (0, 1), (0, 2), (1, 0)
    by_z, by_y, by_x = exchange(piece, *z), exchange(piece, *y), exchange(piece, *x)
    by_zy, by_yx, by_xz = exchange(by_z, *y), exchange(by_y, *x), exchange(by_x, *z)
    by_zyx = exchange(by_zy, *x)
    return jnp.stack([piece, by_y, by_z, by_zy, by_x, by_yx, by_xz, by_zyx])


def on_device(r_slab, arc_rows, arc_blocks):
    n_hi = lax.axis_size("hi")
    group, low = lax.axis_index("hi"), lax.axis_index("lo")
    high_row, side = lax.axis_index("rh"), lax.axis_index("rl")
    col_index = group * P_SIZE + low
    columns = arc_rows.shape[1]
    in_two = n_hi == 2
    panel = low ^ (2 * group) if in_two else low
    place = jnp.stack([side, high_row, panel, col_index, group]).astype(jnp.int32)
    total = r_slab.shape[0] + arc_rows.shape[0]
    parts = 2 * CHUNKS if in_two else CHUNKS
    chunks = on_chip(
        mask_kernel,
        [(total // parts, columns)] * parts,
        "mask",
        place,
        arc_blocks,
        r_slab,
        arc_rows,
        scalars=2,
        scratch=[pltpu.VMEM((total, columns), jnp.float32)],
    )
    y, z = (0, 1), (0, 2)

    def halves(k, sent_after, after):
        if not in_two:
            return from_first(chunks[k], n_hi), chunks[k]
        shape, sent = chunks[k].shape, chunks[CHUNKS + k]
        if sent_after:
            (sent,) = on_chip(pass_kernel, [shape], "sent", sent, after=sent_after)
        return on_chip(
            select_kernel,
            [shape, shape],
            "select",
            place,
            chunks[k],
            other_group(sent),
            scalars=1,
            after=after,
        )

    first, first_right = halves(0, (), ())
    first_y, first_z = exchange(first, *y), exchange(first, *z)
    first_zy = exchange(first_y, *z)
    second, second_right = halves(1, (first_y,), (first_z, first_zy))
    second_y, second_z = exchange(second, *y), exchange(second, *z)
    second_zy = exchange(second_z, *y)
    panels = [first, second, first_y, second_y, first_z, second_z, first_zy, second_zy]
    right = [first_right, second_right]

    pair, block = (2, B, B), (B, B)
    count = len(PAIRS) * B // P_SIZE // P_SIZE
    keep, keep_cross, send = on_chip(
        products_kernel,
        [(2, count, B), pair, (2, count + B, B)],
        "products",
        place,
        *panels,
        *right,
        scalars=1,
        scratch=[
            pltpu.VMEM((P_SIZE * count, B), jnp.float32),
            pltpu.VMEM((P_SIZE, B, B), jnp.float32),
        ],
    )
    got = swap(send)

    def picked(first, kept, after):
        return on_chip(
            functools.partial(pick_kernel, first),
            [kept.shape[1:]] * 2,
            "pick",
            place,
            kept,
            got,
            scalars=1,
            after=(after,),
        )

    mine, other = picked(0, keep, send)
    piece = mine + exchange(other, 1, 0)
    if in_two:
        piece = piece + other_group(piece)
    pieces = spread(piece)
    (gram,) = on_chip(
        collect_kernel,
        [(len(PAIRS), B, B)],
        "collect",
        place,
        pieces,
        swap(pieces),
        scalars=1,
    )

    def added(left, right, after):
        (total,) = on_chip(add_kernel, [block], "add", left, right, after=(after,))
        return total

    rows, inverses = factor(gram)
    mine, other = picked(count, keep_cross, gram)
    mine = added(mine, exchange(other, 1, 0), rows[0])
    if in_two:
        mine = added(mine, other_group(mine), rows[1])
    (own,) = on_chip(stack_kernel, [pair], "stack", mine, exchange(mine, 1, 0), after=(rows[2],))
    (result,) = on_chip(
        solve_kernel,
        [(B, columns)],
        "solve",
        place,
        *rows,
        *inverses,
        gram,
        own,
        swap(own),
        scalars=1,
        scratch=[pltpu.VMEM((P_SIZE, B, columns), jnp.float32)],
    )
    return result


def solution(mesh):
    n_col, n_row = mesh.shape["col"], mesh.shape["row"]
    split = Mesh(
        mesh.devices.reshape(n_col // P_SIZE, P_SIZE, n_row // 2, 2),
        ("hi", "lo", "rh", "rl"),
    )
    spec = P(("rh", "rl"), ("hi", "lo"))
    return jax.shard_map(
        on_device,
        mesh=split,
        in_specs=(spec, spec, spec),
        out_specs=spec,
        check_vma=False,
    )
```

```python
import functools

import jax
import jax.numpy as jnp
from jax import lax
from jax.experimental import pallas as pl
from jax.experimental.pallas import tpu as pltpu
from jax.sharding import Mesh
from jax.sharding import PartitionSpec as P

B = 256
P_SIZE = 4
ARC_ROWS = 128
NB = 128
SUB = 8


def split(value):
    high = value.astype(jnp.bfloat16)
    return high, (value - high.astype(jnp.float32)).astype(jnp.bfloat16)


def left_parts(value, axis=0):
    high, low = split(value)
    return jnp.concatenate([high, high, low], axis=axis)


def right_parts(value):
    high, low = split(value)
    return jnp.concatenate([high, low, high], axis=0)


def parts_dot(left, right):
    return lax.dot_general(
        left, right, (((0,), (0,)), ((), ())), preferred_element_type=jnp.float32
    )


def dot(left, right):
    return jnp.dot(left_parts(left, 1), right_parts(right), preferred_element_type=jnp.float32)


def dot_t(left, right):
    return parts_dot(left_parts(left), right_parts(right))


def lane(value, at):
    return jnp.broadcast_to(value[:, at : at + 1], (SUB, NB))


def row(value, at):
    return jnp.broadcast_to(value[at : at + 1, :], (SUB, NB))


def inverse_factor(rows):
    n = NB // SUB
    row_id = lax.broadcasted_iota(jnp.int32, (SUB, NB), 0)
    col_id = lax.broadcasted_iota(jnp.int32, (SUB, NB), 1)
    order = range(SUB)
    ahead = [lane(rows[0], m) for m in order]
    for b in range(n):
        j = b * SUB
        pivot = {(k, m): row(ahead[m], k) for k in order for m in range(k, SUB)}
        below = [[lane(rows[r], j + k) for k in order] for r in range(b + 1, n)]
        if b + 1 < n:
            ahead = [lane(rows[b + 1], j + SUB + m) for m in order]
        scale, left = [], []
        for k in order:
            scale.append(lax.rsqrt(pivot[k, k]))
            for m in range(k + 1, SUB):
                pivot[k, m] = pivot[k, m] * scale[k]
            for m in range(k + 1, SUB):
                for q in range(m, SUB):
                    pivot[m, q] = pivot[m, q] - pivot[k, m] * pivot[k, q]
            if b + 1 < n:
                part = below[0][k]
                for m in range(k):
                    part = part - pivot[m, k] * left[m]
                part = part * scale[k]
                left.append(part)
                for m in order:
                    ahead[m] = ahead[m] - part * row(part, m)
        inside = (col_id >= j) & (col_id < j + SUB)
        head = jnp.where(inside, jnp.where(col_id - j == row_id, 1.0, 0.0), rows[b])
        top = []
        for k in order:
            part = row(head, k)
            for m in range(k):
                part = part - pivot[m, k] * top[m]
            top.append(part * scale[k])
        if b + 1 < n:
            solved = [None] * SUB
            for k in reversed(order):
                part = top[k]
                for m in range(k + 1, SUB):
                    part = part - pivot[k, m] * solved[m]
                solved[k] = part * scale[k]
            for r in range(b + 1, n):
                body = jnp.where(inside, 0.0, rows[r])
                for k in order:
                    body = body - below[r - b - 1][k] * solved[k]
                rows[r] = body
        strip = top[0]
        for k in range(1, SUB):
            strip = jnp.where(row_id == k, top[k], strip)
        rows[b] = jnp.where(col_id < j + SUB, strip, 0.0)
    return rows


PAIRS = [(r, c) for r in range(P_SIZE) for c in range(r, P_SIZE)]
CHUNKS = 4


def mask_kernel(place_ref, arcs_ref, slab_ref, rows_ref, *refs):
    chunks, work = refs[:-1], refs[-1]
    top = slab_ref.shape[0]
    work[:top, :] = slab_ref[...]
    for a in range(arcs_ref.shape[0]):
        live = arcs_ref[a, 0].astype(jnp.float32)
        at = a * ARC_ROWS
        work[top + at : top + at + ARC_ROWS, :] = rows_ref[at : at + ARC_ROWS, :] * live
    count = chunks[0].shape[0]
    if len(chunks) > CHUNKS:
        first = jnp.where(place_ref[4] == 0, 0, CHUNKS * count)
    else:
        first = 0
    for s, chunk in enumerate(chunks):
        start = first + s * count if s < CHUNKS else CHUNKS * count - first + (s - CHUNKS) * count
        chunk[...] = work[pl.ds(pl.multiple_of(start, 16), count), :]


def select_kernel(place_ref, kept_ref, got_ref, *refs):
    panel_ref, right_ref = refs[-2:]

    @pl.when(place_ref[4] == 0)
    def _():
        panel_ref[...] = kept_ref[...]
        right_ref[...] = got_ref[...]

    @pl.when(place_ref[4] != 0)
    def _():
        panel_ref[...] = got_ref[...]
        right_ref[...] = kept_ref[...]


def products_kernel(place_ref, *refs):
    panels, right = refs[: P_SIZE * CHUNKS], refs[P_SIZE * CHUNKS : (P_SIZE + 1) * CHUNKS]
    keep_ref, keep_cross_ref, send_ref, upper, cross = refs[(P_SIZE + 1) * CHUNKS :]
    side, own = place_ref[0], place_ref[2]

    def whole(chunks):
        return jnp.concatenate([chunk[...] for chunk in chunks], axis=0)

    both = jnp.concatenate(
        [right_parts(whole(panels[:CHUNKS])), right_parts(whole(right))], axis=1
    )
    for t in range(P_SIZE):
        left = left_parts(whole(panels[t * CHUNKS : (t + 1) * CHUNKS]))
        product = parts_dot(left, both)
        cross[own ^ t] = product[:, B:]
        if t == 0:
            upper[:B, :] = product[:, :B]
            continue
        at = B + (t - 1) * B // 2

        @pl.when(own < (own ^ t))
        def _(at=at, product=product):
            upper[at : at + B // 2, :] = product[:, : B // 2].T

        @pl.when(own > (own ^ t))
        def _(at=at, product=product):
            upper[at : at + B // 2, :] = product[B // 2 :, :B]

    count = keep_ref.shape[1]
    for h in range(2):
        here, there = 2 * h + side, 2 * h + 1 - side
        keep_ref[h] = upper[pl.ds(pl.multiple_of(here * count, SUB), count), :]
        keep_cross_ref[h] = cross[here]
        send_ref[h, :count] = upper[pl.ds(pl.multiple_of(there * count, SUB), count), :]
        send_ref[h, count:] = cross[there]


def pick_kernel(first, place_ref, keep_ref, got_ref, _, own_ref, other_ref):
    high = place_ref[1]
    rows = pl.ds(first, own_ref.shape[0])
    own_ref[...] = keep_ref[high] + got_ref[high, rows]
    other_ref[...] = keep_ref[1 - high] + got_ref[1 - high, rows]


def stack_kernel(first_ref, second_ref, _, out_ref):
    out_ref[0] = first_ref[...]
    out_ref[1] = second_ref[...]


def add_kernel(left_ref, right_ref, after_ref, out_ref):
    del after_ref
    out_ref[...] = left_ref[...] + right_ref[...]


def on_chip(kernel, shapes, name, *operands, scratch=(), scalars=0, after=(), outside=()):
    done = pl.pallas_call(
        kernel,
        out_shape=[jax.ShapeDtypeStruct(shape, jnp.float32) for shape in shapes],
        in_specs=[pl.BlockSpec(memory_space=pltpu.SMEM)] * scalars
        + [pl.BlockSpec(memory_space=pltpu.VMEM)] * (len(operands) - scalars)
        + [pl.BlockSpec(memory_space=pltpu.HBM)] * len(outside)
        + [pl.BlockSpec(memory_space=pl.ANY)] * len(after),
        out_specs=[pl.BlockSpec(memory_space=pltpu.VMEM)] * len(shapes),
        scratch_shapes=list(scratch),
        compiler_params=pltpu.CompilerParams(vmem_limit_bytes=16 * 1024 * 1024),
        name=name,
    )(*operands, *outside, *after)
    return list(done)


def collect_kernel(place_ref, mine_ref, other_ref, gram_ref):
    side, at = place_ref[0], place_ref[1] * P_SIZE + place_ref[2]
    count = mine_ref.shape[1]
    for q in range(P_SIZE):
        runs = [(q, q, 0, B)]
        for t in range(1, P_SIZE):
            j = q ^ t
            runs.append((min(q, j), max(q, j), 0 if q < j else B // 2, B // 2))
        done = 0
        for r, c, first, size in runs:
            block, start, end = PAIRS.index((r, c)), done, done + size
            while start < end:
                piece, skip = start // count, start % count
                rows = min(end - start, count - skip)
                spot = ((piece // 2) * P_SIZE + q) ^ at
                into = slice(first + start - done, first + start - done + rows)

                @pl.when(side == piece % 2)
                def _(block=block, into=into, spot=spot, skip=skip, rows=rows):
                    gram_ref[block, into] = mine_ref[spot, skip : skip + rows]

                @pl.when(side != piece % 2)
                def _(block=block, into=into, spot=spot, skip=skip, rows=rows):
                    gram_ref[block, into] = other_ref[spot, skip : skip + rows]

                start += rows
            done = end


def factor_step_kernel(n, gram_ref, *rest):
    if n > 1:
        row_ref, inverse_ref, next_ref, work, inv = rest
    else:
        inverse_ref, work, inv = rest
    for c in range(n):
        work[:, c * B : (c + 1) * B] = gram_ref[c]
    width = n * B

    def step(b, carry):
        start = pl.multiple_of(b * NB, NB)
        rows = [
            work[pl.ds(pl.multiple_of(start + r * SUB, SUB), SUB), pl.ds(start, NB)]
            for r in range(NB // SUB)
        ]
        right = inverse_factor(rows)
        for r in range(NB // SUB):
            inv[pl.ds(pl.multiple_of(start + r * SUB, SUB), SUB), :] = right[r]

        @pl.when(b == 0)
        def _():
            panel = dot(inv[:NB, :], work[:NB, NB:])
            work[:NB, NB:] = panel
            work[NB:, NB:] = work[NB:, NB:] - dot_t(panel[:, :NB], panel)

        return carry

    lax.fori_loop(0, B // NB, step, 0)
    first, second = inv[:NB, :], inv[NB:, :]
    inverse_ref[:NB, :NB] = first
    inverse_ref[:NB, NB:] = jnp.zeros((NB, NB), jnp.float32)
    inverse_ref[NB:, :NB] = -dot(second, dot_t(work[:NB, NB:B], first))
    inverse_ref[NB:, NB:] = second
    if n > 1:
        work[NB:, B:] = dot(second, work[NB:, B:])
        row = work[:, B:]
        row_ref[...] = row
        at = n
        for r in range(1, n):
            left = row[:, (r - 1) * B : r * B]
            for c in range(r, n):
                next_ref[at - n] = gram_ref[at] - dot_t(left, row[:, (c - 1) * B : c * B])
                at += 1


def factor(gram):
    rows, inverses = [], []
    for n in range(P_SIZE, 0, -1):
        shapes = [(B, (n - 1) * B), (B, B), (n * (n - 1) // 2, B, B)] if n > 1 else [(B, B)]
        done = on_chip(
            functools.partial(factor_step_kernel, n),
            shapes,
            "factor_step",
            gram,
            scratch=[pltpu.VMEM((B, n * B), jnp.float32), pltpu.VMEM((B, NB), jnp.float32)],
        )
        if n > 1:
            row, inverse, gram = done
            rows.append(row)
        else:
            (inverse,) = done
        inverses.append(inverse)
    return rows, inverses


def solve_kernel(place_ref, *refs):
    rows, inverses = refs[: P_SIZE - 1], refs[P_SIZE - 1 : 2 * P_SIZE - 1]
    gram_ref, pair_ref, other_ref, out_ref, own_ref = refs[-5:]
    row_index, col_index = 2 * place_ref[1] + place_ref[0], place_ref[3]

    @pl.when(col_index >= P_SIZE)
    def _():
        for h in range(2):
            own_ref[row_index ^ (2 * h)] = pair_ref[h]
            own_ref[row_index ^ (2 * h + 1)] = other_ref[h]

    for c in range(P_SIZE):

        @pl.when(col_index == c)
        def _(c=c):
            for r in range(P_SIZE):
                own_ref[r] = gram_ref[PAIRS.index((min(r, c), c))]

    done = []
    for i in range(P_SIZE):
        block = own_ref[i]
        for k in range(i):
            off = (i - k - 1) * B
            block = block - dot_t(rows[k][:, off : off + B], done[k])
        block = dot(inverses[i][...], block)
        done.append(block)

        @pl.when(row_index == i)
        def _(block=block):
            rows_at = i * B + lax.broadcasted_iota(jnp.int32, block.shape, 0)
            cols_at = col_index * B + lax.broadcasted_iota(jnp.int32, block.shape, 1)
            out_ref[...] = jnp.where(cols_at >= rows_at, block, 0.0)


def from_first(value, n_hi):
    at = lax.axis_index("hi")
    have = 1
    while have < n_hi:
        more = min(have, n_hi - have)
        got = lax.ppermute(value, "hi", [(g, g + have) for g in range(more)])
        value = jnp.where(at < have, value, got)
        have += more
    return value


def exchange(value, high_bits, low_bits):
    bits = low_bits * 2 + high_bits
    return lax.ppermute(value, ("lo", "rh"), [(i, i ^ bits) for i in range(2 * P_SIZE)])


def swap(value, axis="rl"):
    return lax.ppermute(value, axis, [(0, 1), (1, 0)])


def other_group(value):
    return lax.ppermute(value, ("hi", "lo"), [(i, i ^ 6) for i in range(2 * P_SIZE)])


def spread(piece):
    y, z, x = (0, 1), (0, 2), (1, 0)
    by_z, by_y, by_x = exchange(piece, *z), exchange(piece, *y), exchange(piece, *x)
    by_zy, by_yx, by_xz = exchange(by_z, *y), exchange(by_y, *x), exchange(by_x, *z)
    by_zyx = exchange(by_zy, *x)
    return jnp.stack([piece, by_y, by_z, by_zy, by_x, by_yx, by_xz, by_zyx])


def on_device(r_slab, arc_rows, arc_blocks):
    n_hi = lax.axis_size("hi")
    group, low = lax.axis_index("hi"), lax.axis_index("lo")
    high_row, side = lax.axis_index("rh"), lax.axis_index("rl")
    col_index = group * P_SIZE + low
    columns = arc_rows.shape[1]
    in_two = n_hi == 2
    panel = low ^ (2 * group) if in_two else low
    place = jnp.stack([side, high_row, panel, col_index, group]).astype(jnp.int32)
    total = r_slab.shape[0] + arc_rows.shape[0]
    parts = 2 * CHUNKS if in_two else CHUNKS
    chunks = on_chip(
        mask_kernel,
        [(total // parts, columns)] * parts,
        "mask",
        place,
        arc_blocks,
        r_slab,
        arc_rows,
        scalars=2,
        scratch=[pltpu.VMEM((total, columns), jnp.float32)],
    )
    y, z = (0, 1), (0, 2)

    def halves(k, after):
        if not in_two:
            return from_first(chunks[k], n_hi), chunks[k]
        shape = chunks[k].shape
        return on_chip(
            select_kernel,
            [shape, shape],
            "select",
            place,
            chunks[k],
            other_group(chunks[CHUNKS + k]),
            scalars=1,
            after=after,
        )

    panels, right, before, relayed = [[] for _ in range(P_SIZE)], [], (), ()
    for k in range(CHUNKS):
        own, own_right = halves(k, before)
        early, late = (y, z) if k % 2 == 0 else (z, y)
        by_early, by_late = exchange(own, *early), exchange(own, *late)
        before = (by_early, by_late, *relayed)
        by_both = exchange(by_early, *late)
        relayed = (by_both,)
        by_y, by_z = (by_early, by_late) if k % 2 == 0 else (by_late, by_early)
        for chunks_of, chunk in zip(panels, (own, by_y, by_z, by_both)):
            chunks_of.append(chunk)
        right.append(own_right)
    panels = [chunk for chunks_of in panels for chunk in chunks_of]

    pair, block = (2, B, B), (B, B)
    count = len(PAIRS) * B // P_SIZE // P_SIZE
    keep, keep_cross, send = on_chip(
        products_kernel,
        [(2, count, B), pair, (2, count + B, B)],
        "products",
        place,
        *panels,
        *right,
        scalars=1,
        scratch=[
            pltpu.VMEM((P_SIZE * count, B), jnp.float32),
            pltpu.VMEM((P_SIZE, B, B), jnp.float32),
        ],
    )
    got = swap(send)

    def picked(first, kept, after):
        return on_chip(
            functools.partial(pick_kernel, first),
            [kept.shape[1:]] * 2,
            "pick",
            place,
            kept,
            got,
            scalars=1,
            after=(after,),
        )

    mine, other = picked(0, keep, send)
    piece = mine + exchange(other, 1, 0)
    if in_two:
        piece = piece + other_group(piece)
    pieces = spread(piece)
    (gram,) = on_chip(
        collect_kernel,
        [(len(PAIRS), B, B)],
        "collect",
        place,
        pieces,
        swap(pieces),
        scalars=1,
    )

    def added(left, right, after):
        (total,) = on_chip(add_kernel, [block], "add", left, right, after=(after,))
        return total

    rows, inverses = factor(gram)
    mine, other = picked(count, keep_cross, gram)
    mine = added(mine, exchange(other, 1, 0), rows[0])
    if in_two:
        mine = added(mine, other_group(mine), rows[1])
    (own,) = on_chip(stack_kernel, [pair], "stack", mine, exchange(mine, 1, 0), after=(rows[2],))
    (result,) = on_chip(
        solve_kernel,
        [(B, columns)],
        "solve",
        place,
        *rows,
        *inverses,
        gram,
        own,
        swap(own),
        scalars=1,
        scratch=[pltpu.VMEM((P_SIZE, B, columns), jnp.float32)],
    )
    return result


def solution(mesh):
    n_col, n_row = mesh.shape["col"], mesh.shape["row"]
    split = Mesh(
        mesh.devices.reshape(n_col // P_SIZE, P_SIZE, n_row // 2, 2),
        ("hi", "lo", "rh", "rl"),
    )
    spec = P(("rh", "rl"), ("hi", "lo"))
    return jax.shard_map(
        on_device,
        mesh=split,
        in_specs=(spec, spec, spec),
        out_specs=spec,
        check_vma=False,
    )
```

```python
import functools

import jax
import jax.numpy as jnp
from jax import lax
from jax.experimental import pallas as pl
from jax.experimental.pallas import tpu as pltpu
from jax.sharding import Mesh
from jax.sharding import PartitionSpec as P

B = 256
P_SIZE = 4
ARC_ROWS = 128
NB = 128
SUB = 8


def split(value):
    high = value.astype(jnp.bfloat16)
    return high, (value - high.astype(jnp.float32)).astype(jnp.bfloat16)


def left_parts(value, axis=0):
    high, low = split(value)
    return jnp.concatenate([high, high, low], axis=axis)


def right_parts(value):
    high, low = split(value)
    return jnp.concatenate([high, low, high], axis=0)


def parts_dot(left, right):
    return lax.dot_general(
        left, right, (((0,), (0,)), ((), ())), preferred_element_type=jnp.float32
    )


def dot(left, right):
    return jnp.dot(left_parts(left, 1), right_parts(right), preferred_element_type=jnp.float32)


def dot_t(left, right):
    return parts_dot(left_parts(left), right_parts(right))


def lane(value, at):
    return jnp.broadcast_to(value[:, at : at + 1], (SUB, NB))


def row(value, at):
    return jnp.broadcast_to(value[at : at + 1, :], (SUB, NB))


def inverse_factor(rows):
    n = NB // SUB
    row_id = lax.broadcasted_iota(jnp.int32, (SUB, NB), 0)
    col_id = lax.broadcasted_iota(jnp.int32, (SUB, NB), 1)
    order = range(SUB)
    ahead = [lane(rows[0], m) for m in order]
    for b in range(n):
        j = b * SUB
        pivot = {(k, m): row(ahead[m], k) for k in order for m in range(k, SUB)}
        below = [[lane(rows[r], j + k) for k in order] for r in range(b + 1, n)]
        if b + 1 < n:
            ahead = [lane(rows[b + 1], j + SUB + m) for m in order]
        scale, left = [], []
        for k in order:
            scale.append(lax.rsqrt(pivot[k, k]))
            for m in range(k + 1, SUB):
                pivot[k, m] = pivot[k, m] * scale[k]
            for m in range(k + 1, SUB):
                for q in range(m, SUB):
                    pivot[m, q] = pivot[m, q] - pivot[k, m] * pivot[k, q]
            if b + 1 < n:
                part = below[0][k]
                for m in range(k):
                    part = part - pivot[m, k] * left[m]
                part = part * scale[k]
                left.append(part)
                for m in order:
                    ahead[m] = ahead[m] - part * row(part, m)
        inside = (col_id >= j) & (col_id < j + SUB)
        head = jnp.where(inside, jnp.where(col_id - j == row_id, 1.0, 0.0), rows[b])
        top = []
        for k in order:
            part = row(head, k)
            for m in range(k):
                part = part - pivot[m, k] * top[m]
            top.append(part * scale[k])
        if b + 1 < n:
            solved = [None] * SUB
            for k in reversed(order):
                part = top[k]
                for m in range(k + 1, SUB):
                    part = part - pivot[k, m] * solved[m]
                solved[k] = part * scale[k]
            for r in range(b + 1, n):
                body = jnp.where(inside, 0.0, rows[r])
                for k in order:
                    body = body - below[r - b - 1][k] * solved[k]
                rows[r] = body
        strip = top[0]
        for k in range(1, SUB):
            strip = jnp.where(row_id == k, top[k], strip)
        rows[b] = jnp.where(col_id < j + SUB, strip, 0.0)
    return rows


PAIRS = [(r, c) for r in range(P_SIZE) for c in range(r, P_SIZE)]
CHUNKS = 4


def mask_kernel(place_ref, arcs_ref, slab_ref, rows_ref, *refs):
    chunks, work = refs[:-1], refs[-1]
    top = slab_ref.shape[0]
    work[:top, :] = slab_ref[...]
    for a in range(arcs_ref.shape[0]):
        live = arcs_ref[a, 0].astype(jnp.float32)
        at = a * ARC_ROWS
        work[top + at : top + at + ARC_ROWS, :] = rows_ref[at : at + ARC_ROWS, :] * live
    count = chunks[0].shape[0]
    if len(chunks) > CHUNKS:
        first = jnp.where(place_ref[4] == 0, 0, CHUNKS * count)
    else:
        first = 0
    for s, chunk in enumerate(chunks):
        start = first + s * count if s < CHUNKS else CHUNKS * count - first + (s - CHUNKS) * count
        chunk[...] = work[pl.ds(pl.multiple_of(start, 16), count), :]


def select_kernel(place_ref, kept_ref, got_ref, *refs):
    panel_ref, right_ref = refs[-2:]

    @pl.when(place_ref[4] == 0)
    def _():
        panel_ref[...] = kept_ref[...]
        right_ref[...] = got_ref[...]

    @pl.when(place_ref[4] != 0)
    def _():
        panel_ref[...] = got_ref[...]
        right_ref[...] = kept_ref[...]


def products_kernel(place_ref, *refs):
    n = CHUNKS // 2
    panels, right = refs[: P_SIZE * n], refs[P_SIZE * n : (P_SIZE + 1) * n]
    refs = refs[(P_SIZE + 1) * n :]
    last = len(refs) > 2
    if last:
        old_upper, old_cross, keep_ref, keep_cross_ref, send_ref, upper, cross = refs
    else:
        upper, cross = refs
    side, own = place_ref[0], place_ref[2]

    def whole(chunks):
        return jnp.concatenate([chunk[...] for chunk in chunks], axis=0)

    both = jnp.concatenate([right_parts(whole(panels[:n])), right_parts(whole(right))], axis=1)
    for t in range(P_SIZE):
        left = left_parts(whole(panels[t * n : (t + 1) * n]))
        product = parts_dot(left, both)
        spot = own ^ t
        cross[spot] = product[:, B:] + old_cross[spot] if last else product[:, B:]
        rows = slice(0, B) if t == 0 else slice(B + (t - 1) * B // 2, B + t * B // 2)
        if t == 0:
            upper[rows, :] = product[:, :B]
        else:

            @pl.when(own < spot)
            def _(rows=rows, product=product):
                upper[rows, :] = product[:, : B // 2].T

            @pl.when(own > spot)
            def _(rows=rows, product=product):
                upper[rows, :] = product[B // 2 :, :B]

    if not last:
        return
    upper[...] = upper[...] + old_upper[...]
    count = keep_ref.shape[1]
    for h in range(2):
        here, there = 2 * h + side, 2 * h + 1 - side
        keep_ref[h] = upper[pl.ds(pl.multiple_of(here * count, SUB), count), :]
        keep_cross_ref[h] = cross[here]
        send_ref[h, :count] = upper[pl.ds(pl.multiple_of(there * count, SUB), count), :]
        send_ref[h, count:] = cross[there]


def pick_kernel(first, place_ref, keep_ref, got_ref, _, own_ref, other_ref):
    high = place_ref[1]
    rows = pl.ds(first, own_ref.shape[0])
    own_ref[...] = keep_ref[high] + got_ref[high, rows]
    other_ref[...] = keep_ref[1 - high] + got_ref[1 - high, rows]


def stack_kernel(first_ref, second_ref, _, out_ref):
    out_ref[0] = first_ref[...]
    out_ref[1] = second_ref[...]


def add_kernel(left_ref, right_ref, after_ref, out_ref):
    del after_ref
    out_ref[...] = left_ref[...] + right_ref[...]


def on_chip(kernel, shapes, name, *operands, scratch=(), scalars=0, after=(), outside=()):
    done = pl.pallas_call(
        kernel,
        out_shape=[jax.ShapeDtypeStruct(shape, jnp.float32) for shape in shapes],
        in_specs=[pl.BlockSpec(memory_space=pltpu.SMEM)] * scalars
        + [pl.BlockSpec(memory_space=pltpu.VMEM)] * (len(operands) - scalars)
        + [pl.BlockSpec(memory_space=pltpu.HBM)] * len(outside)
        + [pl.BlockSpec(memory_space=pl.ANY)] * len(after),
        out_specs=[pl.BlockSpec(memory_space=pltpu.VMEM)] * len(shapes),
        scratch_shapes=list(scratch),
        compiler_params=pltpu.CompilerParams(vmem_limit_bytes=16 * 1024 * 1024),
        name=name,
    )(*operands, *outside, *after)
    return list(done)


def collect_kernel(place_ref, mine_ref, other_ref, gram_ref):
    side, at = place_ref[0], place_ref[1] * P_SIZE + place_ref[2]
    count = mine_ref.shape[1]
    for q in range(P_SIZE):
        runs = [(q, q, 0, B)]
        for t in range(1, P_SIZE):
            j = q ^ t
            runs.append((min(q, j), max(q, j), 0 if q < j else B // 2, B // 2))
        done = 0
        for r, c, first, size in runs:
            block, start, end = PAIRS.index((r, c)), done, done + size
            while start < end:
                piece, skip = start // count, start % count
                rows = min(end - start, count - skip)
                spot = ((piece // 2) * P_SIZE + q) ^ at
                into = slice(first + start - done, first + start - done + rows)

                @pl.when(side == piece % 2)
                def _(block=block, into=into, spot=spot, skip=skip, rows=rows):
                    gram_ref[block, into] = mine_ref[spot, skip : skip + rows]

                @pl.when(side != piece % 2)
                def _(block=block, into=into, spot=spot, skip=skip, rows=rows):
                    gram_ref[block, into] = other_ref[spot, skip : skip + rows]

                start += rows
            done = end


def factor_step_kernel(n, gram_ref, *rest):
    if n > 1:
        row_ref, inverse_ref, next_ref, work, inv = rest
    else:
        inverse_ref, work, inv = rest
    for c in range(n):
        work[:, c * B : (c + 1) * B] = gram_ref[c]
    width = n * B

    def step(b, carry):
        start = pl.multiple_of(b * NB, NB)
        rows = [
            work[pl.ds(pl.multiple_of(start + r * SUB, SUB), SUB), pl.ds(start, NB)]
            for r in range(NB // SUB)
        ]
        right = inverse_factor(rows)
        for r in range(NB // SUB):
            inv[pl.ds(pl.multiple_of(start + r * SUB, SUB), SUB), :] = right[r]

        @pl.when(b == 0)
        def _():
            panel = dot(inv[:NB, :], work[:NB, NB:])
            work[:NB, NB:] = panel
            work[NB:, NB:] = work[NB:, NB:] - dot_t(panel[:, :NB], panel)

        return carry

    lax.fori_loop(0, B // NB, step, 0)
    first, second = inv[:NB, :], inv[NB:, :]
    inverse_ref[:NB, :NB] = first
    inverse_ref[:NB, NB:] = jnp.zeros((NB, NB), jnp.float32)
    inverse_ref[NB:, :NB] = -dot(second, dot_t(work[:NB, NB:B], first))
    inverse_ref[NB:, NB:] = second
    if n > 1:
        work[NB:, B:] = dot(second, work[NB:, B:])
        row = work[:, B:]
        row_ref[...] = row
        at = n
        for r in range(1, n):
            left = row[:, (r - 1) * B : r * B]
            for c in range(r, n):
                next_ref[at - n] = gram_ref[at] - dot_t(left, row[:, (c - 1) * B : c * B])
                at += 1


def factor(gram):
    rows, inverses = [], []
    for n in range(P_SIZE, 0, -1):
        shapes = [(B, (n - 1) * B), (B, B), (n * (n - 1) // 2, B, B)] if n > 1 else [(B, B)]
        done = on_chip(
            functools.partial(factor_step_kernel, n),
            shapes,
            "factor_step",
            gram,
            scratch=[pltpu.VMEM((B, n * B), jnp.float32), pltpu.VMEM((B, NB), jnp.float32)],
        )
        if n > 1:
            row, inverse, gram = done
            rows.append(row)
        else:
            (inverse,) = done
        inverses.append(inverse)
    return rows, inverses


def solve_kernel(place_ref, *refs):
    rows, inverses = refs[: P_SIZE - 1], refs[P_SIZE - 1 : 2 * P_SIZE - 1]
    gram_ref, pair_ref, other_ref, out_ref, own_ref = refs[-5:]
    row_index, col_index = 2 * place_ref[1] + place_ref[0], place_ref[3]

    @pl.when(col_index >= P_SIZE)
    def _():
        for h in range(2):
            own_ref[row_index ^ (2 * h)] = pair_ref[h]
            own_ref[row_index ^ (2 * h + 1)] = other_ref[h]

    for c in range(P_SIZE):

        @pl.when(col_index == c)
        def _(c=c):
            for r in range(P_SIZE):
                own_ref[r] = gram_ref[PAIRS.index((min(r, c), c))]

    done = []
    for i in range(P_SIZE):
        block = own_ref[i]
        for k in range(i):
            off = (i - k - 1) * B
            block = block - dot_t(rows[k][:, off : off + B], done[k])
        block = dot(inverses[i][...], block)
        done.append(block)

        @pl.when(row_index == i)
        def _(block=block):
            rows_at = i * B + lax.broadcasted_iota(jnp.int32, block.shape, 0)
            cols_at = col_index * B + lax.broadcasted_iota(jnp.int32, block.shape, 1)
            out_ref[...] = jnp.where(cols_at >= rows_at, block, 0.0)


def from_first(value, n_hi):
    at = lax.axis_index("hi")
    have = 1
    while have < n_hi:
        more = min(have, n_hi - have)
        got = lax.ppermute(value, "hi", [(g, g + have) for g in range(more)])
        value = jnp.where(at < have, value, got)
        have += more
    return value


def exchange(value, high_bits, low_bits):
    bits = low_bits * 2 + high_bits
    return lax.ppermute(value, ("lo", "rh"), [(i, i ^ bits) for i in range(2 * P_SIZE)])


def swap(value, axis="rl"):
    return lax.ppermute(value, axis, [(0, 1), (1, 0)])


def other_group(value):
    return lax.ppermute(value, ("hi", "lo"), [(i, i ^ 6) for i in range(2 * P_SIZE)])


def spread(piece):
    y, z, x = (0, 1), (0, 2), (1, 0)
    by_z, by_y, by_x = exchange(piece, *z), exchange(piece, *y), exchange(piece, *x)
    by_zy, by_yx, by_xz = exchange(by_z, *y), exchange(by_y, *x), exchange(by_x, *z)
    by_zyx = exchange(by_zy, *x)
    return jnp.stack([piece, by_y, by_z, by_zy, by_x, by_yx, by_xz, by_zyx])


def on_device(r_slab, arc_rows, arc_blocks):
    n_hi = lax.axis_size("hi")
    group, low = lax.axis_index("hi"), lax.axis_index("lo")
    high_row, side = lax.axis_index("rh"), lax.axis_index("rl")
    col_index = group * P_SIZE + low
    columns = arc_rows.shape[1]
    in_two = n_hi == 2
    panel = low ^ (2 * group) if in_two else low
    place = jnp.stack([side, high_row, panel, col_index, group]).astype(jnp.int32)
    total = r_slab.shape[0] + arc_rows.shape[0]
    parts = 2 * CHUNKS if in_two else CHUNKS
    chunks = on_chip(
        mask_kernel,
        [(total // parts, columns)] * parts,
        "mask",
        place,
        arc_blocks,
        r_slab,
        arc_rows,
        scalars=2,
        scratch=[pltpu.VMEM((total, columns), jnp.float32)],
    )
    y, z = (0, 1), (0, 2)

    def halves(k, after):
        if not in_two:
            return from_first(chunks[k], n_hi), chunks[k]
        shape = chunks[k].shape
        return on_chip(
            select_kernel,
            [shape, shape],
            "select",
            place,
            chunks[k],
            other_group(chunks[CHUNKS + k]),
            scalars=1,
            after=after,
        )

    pair, block = (2, B, B), (B, B)
    count = len(PAIRS) * B // P_SIZE // P_SIZE
    sums = [(P_SIZE * count, B), (P_SIZE, B, B)]
    panels, right, before, relayed = [[] for _ in range(P_SIZE)], [], (), ()
    for k in range(CHUNKS):
        if k == CHUNKS - 1:
            half = [chunk for chunks_of in panels for chunk in chunks_of[: CHUNKS // 2]]
            begun = on_chip(
                products_kernel,
                sums,
                "first_products",
                place,
                *half,
                *right[: CHUNKS // 2],
                scalars=1,
            )
            before = (*before, begun[0])
        own, own_right = halves(k, before)
        early, late = (y, z) if k % 2 == 0 else (z, y)
        by_early, by_late = exchange(own, *early), exchange(own, *late)
        before = (by_early, by_late, *relayed)
        by_both = exchange(by_early, *late)
        relayed = (by_both,)
        by_y, by_z = (by_early, by_late) if k % 2 == 0 else (by_late, by_early)
        for chunks_of, chunk in zip(panels, (own, by_y, by_z, by_both)):
            chunks_of.append(chunk)
        right.append(own_right)
    half = [chunk for chunks_of in panels for chunk in chunks_of[CHUNKS // 2 :]]
    keep, keep_cross, send = on_chip(
        products_kernel,
        [(2, count, B), pair, (2, count + B, B)],
        "products",
        place,
        *half,
        *right[CHUNKS // 2 :],
        *begun,
        scalars=1,
        scratch=[pltpu.VMEM(shape, jnp.float32) for shape in sums],
    )
    got = swap(send)

    def picked(first, kept, after):
        return on_chip(
            functools.partial(pick_kernel, first),
            [kept.shape[1:]] * 2,
            "pick",
            place,
            kept,
            got,
            scalars=1,
            after=(after,),
        )

    mine, other = picked(0, keep, send)
    piece = mine + exchange(other, 1, 0)
    mine, other = picked(count, keep_cross, piece)
    if in_two:
        (piece,) = on_chip(
            add_kernel, [piece.shape], "add", piece, other_group(piece), after=(other,)
        )
    other = exchange(other, 1, 0)
    pieces = spread(piece)
    (gram,) = on_chip(
        collect_kernel,
        [(len(PAIRS), B, B)],
        "collect",
        place,
        pieces,
        swap(pieces),
        scalars=1,
    )

    def added(left, right, after):
        (total,) = on_chip(add_kernel, [block], "add", left, right, after=(after,))
        return total

    rows, inverses = factor(gram)
    mine = added(mine, other, rows[0])
    if in_two:
        mine = added(mine, other_group(mine), rows[1])
    (own,) = on_chip(stack_kernel, [pair], "stack", mine, exchange(mine, 1, 0), after=(rows[2],))
    (result,) = on_chip(
        solve_kernel,
        [(B, columns)],
        "solve",
        place,
        *rows,
        *inverses,
        gram,
        own,
        swap(own),
        scalars=1,
        scratch=[pltpu.VMEM((P_SIZE, B, columns), jnp.float32)],
    )
    return result


def solution(mesh):
    n_col, n_row = mesh.shape["col"], mesh.shape["row"]
    split = Mesh(
        mesh.devices.reshape(n_col // P_SIZE, P_SIZE, n_row // 2, 2),
        ("hi", "lo", "rh", "rl"),
    )
    spec = P(("rh", "rl"), ("hi", "lo"))
    return jax.shard_map(
        on_device,
        mesh=split,
        in_specs=(spec, spec, spec),
        out_specs=spec,
        check_vma=False,
    )
```

```python
import functools

import jax
import jax.numpy as jnp
from jax import lax
from jax.experimental import pallas as pl
from jax.experimental.pallas import tpu as pltpu
from jax.sharding import Mesh
from jax.sharding import PartitionSpec as P

B = 256
P_SIZE = 4
ARC_ROWS = 128
NB = 128
SUB = 8


def split(value):
    high = value.astype(jnp.bfloat16)
    return high, (value - high.astype(jnp.float32)).astype(jnp.bfloat16)


def left_parts(value, axis=0):
    high, low = split(value)
    return jnp.concatenate([high, high, low], axis=axis)


def right_parts(value):
    high, low = split(value)
    return jnp.concatenate([high, low, high], axis=0)


def parts_dot(left, right):
    return lax.dot_general(
        left, right, (((0,), (0,)), ((), ())), preferred_element_type=jnp.float32
    )


def dot(left, right):
    return jnp.dot(left_parts(left, 1), right_parts(right), preferred_element_type=jnp.float32)


def dot_t(left, right):
    return parts_dot(left_parts(left), right_parts(right))


def lane(value, at):
    return jnp.broadcast_to(value[:, at : at + 1], (SUB, NB))


def row(value, at):
    return jnp.broadcast_to(value[at : at + 1, :], (SUB, NB))


def inverse_factor(rows):
    n = NB // SUB
    row_id = lax.broadcasted_iota(jnp.int32, (SUB, NB), 0)
    col_id = lax.broadcasted_iota(jnp.int32, (SUB, NB), 1)
    order = range(SUB)
    ahead = [lane(rows[0], m) for m in order]
    for b in range(n):
        j = b * SUB
        pivot = {(k, m): row(ahead[m], k) for k in order for m in range(k, SUB)}
        below = [[lane(rows[r], j + k) for k in order] for r in range(b + 1, n)]
        if b + 1 < n:
            ahead = [lane(rows[b + 1], j + SUB + m) for m in order]
        scale, left = [], []
        for k in order:
            scale.append(lax.rsqrt(pivot[k, k]))
            for m in range(k + 1, SUB):
                pivot[k, m] = pivot[k, m] * scale[k]
            for m in range(k + 1, SUB):
                for q in range(m, SUB):
                    pivot[m, q] = pivot[m, q] - pivot[k, m] * pivot[k, q]
            if b + 1 < n:
                part = below[0][k]
                for m in range(k):
                    part = part - pivot[m, k] * left[m]
                part = part * scale[k]
                left.append(part)
                for m in order:
                    ahead[m] = ahead[m] - part * row(part, m)
        inside = (col_id >= j) & (col_id < j + SUB)
        head = jnp.where(inside, jnp.where(col_id - j == row_id, 1.0, 0.0), rows[b])
        top = []
        for k in order:
            part = row(head, k)
            for m in range(k):
                part = part - pivot[m, k] * top[m]
            top.append(part * scale[k])
        if b + 1 < n:
            solved = [None] * SUB
            for k in reversed(order):
                part = top[k]
                for m in range(k + 1, SUB):
                    part = part - pivot[k, m] * solved[m]
                solved[k] = part * scale[k]
            for r in range(b + 1, n):
                body = jnp.where(inside, 0.0, rows[r])
                for k in order:
                    body = body - below[r - b - 1][k] * solved[k]
                rows[r] = body
        strip = top[0]
        for k in range(1, SUB):
            strip = jnp.where(row_id == k, top[k], strip)
        rows[b] = jnp.where(col_id < j + SUB, strip, 0.0)
    return rows


PAIRS = [(r, c) for r in range(P_SIZE) for c in range(r, P_SIZE)]
CHUNKS = 4


def mask_kernel(place_ref, arcs_ref, slab_ref, rows_ref, *refs):
    chunks, work = refs[:-1], refs[-1]
    top = slab_ref.shape[0]
    work[:top, :] = slab_ref[...]
    for a in range(arcs_ref.shape[0]):
        live = arcs_ref[a, 0].astype(jnp.float32)
        at = a * ARC_ROWS
        work[top + at : top + at + ARC_ROWS, :] = rows_ref[at : at + ARC_ROWS, :] * live
    count = chunks[0].shape[0]
    if len(chunks) > CHUNKS:
        first = jnp.where(place_ref[4] == 0, 0, CHUNKS * count)
    else:
        first = 0
    for s, chunk in enumerate(chunks):
        start = first + s * count if s < CHUNKS else CHUNKS * count - first + (s - CHUNKS) * count
        chunk[...] = work[pl.ds(pl.multiple_of(start, 16), count), :]


def select_kernel(place_ref, kept_ref, got_ref, *refs):
    panel_ref, right_ref = refs[-2:]

    @pl.when(place_ref[4] == 0)
    def _():
        panel_ref[...] = kept_ref[...]
        right_ref[...] = got_ref[...]

    @pl.when(place_ref[4] != 0)
    def _():
        panel_ref[...] = got_ref[...]
        right_ref[...] = kept_ref[...]


def products_kernel(place_ref, *refs):
    n = CHUNKS // 2
    panels, right = refs[: P_SIZE * n], refs[P_SIZE * n : (P_SIZE + 1) * n]
    refs = refs[(P_SIZE + 1) * n :]
    last = len(refs) > 2
    if last:
        old_upper, old_cross, keep_ref, keep_cross_ref, send_ref, upper, cross = refs
    else:
        upper, cross = refs
    side, own = place_ref[0], place_ref[2]

    def whole(chunks):
        return jnp.concatenate([chunk[...] for chunk in chunks], axis=0)

    both = jnp.concatenate([right_parts(whole(panels[:n])), right_parts(whole(right))], axis=1)
    for t in range(P_SIZE):
        left = left_parts(whole(panels[t * n : (t + 1) * n]))
        product = parts_dot(left, both)
        spot = own ^ t
        cross[spot] = product[:, B:] + old_cross[spot] if last else product[:, B:]
        rows = slice(0, B) if t == 0 else slice(B + (t - 1) * B // 2, B + t * B // 2)
        if t == 0:
            upper[rows, :] = product[:, :B]
        else:

            @pl.when(own < spot)
            def _(rows=rows, product=product):
                upper[rows, :] = product[:, : B // 2].T

            @pl.when(own > spot)
            def _(rows=rows, product=product):
                upper[rows, :] = product[B // 2 :, :B]

    if not last:
        return
    upper[...] = upper[...] + old_upper[...]
    count = keep_ref.shape[1]
    for h in range(2):
        here, there = 2 * h + side, 2 * h + 1 - side
        keep_ref[h] = upper[pl.ds(pl.multiple_of(here * count, SUB), count), :]
        keep_cross_ref[h] = cross[here]
        send_ref[h, :count] = upper[pl.ds(pl.multiple_of(there * count, SUB), count), :]
        send_ref[h, count:] = cross[there]


def pick_kernel(first, place_ref, keep_ref, got_ref, _, own_ref, other_ref):
    high = place_ref[1]
    rows = pl.ds(first, own_ref.shape[0])
    own_ref[...] = keep_ref[high] + got_ref[high, rows]
    other_ref[...] = keep_ref[1 - high] + got_ref[1 - high, rows]


def stack_kernel(first_ref, second_ref, _, out_ref):
    out_ref[0] = first_ref[...]
    out_ref[1] = second_ref[...]


def add_kernel(left_ref, right_ref, after_ref, out_ref):
    del after_ref
    out_ref[...] = left_ref[...] + right_ref[...]


def on_chip(kernel, shapes, name, *operands, scratch=(), scalars=0, after=(), outside=()):
    done = pl.pallas_call(
        kernel,
        out_shape=[jax.ShapeDtypeStruct(shape, jnp.float32) for shape in shapes],
        in_specs=[pl.BlockSpec(memory_space=pltpu.SMEM)] * scalars
        + [pl.BlockSpec(memory_space=pltpu.VMEM)] * (len(operands) - scalars)
        + [pl.BlockSpec(memory_space=pltpu.HBM)] * len(outside)
        + [pl.BlockSpec(memory_space=pl.ANY)] * len(after),
        out_specs=[pl.BlockSpec(memory_space=pltpu.VMEM)] * len(shapes),
        scratch_shapes=list(scratch),
        compiler_params=pltpu.CompilerParams(vmem_limit_bytes=16 * 1024 * 1024),
        name=name,
    )(*operands, *outside, *after)
    return list(done)


def collect_kernel(place_ref, mine_ref, other_ref, gram_ref):
    side, at = place_ref[0], place_ref[1] * P_SIZE + place_ref[2]
    count = mine_ref.shape[1]
    for q in range(P_SIZE):
        runs = [(q, q, 0, B)]
        for t in range(1, P_SIZE):
            j = q ^ t
            runs.append((min(q, j), max(q, j), 0 if q < j else B // 2, B // 2))
        done = 0
        for r, c, first, size in runs:
            block, start, end = PAIRS.index((r, c)), done, done + size
            while start < end:
                piece, skip = start // count, start % count
                rows = min(end - start, count - skip)
                spot = ((piece // 2) * P_SIZE + q) ^ at
                into = slice(first + start - done, first + start - done + rows)

                @pl.when(side == piece % 2)
                def _(block=block, into=into, spot=spot, skip=skip, rows=rows):
                    gram_ref[block, into] = mine_ref[spot, skip : skip + rows]

                @pl.when(side != piece % 2)
                def _(block=block, into=into, spot=spot, skip=skip, rows=rows):
                    gram_ref[block, into] = other_ref[spot, skip : skip + rows]

                start += rows
            done = end


def factor_step_kernel(n, gram_ref, *rest):
    if n > 1:
        row_ref, inverse_ref, next_ref, work, inv = rest
    else:
        inverse_ref, work, inv = rest
    for c in range(n):
        work[:, c * B : (c + 1) * B] = gram_ref[c]
    width = n * B

    def step(b, carry):
        start = pl.multiple_of(b * NB, NB)
        rows = [
            work[pl.ds(pl.multiple_of(start + r * SUB, SUB), SUB), pl.ds(start, NB)]
            for r in range(NB // SUB)
        ]
        right = inverse_factor(rows)
        for r in range(NB // SUB):
            inv[pl.ds(pl.multiple_of(start + r * SUB, SUB), SUB), :] = right[r]

        @pl.when(b == 0)
        def _():
            panel = dot(inv[:NB, :], work[:NB, NB:])
            work[:NB, NB:] = panel
            work[NB:, NB:] = work[NB:, NB:] - dot_t(panel[:, :NB], panel)

        return carry

    lax.fori_loop(0, B // NB, step, 0)
    first, second = inv[:NB, :], inv[NB:, :]
    inverse_ref[:NB, :NB] = first
    inverse_ref[:NB, NB:] = jnp.zeros((NB, NB), jnp.float32)
    inverse_ref[NB:, :NB] = -dot(second, dot_t(work[:NB, NB:B], first))
    inverse_ref[NB:, NB:] = second
    if n > 1:
        work[NB:, B:] = dot(second, work[NB:, B:])
        row = work[:, B:]
        row_ref[...] = row
        at = n
        for r in range(1, n):
            left = row[:, (r - 1) * B : r * B]
            for c in range(r, n):
                next_ref[at - n] = gram_ref[at] - dot_t(left, row[:, (c - 1) * B : c * B])
                at += 1


def factor(gram):
    rows, inverses = [], []
    for n in range(P_SIZE, 0, -1):
        shapes = [(B, (n - 1) * B), (B, B), (n * (n - 1) // 2, B, B)] if n > 1 else [(B, B)]
        done = on_chip(
            functools.partial(factor_step_kernel, n),
            shapes,
            "factor_step",
            gram,
            scratch=[pltpu.VMEM((B, n * B), jnp.float32), pltpu.VMEM((B, NB), jnp.float32)],
        )
        if n > 1:
            row, inverse, gram = done
            rows.append(row)
        else:
            (inverse,) = done
        inverses.append(inverse)
    return rows, inverses


def solve_kernel(place_ref, *refs):
    rows, inverses = refs[: P_SIZE - 1], refs[P_SIZE - 1 : 2 * P_SIZE - 1]
    gram_ref, pair_ref, other_ref, out_ref, own_ref = refs[-5:]
    row_index, col_index = 2 * place_ref[1] + place_ref[0], place_ref[3]

    @pl.when(col_index >= P_SIZE)
    def _():
        for h in range(2):
            own_ref[row_index ^ (2 * h)] = pair_ref[h]
            own_ref[row_index ^ (2 * h + 1)] = other_ref[h]

    for c in range(P_SIZE):

        @pl.when(col_index == c)
        def _(c=c):
            for r in range(P_SIZE):
                own_ref[r] = gram_ref[PAIRS.index((min(r, c), c))]

    done = []
    for i in range(P_SIZE):
        block = own_ref[i]
        for k in range(i):
            off = (i - k - 1) * B
            block = block - dot_t(rows[k][:, off : off + B], done[k])
        block = dot(inverses[i][...], block)
        done.append(block)

        @pl.when(row_index == i)
        def _(block=block):
            rows_at = i * B + lax.broadcasted_iota(jnp.int32, block.shape, 0)
            cols_at = col_index * B + lax.broadcasted_iota(jnp.int32, block.shape, 1)
            out_ref[...] = jnp.where(cols_at >= rows_at, block, 0.0)


def from_first(value, n_hi):
    at = lax.axis_index("hi")
    have = 1
    while have < n_hi:
        more = min(have, n_hi - have)
        got = lax.ppermute(value, "hi", [(g, g + have) for g in range(more)])
        value = jnp.where(at < have, value, got)
        have += more
    return value


def exchange(value, high_bits, low_bits):
    bits = low_bits * 2 + high_bits
    return lax.ppermute(value, ("lo", "rh"), [(i, i ^ bits) for i in range(2 * P_SIZE)])


def swap(value, axis="rl"):
    return lax.ppermute(value, axis, [(0, 1), (1, 0)])


def other_group(value):
    return lax.ppermute(value, ("hi", "lo"), [(i, i ^ 6) for i in range(2 * P_SIZE)])


def spread(piece):
    y, z, x = (0, 1), (0, 2), (1, 0)
    by_x, by_z, by_y = exchange(piece, *x), exchange(piece, *z), exchange(piece, *y)
    by_xz, by_zy, by_yx = exchange(by_x, *z), exchange(by_z, *y), exchange(by_y, *x)
    by_zyx = exchange(by_xz, *y)
    return jnp.stack([piece, by_y, by_z, by_zy, by_x, by_yx, by_xz, by_zyx])


def on_device(r_slab, arc_rows, arc_blocks):
    n_hi = lax.axis_size("hi")
    group, low = lax.axis_index("hi"), lax.axis_index("lo")
    high_row, side = lax.axis_index("rh"), lax.axis_index("rl")
    col_index = group * P_SIZE + low
    columns = arc_rows.shape[1]
    in_two = n_hi == 2
    panel = low ^ (2 * group) if in_two else low
    place = jnp.stack([side, high_row, panel, col_index, group]).astype(jnp.int32)
    total = r_slab.shape[0] + arc_rows.shape[0]
    parts = 2 * CHUNKS if in_two else CHUNKS
    chunks = on_chip(
        mask_kernel,
        [(total // parts, columns)] * parts,
        "mask",
        place,
        arc_blocks,
        r_slab,
        arc_rows,
        scalars=2,
        scratch=[pltpu.VMEM((total, columns), jnp.float32)],
    )
    y, z = (0, 1), (0, 2)

    def halves(k, after):
        if not in_two:
            return from_first(chunks[k], n_hi), chunks[k]
        shape = chunks[k].shape
        return on_chip(
            select_kernel,
            [shape, shape],
            "select",
            place,
            chunks[k],
            other_group(chunks[CHUNKS + k]),
            scalars=1,
            after=after,
        )

    pair, block = (2, B, B), (B, B)
    count = len(PAIRS) * B // P_SIZE // P_SIZE
    sums = [(P_SIZE * count, B), (P_SIZE, B, B)]
    panels, right, before, relayed = [[] for _ in range(P_SIZE)], [], (), ()
    for k in range(CHUNKS):
        if k == CHUNKS - 1:
            half = [chunk for chunks_of in panels for chunk in chunks_of[: CHUNKS // 2]]
            begun = on_chip(
                products_kernel,
                sums,
                "first_products",
                place,
                *half,
                *right[: CHUNKS // 2],
                scalars=1,
            )
            before = (*before, begun[0])
        own, own_right = halves(k, before)
        early, late = (y, z) if k % 2 == 0 else (z, y)
        by_early, by_late = exchange(own, *early), exchange(own, *late)
        before = (by_early, by_late, *relayed)
        by_both = exchange(by_early, *late)
        relayed = (by_both,)
        by_y, by_z = (by_early, by_late) if k % 2 == 0 else (by_late, by_early)
        for chunks_of, chunk in zip(panels, (own, by_y, by_z, by_both)):
            chunks_of.append(chunk)
        right.append(own_right)
    half = [chunk for chunks_of in panels for chunk in chunks_of[CHUNKS // 2 :]]
    keep, keep_cross, send = on_chip(
        products_kernel,
        [(2, count, B), pair, (2, count + B, B)],
        "products",
        place,
        *half,
        *right[CHUNKS // 2 :],
        *begun,
        scalars=1,
        scratch=[pltpu.VMEM(shape, jnp.float32) for shape in sums],
    )
    got = swap(send)

    def picked(first, kept, after):
        return on_chip(
            functools.partial(pick_kernel, first),
            [kept.shape[1:]] * 2,
            "pick",
            place,
            kept,
            got,
            scalars=1,
            after=(after,),
        )

    mine, other = picked(0, keep, send)
    piece = mine + exchange(other, 1, 0)
    mine, other = picked(count, keep_cross, piece)
    if in_two:
        (piece,) = on_chip(
            add_kernel, [piece.shape], "add", piece, other_group(piece), after=(other,)
        )
    other = exchange(other, 1, 0)
    pieces = spread(piece)
    (gram,) = on_chip(
        collect_kernel,
        [(len(PAIRS), B, B)],
        "collect",
        place,
        pieces,
        swap(pieces),
        scalars=1,
    )

    def added(left, right, after):
        (total,) = on_chip(add_kernel, [block], "add", left, right, after=(after,))
        return total

    rows, inverses = factor(gram)
    mine = added(mine, other, rows[0])
    if in_two:
        mine = added(mine, other_group(mine), rows[1])
    (own,) = on_chip(stack_kernel, [pair], "stack", mine, exchange(mine, 1, 0), after=(rows[2],))
    (result,) = on_chip(
        solve_kernel,
        [(B, columns)],
        "solve",
        place,
        *rows,
        *inverses,
        gram,
        own,
        swap(own),
        scalars=1,
        scratch=[pltpu.VMEM((P_SIZE, B, columns), jnp.float32)],
    )
    return result


def solution(mesh):
    n_col, n_row = mesh.shape["col"], mesh.shape["row"]
    split = Mesh(
        mesh.devices.reshape(n_col // P_SIZE, P_SIZE, n_row // 2, 2),
        ("hi", "lo", "rh", "rl"),
    )
    spec = P(("rh", "rl"), ("hi", "lo"))
    return jax.shard_map(
        on_device,
        mesh=split,
        in_specs=(spec, spec, spec),
        out_specs=spec,
        check_vma=False,
    )
```

```python
import functools

import jax
import jax.numpy as jnp
from jax import lax
from jax.experimental import pallas as pl
from jax.experimental.pallas import tpu as pltpu
from jax.sharding import Mesh
from jax.sharding import PartitionSpec as P

B = 256
P_SIZE = 4
ARC_ROWS = 128
NB = 128
SUB = 8


def split(value):
    high = value.astype(jnp.bfloat16)
    return high, (value - high.astype(jnp.float32)).astype(jnp.bfloat16)


def left_parts(value, axis=0):
    high, low = split(value)
    return jnp.concatenate([high, high, low], axis=axis)


def right_parts(value):
    high, low = split(value)
    return jnp.concatenate([high, low, high], axis=0)


def parts_dot(left, right):
    return lax.dot_general(
        left, right, (((0,), (0,)), ((), ())), preferred_element_type=jnp.float32
    )


def dot(left, right):
    return jnp.dot(left_parts(left, 1), right_parts(right), preferred_element_type=jnp.float32)


def dot_t(left, right):
    return parts_dot(left_parts(left), right_parts(right))


def lane(value, at):
    return jnp.broadcast_to(value[:, at : at + 1], (SUB, NB))


def row(value, at):
    return jnp.broadcast_to(value[at : at + 1, :], (SUB, NB))


def inverse_factor(rows):
    n = NB // SUB
    row_id = lax.broadcasted_iota(jnp.int32, (SUB, NB), 0)
    col_id = lax.broadcasted_iota(jnp.int32, (SUB, NB), 1)
    order = range(SUB)
    ahead = [lane(rows[0], m) for m in order]
    for b in range(n):
        j = b * SUB
        pivot = {(k, m): row(ahead[m], k) for k in order for m in range(k, SUB)}
        below = [[lane(rows[r], j + k) for k in order] for r in range(b + 1, n)]
        if b + 1 < n:
            ahead = [lane(rows[b + 1], j + SUB + m) for m in order]
        scale, left = [], []
        for k in order:
            scale.append(lax.rsqrt(pivot[k, k]))
            for m in range(k + 1, SUB):
                pivot[k, m] = pivot[k, m] * scale[k]
            for m in range(k + 1, SUB):
                for q in range(m, SUB):
                    pivot[m, q] = pivot[m, q] - pivot[k, m] * pivot[k, q]
            if b + 1 < n:
                part = below[0][k]
                for m in range(k):
                    part = part - pivot[m, k] * left[m]
                part = part * scale[k]
                left.append(part)
                for m in order:
                    ahead[m] = ahead[m] - part * row(part, m)
        inside = (col_id >= j) & (col_id < j + SUB)
        head = jnp.where(inside, jnp.where(col_id - j == row_id, 1.0, 0.0), rows[b])
        top = []
        for k in order:
            part = row(head, k)
            for m in range(k):
                part = part - pivot[m, k] * top[m]
            top.append(part * scale[k])
        if b + 1 < n:
            solved = [None] * SUB
            for k in reversed(order):
                part = top[k]
                for m in range(k + 1, SUB):
                    part = part - pivot[k, m] * solved[m]
                solved[k] = part * scale[k]
            for r in range(b + 1, n):
                body = jnp.where(inside, 0.0, rows[r])
                for k in order:
                    body = body - below[r - b - 1][k] * solved[k]
                rows[r] = body
        strip = top[0]
        for k in range(1, SUB):
            strip = jnp.where(row_id == k, top[k], strip)
        rows[b] = jnp.where(col_id < j + SUB, strip, 0.0)
    return rows


PAIRS = [(r, c) for r in range(P_SIZE) for c in range(r, P_SIZE)]
CHUNKS = 4


def mask_kernel(place_ref, arcs_ref, slab_ref, rows_ref, *refs):
    chunks, work = refs[:-1], refs[-1]
    top = slab_ref.shape[0]
    work[:top, :] = slab_ref[...]
    for a in range(arcs_ref.shape[0]):
        live = arcs_ref[a, 0].astype(jnp.float32)
        at = a * ARC_ROWS
        work[top + at : top + at + ARC_ROWS, :] = rows_ref[at : at + ARC_ROWS, :] * live
    count = chunks[0].shape[0]
    if len(chunks) > CHUNKS:
        first = jnp.where(place_ref[4] == 0, 0, CHUNKS * count)
    else:
        first = 0
    for s, chunk in enumerate(chunks):
        start = first + s * count if s < CHUNKS else CHUNKS * count - first + (s - CHUNKS) * count
        chunk[...] = work[pl.ds(pl.multiple_of(start, 16), count), :]


def select_kernel(place_ref, kept_ref, got_ref, *refs):
    panel_ref, right_ref = refs[-2:]

    @pl.when(place_ref[4] == 0)
    def _():
        panel_ref[...] = kept_ref[...]
        right_ref[...] = got_ref[...]

    @pl.when(place_ref[4] != 0)
    def _():
        panel_ref[...] = got_ref[...]
        right_ref[...] = kept_ref[...]


def products_kernel(place_ref, *refs):
    n = CHUNKS // 2
    panels, right = refs[: P_SIZE * n], refs[P_SIZE * n : (P_SIZE + 1) * n]
    refs = refs[(P_SIZE + 1) * n :]
    last = len(refs) > 2
    if last:
        old_upper, old_cross, keep_ref, keep_cross_ref, send_ref, upper, cross = refs
    else:
        upper, cross = refs
    side, own = place_ref[0], place_ref[2]

    def whole(chunks):
        return jnp.concatenate([chunk[...] for chunk in chunks], axis=0)

    both = jnp.concatenate([right_parts(whole(panels[:n])), right_parts(whole(right))], axis=1)
    for t in range(P_SIZE):
        left = left_parts(whole(panels[t * n : (t + 1) * n]))
        product = parts_dot(left, both)
        spot = own ^ t
        cross[spot] = product[:, B:] + old_cross[spot] if last else product[:, B:]
        rows = slice(0, B) if t == 0 else slice(B + (t - 1) * B // 2, B + t * B // 2)
        if t == 0:
            upper[rows, :] = product[:, :B]
        else:

            @pl.when(own < spot)
            def _(rows=rows, product=product):
                upper[rows, :] = product[:, : B // 2].T

            @pl.when(own > spot)
            def _(rows=rows, product=product):
                upper[rows, :] = product[B // 2 :, :B]

    if not last:
        return
    upper[...] = upper[...] + old_upper[...]
    count = keep_ref.shape[1]
    for h in range(2):
        here, there = 2 * h + side, 2 * h + 1 - side
        keep_ref[h] = upper[pl.ds(pl.multiple_of(here * count, SUB), count), :]
        keep_cross_ref[h] = cross[here]
        send_ref[h, :count] = upper[pl.ds(pl.multiple_of(there * count, SUB), count), :]
        send_ref[h, count:] = cross[there]


def pick_kernel(first, place_ref, keep_ref, got_ref, _, own_ref, other_ref):
    high = place_ref[1]
    rows = pl.ds(first, own_ref.shape[0])
    own_ref[...] = keep_ref[high] + got_ref[high, rows]
    other_ref[...] = keep_ref[1 - high] + got_ref[1 - high, rows]


def stack_kernel(first_ref, second_ref, _, out_ref):
    out_ref[0] = first_ref[...]
    out_ref[1] = second_ref[...]


def add_kernel(left_ref, right_ref, after_ref, out_ref):
    del after_ref
    out_ref[...] = left_ref[...] + right_ref[...]


def on_chip(kernel, shapes, name, *operands, scratch=(), scalars=0, after=(), outside=()):
    done = pl.pallas_call(
        kernel,
        out_shape=[jax.ShapeDtypeStruct(shape, jnp.float32) for shape in shapes],
        in_specs=[pl.BlockSpec(memory_space=pltpu.SMEM)] * scalars
        + [pl.BlockSpec(memory_space=pltpu.VMEM)] * (len(operands) - scalars)
        + [pl.BlockSpec(memory_space=pltpu.HBM)] * len(outside)
        + [pl.BlockSpec(memory_space=pl.ANY)] * len(after),
        out_specs=[pl.BlockSpec(memory_space=pltpu.VMEM)] * len(shapes),
        scratch_shapes=list(scratch),
        compiler_params=pltpu.CompilerParams(vmem_limit_bytes=16 * 1024 * 1024),
        name=name,
    )(*operands, *outside, *after)
    return list(done)


def collect_kernel(place_ref, mine_ref, other_ref, gram_ref):
    side, at = place_ref[0], place_ref[1] * P_SIZE + place_ref[2]
    count = mine_ref.shape[1]
    for q in range(P_SIZE):
        runs = [(q, q, 0, B)]
        for t in range(1, P_SIZE):
            j = q ^ t
            runs.append((min(q, j), max(q, j), 0 if q < j else B // 2, B // 2))
        done = 0
        for r, c, first, size in runs:
            block, start, end = PAIRS.index((r, c)), done, done + size
            while start < end:
                piece, skip = start // count, start % count
                rows = min(end - start, count - skip)
                spot = ((piece // 2) * P_SIZE + q) ^ at
                into = slice(first + start - done, first + start - done + rows)

                @pl.when(side == piece % 2)
                def _(block=block, into=into, spot=spot, skip=skip, rows=rows):
                    gram_ref[block, into] = mine_ref[spot, skip : skip + rows]

                @pl.when(side != piece % 2)
                def _(block=block, into=into, spot=spot, skip=skip, rows=rows):
                    gram_ref[block, into] = other_ref[spot, skip : skip + rows]

                start += rows
            done = end


def factor_step_kernel(n, gram_ref, *rest):
    if n > 1:
        row_ref, inverse_ref, next_ref, work, inv = rest
    else:
        inverse_ref, work, inv = rest
    for c in range(n):
        work[:, c * B : (c + 1) * B] = gram_ref[c]
    width = n * B

    def step(b, carry):
        start = pl.multiple_of(b * NB, NB)
        rows = [
            work[pl.ds(pl.multiple_of(start + r * SUB, SUB), SUB), pl.ds(start, NB)]
            for r in range(NB // SUB)
        ]
        right = inverse_factor(rows)
        for r in range(NB // SUB):
            inv[pl.ds(pl.multiple_of(start + r * SUB, SUB), SUB), :] = right[r]

        @pl.when(b == 0)
        def _():
            panel = dot(inv[:NB, :], work[:NB, NB:])
            work[:NB, NB:] = panel
            work[NB:, NB:] = work[NB:, NB:] - dot_t(panel[:, :NB], panel)

        return carry

    lax.fori_loop(0, B // NB, step, 0)
    first, second = inv[:NB, :], inv[NB:, :]
    inverse_ref[:NB, :NB] = first
    inverse_ref[:NB, NB:] = jnp.zeros((NB, NB), jnp.float32)
    inverse_ref[NB:, :NB] = -dot(second, dot_t(work[:NB, NB:B], first))
    inverse_ref[NB:, NB:] = second
    if n > 1:
        work[NB:, B:] = dot(second, work[NB:, B:])
        row = work[:, B:]
        row_ref[...] = row
        at = n
        for r in range(1, n):
            left = row[:, (r - 1) * B : r * B]
            for c in range(r, n):
                next_ref[at - n] = gram_ref[at] - dot_t(left, row[:, (c - 1) * B : c * B])
                at += 1


def factor(gram):
    rows, inverses = [], []
    for n in range(P_SIZE, 0, -1):
        shapes = [(B, (n - 1) * B), (B, B), (n * (n - 1) // 2, B, B)] if n > 1 else [(B, B)]
        done = on_chip(
            functools.partial(factor_step_kernel, n),
            shapes,
            "factor_step",
            gram,
            scratch=[pltpu.VMEM((B, n * B), jnp.float32), pltpu.VMEM((B, NB), jnp.float32)],
        )
        if n > 1:
            row, inverse, gram = done
            rows.append(row)
        else:
            (inverse,) = done
        inverses.append(inverse)
    return rows, inverses


def solve_kernel(place_ref, *refs):
    rows, inverses = refs[: P_SIZE - 1], refs[P_SIZE - 1 : 2 * P_SIZE - 1]
    gram_ref, pair_ref, other_ref, out_ref, own_ref = refs[-5:]
    row_index, col_index = 2 * place_ref[1] + place_ref[0], place_ref[3]

    @pl.when(col_index >= P_SIZE)
    def _():
        for h in range(2):
            own_ref[row_index ^ (2 * h)] = pair_ref[h]
            own_ref[row_index ^ (2 * h + 1)] = other_ref[h]

    for c in range(P_SIZE):

        @pl.when(col_index == c)
        def _(c=c):
            for r in range(P_SIZE):
                own_ref[r] = gram_ref[PAIRS.index((min(r, c), c))]

    done = []
    for i in range(P_SIZE):
        block = own_ref[i]
        for k in range(i):
            off = (i - k - 1) * B
            block = block - dot_t(rows[k][:, off : off + B], done[k])
        block = dot(inverses[i][...], block)
        done.append(block)

        @pl.when(row_index == i)
        def _(block=block):
            rows_at = i * B + lax.broadcasted_iota(jnp.int32, block.shape, 0)
            cols_at = col_index * B + lax.broadcasted_iota(jnp.int32, block.shape, 1)
            out_ref[...] = jnp.where(cols_at >= rows_at, block, 0.0)


def from_first(value, n_hi):
    at = lax.axis_index("hi")
    have = 1
    while have < n_hi:
        more = min(have, n_hi - have)
        got = lax.ppermute(value, "hi", [(g, g + have) for g in range(more)])
        value = jnp.where(at < have, value, got)
        have += more
    return value


def exchange(value, high_bits, low_bits):
    bits = low_bits * 2 + high_bits
    return lax.ppermute(value, ("lo", "rh"), [(i, i ^ bits) for i in range(2 * P_SIZE)])


def swap(value, axis="rl"):
    return lax.ppermute(value, axis, [(0, 1), (1, 0)])


def other_group(value):
    return lax.ppermute(value, ("hi", "lo"), [(i, i ^ P_SIZE) for i in range(2 * P_SIZE)])


def spread(piece):
    y, z, x = (0, 1), (0, 2), (1, 0)
    by_x, by_z, by_y = exchange(piece, *x), exchange(piece, *z), exchange(piece, *y)
    by_xz, by_zy, by_yx = exchange(by_x, *z), exchange(by_z, *y), exchange(by_y, *x)
    by_zyx = exchange(by_xz, *y)
    return jnp.stack([piece, by_y, by_z, by_zy, by_x, by_yx, by_xz, by_zyx])


def on_device(r_slab, arc_rows, arc_blocks):
    n_hi = lax.axis_size("hi")
    group, low = lax.axis_index("hi"), lax.axis_index("lo")
    high_row, side = lax.axis_index("rh"), lax.axis_index("rl")
    col_index = group * P_SIZE + low
    columns = arc_rows.shape[1]
    in_two = n_hi == 2
    place = jnp.stack([side, high_row, low, col_index, group]).astype(jnp.int32)
    total = r_slab.shape[0] + arc_rows.shape[0]
    parts = 2 * CHUNKS if in_two else CHUNKS
    chunks = on_chip(
        mask_kernel,
        [(total // parts, columns)] * parts,
        "mask",
        place,
        arc_blocks,
        r_slab,
        arc_rows,
        scalars=2,
        scratch=[pltpu.VMEM((total, columns), jnp.float32)],
    )
    y, z = (0, 1), (0, 2)

    def halves(k, after):
        if not in_two:
            return from_first(chunks[k], n_hi), chunks[k]
        shape = chunks[k].shape
        return on_chip(
            select_kernel,
            [shape, shape],
            "select",
            place,
            chunks[k],
            other_group(chunks[CHUNKS + k]),
            scalars=1,
            after=after,
        )

    pair, block = (2, B, B), (B, B)
    count = len(PAIRS) * B // P_SIZE // P_SIZE
    sums = [(P_SIZE * count, B), (P_SIZE, B, B)]
    panels, right, before, relayed = [[] for _ in range(P_SIZE)], [], (), ()
    for k in range(CHUNKS):
        if k == CHUNKS - 1:
            half = [chunk for chunks_of in panels for chunk in chunks_of[: CHUNKS // 2]]
            begun = on_chip(
                products_kernel,
                sums,
                "first_products",
                place,
                *half,
                *right[: CHUNKS // 2],
                scalars=1,
            )
            before = (*before, begun[0])
        own, own_right = halves(k, before)
        early, late = (y, z) if k % 2 == 0 else (z, y)
        by_early, by_late = exchange(own, *early), exchange(own, *late)
        before = (by_early, by_late, *relayed)
        by_both = exchange(by_early, *late)
        relayed = (by_both,)
        by_y, by_z = (by_early, by_late) if k % 2 == 0 else (by_late, by_early)
        for chunks_of, chunk in zip(panels, (own, by_y, by_z, by_both)):
            chunks_of.append(chunk)
        right.append(own_right)
    half = [chunk for chunks_of in panels for chunk in chunks_of[CHUNKS // 2 :]]
    keep, keep_cross, send = on_chip(
        products_kernel,
        [(2, count, B), pair, (2, count + B, B)],
        "products",
        place,
        *half,
        *right[CHUNKS // 2 :],
        *begun,
        scalars=1,
        scratch=[pltpu.VMEM(shape, jnp.float32) for shape in sums],
    )
    got = swap(send)

    def picked(first, kept, after):
        return on_chip(
            functools.partial(pick_kernel, first),
            [kept.shape[1:]] * 2,
            "pick",
            place,
            kept,
            got,
            scalars=1,
            after=(after,),
        )

    mine, other = picked(0, keep, send)
    piece = mine + exchange(other, 1, 0)
    mine, other = picked(count, keep_cross, piece)
    if in_two:
        (piece,) = on_chip(
            add_kernel, [piece.shape], "add", piece, other_group(piece), after=(other,)
        )
    other = exchange(other, 1, 0)
    pieces = spread(piece)
    (gram,) = on_chip(
        collect_kernel,
        [(len(PAIRS), B, B)],
        "collect",
        place,
        pieces,
        swap(pieces),
        scalars=1,
    )

    def added(left, right, after):
        (total,) = on_chip(add_kernel, [block], "add", left, right, after=(after,))
        return total

    rows, inverses = factor(gram)
    mine = added(mine, other, rows[0])
    if in_two:
        mine = added(mine, other_group(mine), rows[1])
    (own,) = on_chip(stack_kernel, [pair], "stack", mine, exchange(mine, 1, 0), after=(rows[2],))
    (result,) = on_chip(
        solve_kernel,
        [(B, columns)],
        "solve",
        place,
        *rows,
        *inverses,
        gram,
        own,
        swap(own),
        scalars=1,
        scratch=[pltpu.VMEM((P_SIZE, B, columns), jnp.float32)],
    )
    return result


def solution(mesh):
    n_col, n_row = mesh.shape["col"], mesh.shape["row"]
    split = Mesh(
        mesh.devices.reshape(n_col // P_SIZE, P_SIZE, n_row // 2, 2),
        ("hi", "lo", "rh", "rl"),
    )
    spec = P(("rh", "rl"), ("hi", "lo"))
    return jax.shard_map(
        on_device,
        mesh=split,
        in_specs=(spec, spec, spec),
        out_specs=spec,
        check_vma=False,
    )
```

```python
import functools

import jax
import jax.numpy as jnp
from jax import lax
from jax.experimental import pallas as pl
from jax.experimental.pallas import tpu as pltpu
from jax.sharding import Mesh
from jax.sharding import PartitionSpec as P

B = 256
P_SIZE = 4
ARC_ROWS = 128
NB = 128
SUB = 8


def split(value):
    high = value.astype(jnp.bfloat16)
    return high, (value - high.astype(jnp.float32)).astype(jnp.bfloat16)


def left_parts(value, axis=0):
    high, low = split(value)
    return jnp.concatenate([high, high, low], axis=axis)


def right_parts(value):
    high, low = split(value)
    return jnp.concatenate([high, low, high], axis=0)


def parts_dot(left, right):
    return lax.dot_general(
        left, right, (((0,), (0,)), ((), ())), preferred_element_type=jnp.float32
    )


def dot(left, right):
    return jnp.dot(left_parts(left, 1), right_parts(right), preferred_element_type=jnp.float32)


def dot_t(left, right):
    return parts_dot(left_parts(left), right_parts(right))


def lane(value, at):
    return jnp.broadcast_to(value[:, at : at + 1], (SUB, NB))


def row(value, at):
    return jnp.broadcast_to(value[at : at + 1, :], (SUB, NB))


def inverse_factor(rows):
    n = NB // SUB
    row_id = lax.broadcasted_iota(jnp.int32, (SUB, NB), 0)
    col_id = lax.broadcasted_iota(jnp.int32, (SUB, NB), 1)
    order = range(SUB)
    ahead = [lane(rows[0], m) for m in order]
    for b in range(n):
        j = b * SUB
        pivot = {(k, m): row(ahead[m], k) for k in order for m in range(k, SUB)}
        below = [[lane(rows[r], j + k) for k in order] for r in range(b + 1, n)]
        if b + 1 < n:
            ahead = [lane(rows[b + 1], j + SUB + m) for m in order]
        scale, left = [], []
        for k in order:
            scale.append(lax.rsqrt(pivot[k, k]))
            for m in range(k + 1, SUB):
                pivot[k, m] = pivot[k, m] * scale[k]
            for m in range(k + 1, SUB):
                for q in range(m, SUB):
                    pivot[m, q] = pivot[m, q] - pivot[k, m] * pivot[k, q]
            if b + 1 < n:
                part = below[0][k]
                for m in range(k):
                    part = part - pivot[m, k] * left[m]
                part = part * scale[k]
                left.append(part)
                for m in order:
                    ahead[m] = ahead[m] - part * row(part, m)
        inside = (col_id >= j) & (col_id < j + SUB)
        head = jnp.where(inside, jnp.where(col_id - j == row_id, 1.0, 0.0), rows[b])
        top = []
        for k in order:
            part = row(head, k)
            for m in range(k):
                part = part - pivot[m, k] * top[m]
            top.append(part * scale[k])
        if b + 1 < n:
            solved = [None] * SUB
            for k in reversed(order):
                part = top[k]
                for m in range(k + 1, SUB):
                    part = part - pivot[k, m] * solved[m]
                solved[k] = part * scale[k]
            for r in range(b + 1, n):
                body = jnp.where(inside, 0.0, rows[r])
                for k in order:
                    body = body - below[r - b - 1][k] * solved[k]
                rows[r] = body
        strip = top[0]
        for k in range(1, SUB):
            strip = jnp.where(row_id == k, top[k], strip)
        rows[b] = jnp.where(col_id < j + SUB, strip, 0.0)
    return rows


PAIRS = [(r, c) for r in range(P_SIZE) for c in range(r, P_SIZE)]
CHUNKS = 4


def mask_kernel(place_ref, arcs_ref, slab_ref, rows_ref, *refs):
    chunks, work = refs[:-1], refs[-1]
    top = slab_ref.shape[0]
    work[:top, :] = slab_ref[...]
    for a in range(arcs_ref.shape[0]):
        live = arcs_ref[a, 0].astype(jnp.float32)
        at = a * ARC_ROWS
        work[top + at : top + at + ARC_ROWS, :] = rows_ref[at : at + ARC_ROWS, :] * live
    count = chunks[0].shape[0]
    if len(chunks) > CHUNKS:
        first = jnp.where(place_ref[4] == 0, 0, CHUNKS * count)
    else:
        first = 0
    for s, chunk in enumerate(chunks):
        start = first + s * count if s < CHUNKS else CHUNKS * count - first + (s - CHUNKS) * count
        chunk[...] = work[pl.ds(pl.multiple_of(start, 16), count), :]


def select_kernel(place_ref, kept_ref, got_ref, *refs):
    panel_ref, right_ref = refs[-2:]

    @pl.when(place_ref[4] == 0)
    def _():
        panel_ref[...] = kept_ref[...]
        right_ref[...] = got_ref[...]

    @pl.when(place_ref[4] != 0)
    def _():
        panel_ref[...] = got_ref[...]
        right_ref[...] = kept_ref[...]


def products_kernel(place_ref, *refs):
    n = CHUNKS // 2
    panels, right = refs[: P_SIZE * n], refs[P_SIZE * n : (P_SIZE + 1) * n]
    refs = refs[(P_SIZE + 1) * n :]
    last = len(refs) > 2
    if last:
        old_upper, old_cross, keep_ref, keep_cross_ref, send_ref, upper, cross = refs
    else:
        upper, cross = refs
    side, own = place_ref[0], place_ref[2]

    def whole(chunks):
        return jnp.concatenate([chunk[...] for chunk in chunks], axis=0)

    both = jnp.concatenate([right_parts(whole(panels[:n])), right_parts(whole(right))], axis=1)
    for t in range(P_SIZE):
        left = left_parts(whole(panels[t * n : (t + 1) * n]))
        product = parts_dot(left, both)
        spot = own ^ t
        cross[spot] = product[:, B:] + old_cross[spot] if last else product[:, B:]
        rows = slice(0, B) if t == 0 else slice(B + (t - 1) * B // 2, B + t * B // 2)
        if t == 0:
            upper[rows, :] = product[:, :B]
        else:

            @pl.when(own < spot)
            def _(rows=rows, product=product):
                upper[rows, :] = product[:, : B // 2].T

            @pl.when(own > spot)
            def _(rows=rows, product=product):
                upper[rows, :] = product[B // 2 :, :B]

    if not last:
        return
    upper[...] = upper[...] + old_upper[...]
    count = keep_ref.shape[1]
    for h in range(2):
        here, there = 2 * h + side, 2 * h + 1 - side
        keep_ref[h] = upper[pl.ds(pl.multiple_of(here * count, SUB), count), :]
        keep_cross_ref[h] = cross[here]
        send_ref[h, :count] = upper[pl.ds(pl.multiple_of(there * count, SUB), count), :]
        send_ref[h, count:] = cross[there]


def pick_kernel(first, place_ref, keep_ref, got_ref, _, own_ref, other_ref):
    high = place_ref[1]
    rows = pl.ds(first, own_ref.shape[0])
    own_ref[...] = keep_ref[high] + got_ref[high, rows]
    other_ref[...] = keep_ref[1 - high] + got_ref[1 - high, rows]


def stack_kernel(first_ref, second_ref, _, out_ref):
    out_ref[0] = first_ref[...]
    out_ref[1] = second_ref[...]


def add_kernel(left_ref, right_ref, after_ref, out_ref):
    del after_ref
    out_ref[...] = left_ref[...] + right_ref[...]


def on_chip(kernel, shapes, name, *operands, scratch=(), scalars=0, after=(), outside=()):
    done = pl.pallas_call(
        kernel,
        out_shape=[jax.ShapeDtypeStruct(shape, jnp.float32) for shape in shapes],
        in_specs=[pl.BlockSpec(memory_space=pltpu.SMEM)] * scalars
        + [pl.BlockSpec(memory_space=pltpu.VMEM)] * (len(operands) - scalars)
        + [pl.BlockSpec(memory_space=pltpu.HBM)] * len(outside)
        + [pl.BlockSpec(memory_space=pl.ANY)] * len(after),
        out_specs=[pl.BlockSpec(memory_space=pltpu.VMEM)] * len(shapes),
        scratch_shapes=list(scratch),
        compiler_params=pltpu.CompilerParams(vmem_limit_bytes=16 * 1024 * 1024),
        name=name,
    )(*operands, *outside, *after)
    return list(done)


def collect_kernel(place_ref, mine_ref, other_ref, gram_ref):
    side, at = place_ref[0], place_ref[1] * P_SIZE + place_ref[2]
    count = mine_ref.shape[1]
    for q in range(P_SIZE):
        runs = [(q, q, 0, B)]
        for t in range(1, P_SIZE):
            j = q ^ t
            runs.append((min(q, j), max(q, j), 0 if q < j else B // 2, B // 2))
        done = 0
        for r, c, first, size in runs:
            block, start, end = PAIRS.index((r, c)), done, done + size
            while start < end:
                piece, skip = start // count, start % count
                rows = min(end - start, count - skip)
                spot = ((piece // 2) * P_SIZE + q) ^ at
                into = slice(first + start - done, first + start - done + rows)

                @pl.when(side == piece % 2)
                def _(block=block, into=into, spot=spot, skip=skip, rows=rows):
                    gram_ref[block, into] = mine_ref[spot, skip : skip + rows]

                @pl.when(side != piece % 2)
                def _(block=block, into=into, spot=spot, skip=skip, rows=rows):
                    gram_ref[block, into] = other_ref[spot, skip : skip + rows]

                start += rows
            done = end


def factor_step_kernel(n, gram_ref, *rest):
    if n > 1:
        row_ref, inverse_ref, next_ref, work, inv = rest
    else:
        inverse_ref, work, inv = rest
    for c in range(n):
        work[:, c * B : (c + 1) * B] = gram_ref[c]
    width = n * B

    def step(b, carry):
        start = pl.multiple_of(b * NB, NB)
        rows = [
            work[pl.ds(pl.multiple_of(start + r * SUB, SUB), SUB), pl.ds(start, NB)]
            for r in range(NB // SUB)
        ]
        right = inverse_factor(rows)
        for r in range(NB // SUB):
            inv[pl.ds(pl.multiple_of(start + r * SUB, SUB), SUB), :] = right[r]

        @pl.when(b == 0)
        def _():
            panel = dot(inv[:NB, :], work[:NB, NB:])
            work[:NB, NB:] = panel
            work[NB:, NB:] = work[NB:, NB:] - dot_t(panel[:, :NB], panel)

        return carry

    lax.fori_loop(0, B // NB, step, 0)
    first, second = inv[:NB, :], inv[NB:, :]
    inverse_ref[:NB, :NB] = first
    inverse_ref[:NB, NB:] = jnp.zeros((NB, NB), jnp.float32)
    inverse_ref[NB:, :NB] = -dot(second, dot_t(work[:NB, NB:B], first))
    inverse_ref[NB:, NB:] = second
    if n > 1:
        work[NB:, B:] = dot(second, work[NB:, B:])
        row = work[:, B:]
        row_ref[...] = row
        at = n
        left, right = left_parts(row), right_parts(row)
        for r in range(1, n):
            off = (r - 1) * B
            update = parts_dot(left[:, off : off + B], right[:, off:])
            for c in range(n - r):
                next_ref[at - n] = gram_ref[at] - update[:, c * B : (c + 1) * B]
                at += 1


def factor(gram):
    rows, inverses = [], []
    for n in range(P_SIZE, 0, -1):
        shapes = [(B, (n - 1) * B), (B, B), (n * (n - 1) // 2, B, B)] if n > 1 else [(B, B)]
        done = on_chip(
            functools.partial(factor_step_kernel, n),
            shapes,
            "factor_step",
            gram,
            scratch=[pltpu.VMEM((B, n * B), jnp.float32), pltpu.VMEM((B, NB), jnp.float32)],
        )
        if n > 1:
            row, inverse, gram = done
            rows.append(row)
        else:
            (inverse,) = done
        inverses.append(inverse)
    return rows, inverses


def solve_kernel(place_ref, *refs):
    rows, inverses = refs[: P_SIZE - 1], refs[P_SIZE - 1 : 2 * P_SIZE - 1]
    gram_ref, pair_ref, other_ref, out_ref, own_ref = refs[-5:]
    row_index, col_index = 2 * place_ref[1] + place_ref[0], place_ref[3]

    @pl.when(col_index >= P_SIZE)
    def _():
        for h in range(2):
            own_ref[row_index ^ (2 * h)] = pair_ref[h]
            own_ref[row_index ^ (2 * h + 1)] = other_ref[h]

    for c in range(P_SIZE):

        @pl.when(col_index == c)
        def _(c=c):
            for r in range(P_SIZE):
                own_ref[r] = gram_ref[PAIRS.index((min(r, c), c))]

    done = []
    for i in range(P_SIZE):
        block = own_ref[i]
        if i:
            above = [rows[k][:, (i - k - 1) * B : (i - k) * B] for k in range(i)]
            block = block - dot_t(jnp.concatenate(above, axis=0), jnp.concatenate(done, axis=0))
        block = dot(inverses[i][...], block)
        done.append(block)

        @pl.when(row_index == i)
        def _(block=block):
            rows_at = i * B + lax.broadcasted_iota(jnp.int32, block.shape, 0)
            cols_at = col_index * B + lax.broadcasted_iota(jnp.int32, block.shape, 1)
            out_ref[...] = jnp.where(cols_at >= rows_at, block, 0.0)


def from_first(value, n_hi):
    at = lax.axis_index("hi")
    have = 1
    while have < n_hi:
        more = min(have, n_hi - have)
        got = lax.ppermute(value, "hi", [(g, g + have) for g in range(more)])
        value = jnp.where(at < have, value, got)
        have += more
    return value


def exchange(value, high_bits, low_bits):
    bits = low_bits * 2 + high_bits
    return lax.ppermute(value, ("lo", "rh"), [(i, i ^ bits) for i in range(2 * P_SIZE)])


def swap(value, axis="rl"):
    return lax.ppermute(value, axis, [(0, 1), (1, 0)])


def other_group(value):
    return lax.ppermute(value, ("hi", "lo"), [(i, i ^ 6) for i in range(2 * P_SIZE)])


def spread(piece):
    y, z, x = (0, 1), (0, 2), (1, 0)
    by_x, by_z, by_y = exchange(piece, *x), exchange(piece, *z), exchange(piece, *y)
    by_xz, by_zy, by_yx = exchange(by_x, *z), exchange(by_z, *y), exchange(by_y, *x)
    by_zyx = exchange(by_xz, *y)
    return jnp.stack([piece, by_y, by_z, by_zy, by_x, by_yx, by_xz, by_zyx])


def on_device(r_slab, arc_rows, arc_blocks):
    n_hi = lax.axis_size("hi")
    group, low = lax.axis_index("hi"), lax.axis_index("lo")
    high_row, side = lax.axis_index("rh"), lax.axis_index("rl")
    col_index = group * P_SIZE + low
    columns = arc_rows.shape[1]
    in_two = n_hi == 2
    panel = low ^ (2 * group) if in_two else low
    place = jnp.stack([side, high_row, panel, col_index, group]).astype(jnp.int32)
    total = r_slab.shape[0] + arc_rows.shape[0]
    parts = 2 * CHUNKS if in_two else CHUNKS
    chunks = on_chip(
        mask_kernel,
        [(total // parts, columns)] * parts,
        "mask",
        place,
        arc_blocks,
        r_slab,
        arc_rows,
        scalars=2,
        scratch=[pltpu.VMEM((total, columns), jnp.float32)],
    )
    y, z = (0, 1), (0, 2)

    def halves(k, after):
        if not in_two:
            return from_first(chunks[k], n_hi), chunks[k]
        shape = chunks[k].shape
        return on_chip(
            select_kernel,
            [shape, shape],
            "select",
            place,
            chunks[k],
            other_group(chunks[CHUNKS + k]),
            scalars=1,
            after=after,
        )

    pair, block = (2, B, B), (B, B)
    count = len(PAIRS) * B // P_SIZE // P_SIZE
    sums = [(P_SIZE * count, B), (P_SIZE, B, B)]
    panels, right, before, relayed = [[] for _ in range(P_SIZE)], [], (), ()
    for k in range(CHUNKS):
        if k == CHUNKS - 1:
            half = [chunk for chunks_of in panels for chunk in chunks_of[: CHUNKS // 2]]
            begun = on_chip(
                products_kernel,
                sums,
                "first_products",
                place,
                *half,
                *right[: CHUNKS // 2],
                scalars=1,
            )
            before = (*before, begun[0])
        own, own_right = halves(k, before)
        early, late = (y, z) if k % 2 == 0 else (z, y)
        by_early, by_late = exchange(own, *early), exchange(own, *late)
        before = (by_early, by_late, *relayed)
        by_both = exchange(by_early, *late)
        relayed = (by_both,)
        by_y, by_z = (by_early, by_late) if k % 2 == 0 else (by_late, by_early)
        for chunks_of, chunk in zip(panels, (own, by_y, by_z, by_both)):
            chunks_of.append(chunk)
        right.append(own_right)
    half = [chunk for chunks_of in panels for chunk in chunks_of[CHUNKS // 2 :]]
    keep, keep_cross, send = on_chip(
        products_kernel,
        [(2, count, B), pair, (2, count + B, B)],
        "products",
        place,
        *half,
        *right[CHUNKS // 2 :],
        *begun,
        scalars=1,
        scratch=[pltpu.VMEM(shape, jnp.float32) for shape in sums],
    )
    got = swap(send)

    def picked(first, kept, after):
        return on_chip(
            functools.partial(pick_kernel, first),
            [kept.shape[1:]] * 2,
            "pick",
            place,
            kept,
            got,
            scalars=1,
            after=(after,),
        )

    mine, other = picked(0, keep, send)
    piece = mine + exchange(other, 1, 0)
    mine, other = picked(count, keep_cross, piece)
    if in_two:
        (piece,) = on_chip(
            add_kernel, [piece.shape], "add", piece, other_group(piece), after=(other,)
        )
    other = exchange(other, 1, 0)
    pieces = spread(piece)
    (gram,) = on_chip(
        collect_kernel,
        [(len(PAIRS), B, B)],
        "collect",
        place,
        pieces,
        swap(pieces),
        scalars=1,
    )

    def added(left, right, after):
        (total,) = on_chip(add_kernel, [block], "add", left, right, after=(after,))
        return total

    rows, inverses = factor(gram)
    mine = added(mine, other, rows[0])
    if in_two:
        mine = added(mine, other_group(mine), rows[1])
    (own,) = on_chip(stack_kernel, [pair], "stack", mine, exchange(mine, 1, 0), after=(rows[2],))
    (result,) = on_chip(
        solve_kernel,
        [(B, columns)],
        "solve",
        place,
        *rows,
        *inverses,
        gram,
        own,
        swap(own),
        scalars=1,
        scratch=[pltpu.VMEM((P_SIZE, B, columns), jnp.float32)],
    )
    return result


def solution(mesh):
    n_col, n_row = mesh.shape["col"], mesh.shape["row"]
    split = Mesh(
        mesh.devices.reshape(n_col // P_SIZE, P_SIZE, n_row // 2, 2),
        ("hi", "lo", "rh", "rl"),
    )
    spec = P(("rh", "rl"), ("hi", "lo"))
    return jax.shard_map(
        on_device,
        mesh=split,
        in_specs=(spec, spec, spec),
        out_specs=spec,
        check_vma=False,
    )
```
